32 devices in a mesh: wide: 16 (over z, x, core), narrow: 2 (over y).
Axes of the slice: x: 2, y: 2, z: 4, core: 2. Of those that a mesh axis runs over, the one named last changes fastest.
Arguments:
- features: float32 [32768, 1024], P(('wide', 'narrow')), may hold values from -6 to 6
- sketch: float32 [1024, 256], replicated, may hold values from -0.1875 to 0.1875
Outputs:
- basis: float32 [32768, 256], P(('wide', 'narrow'))
- factor: float32 [256, 256], replicated
- projection: float32 [256, 1024], replicated
The draws below stay inside these ranges and needn't reach their ends.
All inputs are finite; a program needn't handle non-finite values.
Results may differ from the reference program's by a relative error of at most 0.000073.
Values sent between devices are 32-bit elements; how exact they have to be, the bound alone decides.
No kernel may reach another device: no remote copies, remote signals or barrier semaphores. Data moves between devices by JAX's collectives and lax.ppermute only.
A program may use at most 64 MiB of HBM per device.

```python
import jax
import jax.numpy as jnp
from jax import lax

FEAT = 1024
RANK = 256
ROWS = 32768


def shard_levels(stream_key, shape, shards, low, top_value):
    def one(axis_at, shards_of):
        steps = jax.random.uniform(jax.random.fold_in(jax.random.fold_in(stream_key, 6), axis_at), (shards_of,), jnp.float32, low / len(shards), top_value / len(shards))
        return jnp.repeat(jnp.exp(steps), shape[axis_at] // shards_of).reshape((-1,) + (1,) * (len(shape) - axis_at - 1))

    gain = one(*shards[0])
    for cut in shards[1:]:
        gain = gain * one(*cut)
    return gain


def bell_draw(own_key, shape, spread, limit, shards=(), dtype=jnp.bfloat16):
    drawn = jax.random.normal(own_key, shape, jnp.float32) * spread
    if len(shards) > 0:
        drawn = shard_levels(own_key, shape, shards, -0.22, 0.18) * drawn
    return jnp.clip(drawn, min=-limit, max=limit).astype(dtype)


def setup_inputs(seed: int = 0) -> dict:
    keys = jax.random.split(jax.random.key(seed), 3)
    return {
        "features": bell_draw(keys[0], (ROWS, FEAT), 1.0, 6.0, ((0, 32),), jnp.float32),
        "sketch": bell_draw(keys[1], (FEAT, RANK), FEAT ** -0.5, 0.1875, (), jnp.float32),
    }


def reference(features, sketch):
    high = lax.Precision.HIGHEST
    sampled = jnp.dot(features.astype(jnp.float32), sketch.astype(jnp.float32), preferred_element_type=jnp.float32, precision=high)
    gram = jnp.dot(sampled.T.astype(jnp.float32), sampled.astype(jnp.float32), preferred_element_type=jnp.float32, precision=high)
    lower = jnp.linalg.cholesky(gram)
    ortho_t = lax.linalg.triangular_solve(lower, sampled.T, left_side=True, lower=True)
    scale = jnp.sqrt(jnp.float32(ROWS))
    projection = jnp.dot(ortho_t.astype(jnp.float32), features.astype(jnp.float32), preferred_element_type=jnp.float32, precision=high)
    return (ortho_t.T * scale, lower.T / scale, projection)
```

```python
import jax, jax.numpy as jnp
from jax import lax
from jax.experimental import pallas as pl
from jax.experimental.pallas import tpu as pltpu
from jax.sharding import PartitionSpec as P

GROUP = 8
LANES = 128
PANEL = 64


def factor_panel(a_ref, upper_ref, base, height, size):
    lane = lax.broadcasted_iota(jnp.int32, (GROUP, LANES), 1)
    sub = lax.broadcasted_iota(jnp.int32, (GROUP, LANES), 0)
    tiles = size // LANES
    for top in range(base, base + height, GROUP):
        groups = list(range(top, base + height, GROUP))
        home = top // LANES
        offset = top - home * LANES
        inside = (lane >= offset) & (lane < offset + GROUP)
        rows = {}
        for g in groups:
            for t in range(tiles):
                rows[g, t] = a_ref[g:g + GROUP, t * LANES:(t + 1) * LANES]
        diag = rows[top, home]
        col = {}
        for g in groups:
            for j in range(GROUP):
                at = rows[g, home][:, offset + j:offset + j + 1]
                col[g, j] = jnp.broadcast_to(at, (GROUP, LANES))
        one = {}
        for j in range(GROUP):
            for k in range(j, GROUP):
                one[k, j] = jnp.broadcast_to(col[top, j][k:k + 1, :], (GROUP, LANES))
        for g in groups:
            fresh = jnp.where(lane == sub + offset, 1.0, 0.0) if g == top else 0.0
            rows[g, home] = jnp.where(inside, fresh, rows[g, home])
        for j in range(GROUP):
            inv = lax.rsqrt(one[j, j])
            low = {k: one[k, j] * inv for k in range(j + 1, GROUP)}
            for k in range(j + 1, GROUP):
                for m in range(k, GROUP):
                    one[m, k] = one[m, k] - low[m] * low[k]
            scaled = {g: col[g, j] * inv for g in groups}
            for k in range(j + 1, GROUP):
                for g in groups:
                    col[g, k] = col[g, k] - scaled[g] * low[k]
            pivot = {t: jnp.broadcast_to(rows[top, t][j:j + 1, :], (GROUP, LANES)) * inv for t in range(tiles)}
            pivot_diag = jnp.broadcast_to(diag[j:j + 1, :], (GROUP, LANES)) * inv
            below = jnp.where(sub > j, scaled[top], 0.0)
            diag = jnp.where(sub == j, pivot_diag, diag - below * pivot_diag)
            for t in range(tiles):
                rows[top, t] = jnp.where(sub == j, pivot[t], rows[top, t] - below * pivot[t])
                for g in groups[1:]:
                    rows[g, t] = rows[g, t] - scaled[g] * pivot[t]
        for g in groups:
            for t in range(tiles):
                a_ref[g:g + GROUP, t * LANES:(t + 1) * LANES] = rows[g, t]
        for t in range(tiles):
            span = slice(t * LANES, (t + 1) * LANES)
            if t < home:
                upper_ref[top:top + GROUP, span] = jnp.zeros((GROUP, LANES), jnp.float32)
            elif t == home:
                upper_ref[top:top + GROUP, span] = jnp.where(lane >= sub + offset, diag, 0.0)
            else:
                upper_ref[top:top + GROUP, span] = rows[top, t]


def trailing(a_ref, base, height, size):
    end = base + height
    if end == size:
        return
    panel = a_ref[base:end, :]
    col = lax.broadcasted_iota(jnp.int32, (height, size), 1)
    row = lax.broadcasted_iota(jnp.int32, (height, size), 0) + base
    right = jnp.where((col <= row) | (col >= end), panel, 0.0)
    left = panel[:, end:]
    update = lax.dot_general(left, right, (((0,), (0,)), ((), ())), precision=lax.Precision.HIGHEST, preferred_element_type=jnp.float32)
    rest = a_ref[end:, :]
    at = lax.broadcasted_iota(jnp.int32, (size - end, size), 1)
    a_ref[end:, :] = jnp.where((at >= base) & (at < end), 0.0, rest) - update


def factor_kernel(gram_ref, upper_ref, inverse_ref, a_ref):
    size = gram_ref.shape[0]
    a_ref[...] = gram_ref[...]
    for base in range(0, size, PANEL):
        factor_panel(a_ref, upper_ref, base, PANEL, size)
        trailing(a_ref, base, PANEL, size)
    col = lax.broadcasted_iota(jnp.int32, (size, size), 1)
    row = lax.broadcasted_iota(jnp.int32, (size, size), 0)
    inverse_ref[...] = jnp.where(col <= row, a_ref[...], 0.0)


def factor_and_inverse(gram):
    size = gram.shape[0]
    vmem = pl.BlockSpec(memory_space=pltpu.VMEM)
    square = jax.ShapeDtypeStruct((size, size), jnp.float32)
    return pl.pallas_call(
        factor_kernel,
        out_shape=(square, square),
        in_specs=[vmem],
        out_specs=(vmem, vmem),
        scratch_shapes=[pltpu.VMEM((size, size), jnp.float32)],
        compiler_params=pltpu.CompilerParams(vmem_limit_bytes=16 * 2**20),
        cost_estimate=pl.CostEstimate(flops=100_000_000, bytes_accessed=1_000_000, transcendentals=256),
        name="factor_and_inverse",
    )(gram)


def swap(value, axis, bit):
    mask = 2**bit
    pairs = [(source, source ^ mask) for source in range(lax.axis_size(axis))]
    return lax.ppermute(value, axis, pairs)


def bit_of(axis, bit):
    return (lax.axis_index(axis) // 2**bit) % 2


def levels():
    wide = lax.axis_size("wide").bit_length() - 1
    narrow = lax.axis_size("narrow").bit_length() - 1
    return [("wide", 0)] + [("narrow", bit) for bit in range(narrow)] + [("wide", bit) for bit in range(1, wide)]


def halve(value, axis, bit):
    cut = 0 if value.shape[0] > GROUP else 1
    mine = bit_of(axis, bit) == 0
    first, second = jnp.split(value, 2, axis=cut)
    return jnp.where(mine, first, second) + swap(jnp.where(mine, second, first), axis, bit), cut


def unhalve(value, axis, bit, cut):
    other = swap(value, axis, bit)
    mine = bit_of(axis, bit) == 0
    return jnp.concatenate([jnp.where(mine, value, other), jnp.where(mine, other, value)], axis=cut)


def sum_everywhere(value, halvings):
    undo = []
    for at, (axis, bit) in enumerate(levels()):
        if at < halvings:
            value, cut = halve(value, axis, bit)
            undo.append((axis, bit, cut))
        else:
            value = value + swap(value, axis, bit)
    for axis, bit, cut in reversed(undo):
        value = unhalve(value, axis, bit, cut)
    return value


def per_device(features, sketch):
    high = lax.Precision.HIGH
    dot = lambda a, b: jnp.dot(a, b, preferred_element_type=jnp.float32, precision=high)
    sampled = dot(features, sketch)
    gram = sum_everywhere(dot(sampled.T, sampled), 1)
    cross = sum_everywhere(dot(sampled.T, features), len(levels()))
    upper, inverse = factor_and_inverse(gram)
    count = features.shape[0] * lax.axis_size("wide") * lax.axis_size("narrow")
    scale = jnp.sqrt(jnp.float32(count))
    basis = dot(sampled, (inverse * scale).T)
    return (basis, upper / scale, dot(inverse, cross))


def solution(mesh):
    in_specs = (P(("wide", "narrow"), None), P())
    out_specs = (P(("wide", "narrow"), None), P(), P())
    return jax.shard_map(
        per_device, mesh=mesh, in_specs=in_specs, out_specs=out_specs, check_vma=False
    )
```

```python
import jax, jax.numpy as jnp
from jax import lax
from jax.experimental import pallas as pl
from jax.experimental.pallas import tpu as pltpu
from jax.sharding import Mesh, PartitionSpec as P

GROUP = 8
LANES = 128
PANEL = 64


def factor_panel(a_ref, upper_ref, base, height, size):
    lane = lax.broadcasted_iota(jnp.int32, (GROUP, LANES), 1)
    sub = lax.broadcasted_iota(jnp.int32, (GROUP, LANES), 0)
    tiles = size // LANES
    for top in range(base, base + height, GROUP):
        groups = list(range(top, base + height, GROUP))
        home = top // LANES
        offset = top - home * LANES
        inside = (lane >= offset) & (lane < offset + GROUP)
        rows = {}
        for g in groups:
            for t in range(tiles):
                rows[g, t] = a_ref[g:g + GROUP, t * LANES:(t + 1) * LANES]
        diag = rows[top, home]
        col = {}
        for g in groups:
            for j in range(GROUP):
                at = rows[g, home][:, offset + j:offset + j + 1]
                col[g, j] = jnp.broadcast_to(at, (GROUP, LANES))
        one = {}
        for j in range(GROUP):
            for k in range(j, GROUP):
                one[k, j] = jnp.broadcast_to(col[top, j][k:k + 1, :], (GROUP, LANES))
        for g in groups:
            fresh = jnp.where(lane == sub + offset, 1.0, 0.0) if g == top else 0.0
            rows[g, home] = jnp.where(inside, fresh, rows[g, home])
        for j in range(GROUP):
            inv = lax.rsqrt(one[j, j])
            low = {k: one[k, j] * inv for k in range(j + 1, GROUP)}
            for k in range(j + 1, GROUP):
                for m in range(k, GROUP):
                    one[m, k] = one[m, k] - low[m] * low[k]
            scaled = {g: col[g, j] * inv for g in groups}
            for k in range(j + 1, GROUP):
                for g in groups:
                    col[g, k] = col[g, k] - scaled[g] * low[k]
            pivot = {t: jnp.broadcast_to(rows[top, t][j:j + 1, :], (GROUP, LANES)) * inv for t in range(tiles)}
            pivot_diag = jnp.broadcast_to(diag[j:j + 1, :], (GROUP, LANES)) * inv
            below = jnp.where(sub > j, scaled[top], 0.0)
            diag = jnp.where(sub == j, pivot_diag, diag - below * pivot_diag)
            for t in range(tiles):
                rows[top, t] = jnp.where(sub == j, pivot[t], rows[top, t] - below * pivot[t])
                for g in groups[1:]:
                    rows[g, t] = rows[g, t] - scaled[g] * pivot[t]
        for g in groups:
            for t in range(tiles):
                a_ref[g:g + GROUP, t * LANES:(t + 1) * LANES] = rows[g, t]
        for t in range(tiles):
            span = slice(t * LANES, (t + 1) * LANES)
            if t < home:
                upper_ref[top:top + GROUP, span] = jnp.zeros((GROUP, LANES), jnp.float32)
            elif t == home:
                upper_ref[top:top + GROUP, span] = jnp.where(lane >= sub + offset, diag, 0.0)
            else:
                upper_ref[top:top + GROUP, span] = rows[top, t]


def trailing(a_ref, base, height, size):
    end = base + height
    if end == size:
        return
    panel = a_ref[base:end, :]
    col = lax.broadcasted_iota(jnp.int32, (height, size), 1)
    row = lax.broadcasted_iota(jnp.int32, (height, size), 0) + base
    right = jnp.where((col <= row) | (col >= end), panel, 0.0)
    left = panel[:, end:]
    update = lax.dot_general(left, right, (((0,), (0,)), ((), ())), precision=lax.Precision.HIGHEST, preferred_element_type=jnp.float32)
    rest = a_ref[end:, :]
    at = lax.broadcasted_iota(jnp.int32, (size - end, size), 1)
    a_ref[end:, :] = jnp.where((at >= base) & (at < end), 0.0, rest) - update


def factor_kernel(gram_ref, upper_ref, inverse_ref, a_ref):
    size = gram_ref.shape[0]
    a_ref[...] = gram_ref[...]
    for base in range(0, size, PANEL):
        factor_panel(a_ref, upper_ref, base, PANEL, size)
        trailing(a_ref, base, PANEL, size)
    col = lax.broadcasted_iota(jnp.int32, (size, size), 1)
    row = lax.broadcasted_iota(jnp.int32, (size, size), 0)
    inverse_ref[...] = jnp.where(col <= row, a_ref[...], 0.0)


def factor_and_inverse(gram):
    size = gram.shape[0]
    vmem = pl.BlockSpec(memory_space=pltpu.VMEM)
    square = jax.ShapeDtypeStruct((size, size), jnp.float32)
    return pl.pallas_call(
        factor_kernel,
        out_shape=(square, square),
        in_specs=[vmem],
        out_specs=(vmem, vmem),
        scratch_shapes=[pltpu.VMEM((size, size), jnp.float32)],
        compiler_params=pltpu.CompilerParams(vmem_limit_bytes=16 * 2**20),
        cost_estimate=pl.CostEstimate(flops=100_000_000, bytes_accessed=1_000_000, transcendentals=256),
        name="factor_and_inverse",
    )(gram)


CHIPS = ("chip", "narrow")


def exchange(blocks, axes):
    return lax.all_to_all(blocks, axes, 0, 0, tiled=True)


def scatter_sum(value, axes):
    count = lax.axis_size(axes)
    blocks = value.reshape((count, value.shape[0] // count) + value.shape[1:])
    return jnp.sum(exchange(blocks, axes), axis=0)


def gather(value, axes):
    count = lax.axis_size(axes)
    blocks = exchange(jnp.broadcast_to(value, (count,) + value.shape), axes)
    return blocks.reshape((count * value.shape[0],) + value.shape[1:])


def sum_everywhere(value):
    half = scatter_sum(value, "core")
    rows, columns = half.shape
    count = lax.axis_size(CHIPS)
    tall = max(rows, count * GROUP)
    own = scatter_sum(half.reshape(tall, rows * columns // tall), CHIPS)
    half = gather(own, CHIPS).reshape(rows, columns)
    return gather(half, "core")


def per_device(features, sketch):
    high = lax.Precision.HIGH
    dot = lambda a, b: jnp.dot(a, b, preferred_element_type=jnp.float32, precision=high)
    sampled = dot(features, sketch)
    terms = jnp.concatenate([dot(sampled.T, sampled), dot(sampled.T, features)], axis=1)
    summed = sum_everywhere(terms)
    gram, cross = jnp.split(summed, [sampled.shape[1]], axis=1)
    upper, inverse = factor_and_inverse(gram)
    count = features.shape[0] * lax.axis_size(("chip", "core", "narrow"))
    scale = jnp.sqrt(jnp.float32(count))
    basis = dot(sampled, (inverse * scale).T)
    return (basis, upper / scale, dot(inverse, cross))


def solution(mesh):
    wide, narrow = mesh.shape["wide"], mesh.shape["narrow"]
    split = Mesh(mesh.devices.reshape(wide // 2, 2, narrow), ("chip", "core", "narrow"))
    rows = P(("chip", "core", "narrow"), None)
    return jax.shard_map(
        per_device, mesh=split, in_specs=(rows, P()), out_specs=(rows, P(), P()), check_vma=False
    )
```

```python
import jax, jax.numpy as jnp
from jax import lax
from jax.experimental import pallas as pl
from jax.experimental.pallas import tpu as pltpu
from jax.sharding import PartitionSpec as P

GROUP = 8
LANES = 128
PANEL = 64
BLOCK = 256
BLOCKS = 32
AXES = ("wide", "narrow")
VMEM = pl.BlockSpec(memory_space=pltpu.VMEM)


def factor_panel(a_ref, factor_ref, scale, base, height, size):
    lane = lax.broadcasted_iota(jnp.int32, (GROUP, LANES), 1)
    sub = lax.broadcasted_iota(jnp.int32, (GROUP, LANES), 0)
    tiles = size // LANES
    for top in range(base, base + height, GROUP):
        groups = list(range(top, base + height, GROUP))
        home = top // LANES
        offset = top - home * LANES
        inside = (lane >= offset) & (lane < offset + GROUP)
        rows = {}
        for g in groups:
            for t in range(tiles):
                rows[g, t] = a_ref[g:g + GROUP, t * LANES:(t + 1) * LANES]
        diag = rows[top, home]
        col = {}
        for g in groups:
            for j in range(GROUP):
                at = rows[g, home][:, offset + j:offset + j + 1]
                col[g, j] = jnp.broadcast_to(at, (GROUP, LANES))
        one = {}
        for j in range(GROUP):
            for k in range(j, GROUP):
                one[k, j] = jnp.broadcast_to(col[top, j][k:k + 1, :], (GROUP, LANES))
        for g in groups:
            fresh = jnp.where(lane == sub + offset, 1.0, 0.0) if g == top else 0.0
            rows[g, home] = jnp.where(inside, fresh, rows[g, home])
        for j in range(GROUP):
            inv = lax.rsqrt(one[j, j])
            low = {k: one[k, j] * inv for k in range(j + 1, GROUP)}
            for k in range(j + 1, GROUP):
                for m in range(k, GROUP):
                    one[m, k] = one[m, k] - low[m] * low[k]
            scaled = {g: col[g, j] * inv for g in groups}
            for k in range(j + 1, GROUP):
                for g in groups:
                    col[g, k] = col[g, k] - scaled[g] * low[k]
            pivot = {t: jnp.broadcast_to(rows[top, t][j:j + 1, :], (GROUP, LANES)) * inv for t in range(tiles)}
            pivot_diag = jnp.broadcast_to(diag[j:j + 1, :], (GROUP, LANES)) * inv
            below = jnp.where(sub > j, scaled[top], 0.0)
            diag = jnp.where(sub == j, pivot_diag, diag - below * pivot_diag)
            for t in range(tiles):
                rows[top, t] = jnp.where(sub == j, pivot[t], rows[top, t] - below * pivot[t])
                for g in groups[1:]:
                    rows[g, t] = rows[g, t] - scaled[g] * pivot[t]
        for g in groups:
            for t in range(tiles):
                a_ref[g:g + GROUP, t * LANES:(t + 1) * LANES] = rows[g, t]
        for t in range(tiles):
            span = slice(t * LANES, (t + 1) * LANES)
            if t < home:
                factor_ref[top:top + GROUP, span] = jnp.zeros((GROUP, LANES), jnp.float32)
            elif t == home:
                factor_ref[top:top + GROUP, span] = jnp.where(lane >= sub + offset, diag / scale, 0.0)
            else:
                factor_ref[top:top + GROUP, span] = rows[top, t] / scale


def trailing(a_ref, base, height, size):
    end = base + height
    if end == size:
        return
    panel = a_ref[base:end, :]
    col = lax.broadcasted_iota(jnp.int32, (height, size), 1)
    row = lax.broadcasted_iota(jnp.int32, (height, size), 0) + base
    right = jnp.where((col <= row) | (col >= end), panel, 0.0)
    left = panel[:, end:]
    update = lax.dot_general(left, right, (((0,), (0,)), ((), ())), precision=lax.Precision.HIGHEST, preferred_element_type=jnp.float32)
    rest = a_ref[end:, :]
    at = lax.broadcasted_iota(jnp.int32, (size - end, size), 1)
    a_ref[end:, :] = jnp.where((at >= base) & (at < end), 0.0, rest) - update


def split(value):
    high = value.astype(jnp.bfloat16)
    return high, (value - high.astype(jnp.float32)).astype(jnp.bfloat16)


def product(left, right, left_dim, right_dim):
    dims = (((left_dim,), (right_dim,)), ((), ()))
    dot = lambda a, b: lax.dot_general(a, b, dims, preferred_element_type=jnp.float32)
    return dot(left[0], right[0]) + (dot(left[0], right[1]) + dot(left[1], right[0]))


def core_bit():
    return lax.rem(lax.axis_index("wide"), 2)


def own_block():
    wide, narrow = lax.axis_index("wide"), lax.axis_index("narrow")
    plane = lax.rem(narrow, 2) + 2 * lax.rem(wide // 2, 2)
    return 16 * lax.rem(wide, 2) + 4 * plane + lax.rem(wide // 4, 4)


def rows_of(block, height):
    return pl.ds(pl.multiple_of(block * height, GROUP), height)


def local_kernel(features_ref, sketch_ref, sampled_ref, keep_ref, send_ref, gram_keep_ref, gram_send_ref, high_ref, low_ref, cross_ref, gram_ref, packed_ref):
    step = pl.program_id(0)

    @pl.when(step == 0)
    def _():
        high_ref[...], low_ref[...] = split(sketch_ref[...])
        cross_ref[...] = jnp.zeros_like(cross_ref)
        gram_ref[...] = jnp.zeros_like(gram_ref)

    features = split(features_ref[...])
    sampled = product(features, (high_ref[...], low_ref[...]), 1, 0)
    sampled_ref[...] = sampled
    parts = split(sampled)
    cross_ref[...] += product(parts, features, 0, 0)
    gram_ref[...] += product(parts, parts, 0, 0)

    @pl.when(step == pl.num_programs(0) - 1)
    def _():
        own = own_block()
        height = cross_ref.shape[0] // BLOCKS
        for at in range(BLOCKS):
            block = cross_ref[rows_of(at ^ own, height), :]
            if at < BLOCKS // 2:
                keep_ref[at * height:(at + 1) * height, :] = block
            else:
                rest = at - BLOCKS // 2
                send_ref[rest * height:(rest + 1) * height, :] = block
        packed_ref[:LANES, :] = gram_ref[:LANES, :LANES]
        packed_ref[LANES:2 * LANES, :] = gram_ref[:LANES, LANES:]
        packed_ref[2 * LANES:, :] = gram_ref[LANES:, LANES:]
        half = packed_ref.shape[0] // 2
        core = core_bit()
        gram_keep_ref[...] = packed_ref[rows_of(core, half), :]
        gram_send_ref[...] = packed_ref[rows_of(1 - core, half), :]


def local_terms(features, sketch):
    rows, depth = features.shape
    rank = sketch.shape[1]
    f32 = lambda *shape: jax.ShapeDtypeStruct(shape, jnp.float32)
    whole = lambda *shape: pl.BlockSpec(shape, lambda i: (0, 0))
    packed = 3 * LANES
    return pl.pallas_call(
        local_kernel,
        grid=(rows // BLOCK,),
        out_shape=(f32(rows, rank), f32(rank // 2, depth), f32(rank // 2, depth), f32(packed // 2, LANES), f32(packed // 2, LANES)),
        in_specs=[pl.BlockSpec((BLOCK, depth), lambda i: (i, 0)), whole(depth, rank)],
        out_specs=(
            pl.BlockSpec((BLOCK, rank), lambda i: (i, 0)),
            whole(rank // 2, depth), whole(rank // 2, depth),
            whole(packed // 2, LANES), whole(packed // 2, LANES),
        ),
        scratch_shapes=[
            pltpu.VMEM((depth, rank), jnp.bfloat16), pltpu.VMEM((depth, rank), jnp.bfloat16),
            pltpu.VMEM((rank, depth), jnp.float32), pltpu.VMEM((rank, rank), jnp.float32),
            pltpu.VMEM((packed, LANES), jnp.float32),
        ],
        compiler_params=pltpu.CompilerParams(vmem_limit_bytes=32 * 2**20),
        cost_estimate=pl.CostEstimate(flops=4 * 10**9, bytes_accessed=8 * 2**20, transcendentals=0),
        name="local_terms",
    )(features, sketch)


def factor_kernel(scale, first, last, *refs):
    if first == 0:
        keep_ref, other_ref, a_ref, factor_ref, packed_ref = refs
        half = keep_ref.shape[0]
        core = core_bit()
        packed_ref[rows_of(core, half), :] = keep_ref[...]
        packed_ref[rows_of(1 - core, half), :] = other_ref[...]
        a_ref[:LANES, :LANES] = packed_ref[:LANES, :]
        a_ref[:LANES, LANES:] = packed_ref[LANES:2 * LANES, :]
        a_ref[LANES:, :LANES] = jnp.zeros((LANES, LANES), jnp.float32)
        a_ref[LANES:, LANES:] = packed_ref[2 * LANES:, :]
    else:
        from_ref, upper_ref, a_ref, factor_ref = refs
        a_ref[...] = from_ref[...]
        factor_ref[...] = upper_ref[...]
    size = a_ref.shape[0]
    for base in range(first, last, PANEL):
        factor_panel(a_ref, factor_ref, scale, base, PANEL, size)
        trailing(a_ref, base, PANEL, size)
    if last == size:
        col = lax.broadcasted_iota(jnp.int32, (size, size), 1)
        row = lax.broadcasted_iota(jnp.int32, (size, size), 0)
        a_ref[...] = jnp.where(col <= row, a_ref[...], 0.0)


def factor_part(operands, size, scale, first, last):
    square = jax.ShapeDtypeStruct((size, size), jnp.float32)
    return pl.pallas_call(
        lambda *refs: factor_kernel(scale, first, last, *refs),
        out_shape=(square, square),
        in_specs=[VMEM] * 2,
        out_specs=(VMEM, VMEM),
        scratch_shapes=[pltpu.VMEM((3 * LANES, LANES), jnp.float32)] if first == 0 else [],
        compiler_params=pltpu.CompilerParams(vmem_limit_bytes=16 * 2**20),
        cost_estimate=pl.CostEstimate(flops=10**9 * (last - first) // size, bytes_accessed=2**20, transcendentals=last - first),
        name="factor_part",
    )(*operands)


def basis_kernel(scale, sampled_ref, inverse_ref, basis_ref):
    basis_ref[...] = product(split(sampled_ref[...]), split(inverse_ref[...] * scale), 1, 1)


def basis_of(sampled, inverse, scale):
    rows, rank = sampled.shape
    return pl.pallas_call(
        lambda *refs: basis_kernel(scale, *refs),
        grid=(rows // BLOCK,),
        out_shape=jax.ShapeDtypeStruct(sampled.shape, jnp.float32),
        in_specs=[pl.BlockSpec((BLOCK, rank), lambda i: (i, 0)), pl.BlockSpec((rank, rank), lambda i: (0, 0))],
        out_specs=pl.BlockSpec((BLOCK, rank), lambda i: (i, 0)),
        cost_estimate=pl.CostEstimate(flops=4 * 10**8, bytes_accessed=2 * 2**20, transcendentals=0),
        name="basis",
    )(sampled, inverse)


def project_kernel(inverse_ref, *refs):
    *pieces, projection_ref, cross_ref = refs
    own = own_block()
    height = cross_ref.shape[0] // BLOCKS
    at = 0
    for piece in pieces:
        for top in range(0, piece.shape[0], height):
            cross_ref[rows_of(at ^ own, height), :] = piece[top:top + height, :]
            at += 1
    inverse = split(inverse_ref[...])
    for left in range(0, cross_ref.shape[1], BLOCK):
        span = slice(left, left + BLOCK)
        projection_ref[:, span] = product(inverse, split(cross_ref[:, span]), 1, 0)


def project(inverse, pieces):
    rank = inverse.shape[0]
    depth = pieces[0].shape[1]
    return pl.pallas_call(
        project_kernel,
        out_shape=jax.ShapeDtypeStruct((rank, depth), jnp.float32),
        in_specs=[VMEM] * (1 + len(pieces)),
        out_specs=VMEM,
        scratch_shapes=[pltpu.VMEM((rank, depth), jnp.float32)],
        compiler_params=pltpu.CompilerParams(vmem_limit_bytes=16 * 2**20),
        cost_estimate=pl.CostEstimate(flops=4 * 10**8, bytes_accessed=2 * 2**20, transcendentals=0),
        name="project",
    )(inverse, *pieces)


def send(value, wide, narrow):
    mask = wide * lax.axis_size("narrow") + narrow
    pairs = [(source, source ^ mask) for source in range(lax.axis_size(AXES))]
    return lax.ppermute(value, AXES, pairs)


CORE = (1, 0)
PLANE = [(0, 1), (2, 0), (2, 1)]
LINE = [(4, 0), (8, 0), (12, 0)]


def spare_bits():
    wide = [(2**bit, 0) for bit in range(4, lax.axis_size("wide").bit_length() - 1)]
    narrow = [(0, 2**bit) for bit in range(1, lax.axis_size("narrow").bit_length() - 1)]
    return wide + narrow


def sum_gram(keep, other):
    half = keep + send(other, *CORE)
    for mask in [(0, 1), (2, 0), (4, 0), (8, 0)] + spare_bits():
        half = half + send(half, *mask)
    return half, send(half, *CORE)


def quarters(values):
    height = values[0].shape[0] // 4
    return [sum(value[at * height:(at + 1) * height] for value in values) for at in range(4)]


def scatter(values, masks):
    first, *rest = quarters(values)
    return [first] + [send(part, *mask) for part, mask in zip(rest, masks)]


def sum_cross(keep, other):
    values = scatter([keep, send(other, *CORE)], PLANE)
    values = scatter(values, LINE)
    own = sum(values)
    for mask in spare_bits():
        own = own + send(own, *mask)
    line = jnp.concatenate([own] + [send(own, *mask) for mask in LINE])
    plane = [line] + [send(line, *mask) for mask in PLANE]
    return plane + [send(part, *CORE) for part in plane]


def per_device(features, sketch):
    scale = (features.shape[0] * lax.axis_size(AXES)) ** 0.5
    size = sketch.shape[1]
    sampled, keep, other, gram_keep, gram_other = local_terms(features, sketch)
    gram = sum_gram(gram_keep, gram_other)
    cross = sum_cross(keep, other)
    state = factor_part(gram, size, scale, 0, size // 2)
    inverse, factor = factor_part(state, size, scale, size // 2, size)
    return (basis_of(sampled, inverse, scale), factor, project(inverse, cross))


def solution(mesh):
    rows = P(AXES, None)
    return jax.shard_map(
        per_device, mesh=mesh, in_specs=(rows, P()), out_specs=(rows, P(), P()), check_vma=False
    )
```

```python
import jax, jax.numpy as jnp
from jax import lax
from jax.experimental import pallas as pl
from jax.experimental.pallas import tpu as pltpu
from jax.sharding import PartitionSpec as P

GROUP = 8
LANES = 128
PANEL = 64
BLOCK = 256
BLOCKS = 32
AXES = ("wide", "narrow")
VMEM = pl.BlockSpec(memory_space=pltpu.VMEM)


def factor_panel(a_ref, factor_ref, scale, base, height, size):
    lane = lax.broadcasted_iota(jnp.int32, (GROUP, LANES), 1)
    sub = lax.broadcasted_iota(jnp.int32, (GROUP, LANES), 0)
    tiles = size // LANES
    for top in range(base, base + height, GROUP):
        groups = list(range(top, base + height, GROUP))
        home = top // LANES
        offset = top - home * LANES
        inside = (lane >= offset) & (lane < offset + GROUP)
        rows = {}
        for g in groups:
            for t in range(tiles):
                rows[g, t] = a_ref[g:g + GROUP, t * LANES:(t + 1) * LANES]
        diag = rows[top, home]
        col = {}
        for g in groups:
            for j in range(GROUP):
                at = rows[g, home][:, offset + j:offset + j + 1]
                col[g, j] = jnp.broadcast_to(at, (GROUP, LANES))
        one = {}
        for j in range(GROUP):
            for k in range(j, GROUP):
                one[k, j] = jnp.broadcast_to(col[top, j][k:k + 1, :], (GROUP, LANES))
        for g in groups:
            fresh = jnp.where(lane == sub + offset, 1.0, 0.0) if g == top else 0.0
            rows[g, home] = jnp.where(inside, fresh, rows[g, home])
        for j in range(GROUP):
            inv = lax.rsqrt(one[j, j])
            low = {k: one[k, j] * inv for k in range(j + 1, GROUP)}
            for k in range(j + 1, GROUP):
                for m in range(k, GROUP):
                    one[m, k] = one[m, k] - low[m] * low[k]
            scaled = {g: col[g, j] * inv for g in groups}
            for k in range(j + 1, GROUP):
                for g in groups:
                    col[g, k] = col[g, k] - scaled[g] * low[k]
            pivot = {t: jnp.broadcast_to(rows[top, t][j:j + 1, :], (GROUP, LANES)) * inv for t in range(tiles)}
            pivot_diag = jnp.broadcast_to(diag[j:j + 1, :], (GROUP, LANES)) * inv
            below = jnp.where(sub > j, scaled[top], 0.0)
            diag = jnp.where(sub == j, pivot_diag, diag - below * pivot_diag)
            for t in range(tiles):
                rows[top, t] = jnp.where(sub == j, pivot[t], rows[top, t] - below * pivot[t])
                for g in groups[1:]:
                    rows[g, t] = rows[g, t] - scaled[g] * pivot[t]
        for g in groups:
            for t in range(tiles):
                a_ref[g:g + GROUP, t * LANES:(t + 1) * LANES] = rows[g, t]
        for t in range(tiles):
            span = slice(t * LANES, (t + 1) * LANES)
            if t < home:
                factor_ref[top:top + GROUP, span] = jnp.zeros((GROUP, LANES), jnp.float32)
            elif t == home:
                factor_ref[top:top + GROUP, span] = jnp.where(lane >= sub + offset, diag / scale, 0.0)
            else:
                factor_ref[top:top + GROUP, span] = rows[top, t] / scale


def trailing(a_ref, base, height, size):
    end = base + height
    if end == size:
        return
    panel = a_ref[base:end, :]
    col = lax.broadcasted_iota(jnp.int32, (height, size), 1)
    row = lax.broadcasted_iota(jnp.int32, (height, size), 0) + base
    right = jnp.where((col <= row) | (col >= end), panel, 0.0)
    left = panel[:, end:]
    update = lax.dot_general(left, right, (((0,), (0,)), ((), ())), precision=lax.Precision.HIGHEST, preferred_element_type=jnp.float32)
    rest = a_ref[end:, :]
    at = lax.broadcasted_iota(jnp.int32, (size - end, size), 1)
    a_ref[end:, :] = jnp.where((at >= base) & (at < end), 0.0, rest) - update


def split(value):
    high = value.astype(jnp.bfloat16)
    return high, (value - high.astype(jnp.float32)).astype(jnp.bfloat16)


def product(left, right, left_dim, right_dim):
    dims = (((left_dim,), (right_dim,)), ((), ()))
    dot = lambda a, b: lax.dot_general(a, b, dims, preferred_element_type=jnp.float32)
    return dot(left[0], right[0]) + (dot(left[0], right[1]) + dot(left[1], right[0]))


def core_bit():
    return lax.rem(lax.axis_index("wide"), 2)


def own_block():
    wide, narrow = lax.axis_index("wide"), lax.axis_index("narrow")
    plane = lax.rem(narrow, 2) + 2 * lax.rem(wide // 2, 2)
    return 16 * lax.rem(wide, 2) + 4 * plane + lax.rem(wide // 4, 4)


def rows_of(block, height):
    return pl.ds(pl.multiple_of(block * height, GROUP), height)


def local_kernel(features_ref, sketch_ref, sampled_ref, keep_ref, send_ref, gram_keep_ref, gram_send_ref, high_ref, low_ref, cross_ref, gram_ref, packed_ref):
    step = pl.program_id(0)

    @pl.when(step == 0)
    def _():
        high_ref[...], low_ref[...] = split(sketch_ref[...])
        cross_ref[...] = jnp.zeros_like(cross_ref)
        gram_ref[...] = jnp.zeros_like(gram_ref)

    features = split(features_ref[...])
    sampled = product(features, (high_ref[...], low_ref[...]), 1, 0)
    sampled_ref[...] = sampled
    flipped = split(sampled.T)
    cross_ref[...] += product(flipped, features, 1, 0)
    gram_ref[...] += product(flipped, split(sampled), 1, 0)

    @pl.when(step == pl.num_programs(0) - 1)
    def _():
        own = own_block()
        height = cross_ref.shape[0] // BLOCKS
        for at in range(BLOCKS):
            block = cross_ref[rows_of(at ^ own, height), :]
            if at < BLOCKS // 2:
                keep_ref[at * height:(at + 1) * height, :] = block
            else:
                rest = at - BLOCKS // 2
                send_ref[rest * height:(rest + 1) * height, :] = block
        packed_ref[:LANES, :] = gram_ref[:LANES, :LANES]
        packed_ref[LANES:2 * LANES, :] = gram_ref[:LANES, LANES:]
        packed_ref[2 * LANES:, :] = gram_ref[LANES:, LANES:]
        half = packed_ref.shape[0] // 2
        core = core_bit()
        gram_keep_ref[...] = packed_ref[rows_of(core, half), :]
        gram_send_ref[...] = packed_ref[rows_of(1 - core, half), :]


def local_terms(features, sketch):
    rows, depth = features.shape
    rank = sketch.shape[1]
    f32 = lambda *shape: jax.ShapeDtypeStruct(shape, jnp.float32)
    whole = lambda *shape: pl.BlockSpec(shape, lambda i: (0, 0))
    packed = 3 * LANES
    return pl.pallas_call(
        local_kernel,
        grid=(rows // BLOCK,),
        out_shape=(f32(rows, rank), f32(rank // 2, depth), f32(rank // 2, depth), f32(packed // 2, LANES), f32(packed // 2, LANES)),
        in_specs=[pl.BlockSpec((BLOCK, depth), lambda i: (i, 0)), whole(depth, rank)],
        out_specs=(
            pl.BlockSpec((BLOCK, rank), lambda i: (i, 0)),
            whole(rank // 2, depth), whole(rank // 2, depth),
            whole(packed // 2, LANES), whole(packed // 2, LANES),
        ),
        scratch_shapes=[
            pltpu.VMEM((depth, rank), jnp.bfloat16), pltpu.VMEM((depth, rank), jnp.bfloat16),
            pltpu.VMEM((rank, depth), jnp.float32), pltpu.VMEM((rank, rank), jnp.float32),
            pltpu.VMEM((packed, LANES), jnp.float32),
        ],
        compiler_params=pltpu.CompilerParams(vmem_limit_bytes=58 * 2**20),
        cost_estimate=pl.CostEstimate(flops=4 * 10**9, bytes_accessed=8 * 2**20, transcendentals=0),
        name="local_terms",
    )(features, sketch)


def factor_kernel(scale, first, last, *refs):
    if first == 0:
        keep_ref, other_ref, a_ref, factor_ref, packed_ref = refs
        half = keep_ref.shape[0]
        core = core_bit()
        packed_ref[rows_of(core, half), :] = keep_ref[...]
        packed_ref[rows_of(1 - core, half), :] = other_ref[...]
        a_ref[:LANES, :LANES] = packed_ref[:LANES, :]
        a_ref[:LANES, LANES:] = packed_ref[LANES:2 * LANES, :]
        a_ref[LANES:, :LANES] = jnp.zeros((LANES, LANES), jnp.float32)
        a_ref[LANES:, LANES:] = packed_ref[2 * LANES:, :]
    else:
        from_ref, upper_ref, a_ref, factor_ref, *flipped_ref = refs
        a_ref[...] = from_ref[...]
        factor_ref[:first, :] = upper_ref[:first, :]
    size = a_ref.shape[0]
    for base in range(first, last, PANEL):
        factor_panel(a_ref, factor_ref, scale, base, PANEL, size)
        trailing(a_ref, base, PANEL, size)
    if last == size:
        col = lax.broadcasted_iota(jnp.int32, (size, size), 1)
        row = lax.broadcasted_iota(jnp.int32, (size, size), 0)
        inverse = jnp.where(col <= row, a_ref[...], 0.0)
        a_ref[...] = inverse
        flipped_ref[0][...] = inverse.T * scale


def factor_part(operands, size, scale, first, last):
    square = jax.ShapeDtypeStruct((size, size), jnp.float32)
    outs = 3 if last == size else 2
    return pl.pallas_call(
        lambda *refs: factor_kernel(scale, first, last, *refs),
        out_shape=(square,) * outs,
        in_specs=[VMEM] * 2,
        out_specs=(VMEM,) * outs,
        scratch_shapes=[pltpu.VMEM((3 * LANES, LANES), jnp.float32)] if first == 0 else [],
        compiler_params=pltpu.CompilerParams(vmem_limit_bytes=16 * 2**20),
        cost_estimate=pl.CostEstimate(flops=12 * 10**9 * (last - first) // size, bytes_accessed=2**20, transcendentals=last - first),
        name="factor_part",
    )(*operands)


def basis_kernel(sampled_ref, flipped_ref, basis_ref):
    basis_ref[...] = product(split(sampled_ref[...]), split(flipped_ref[...]), 1, 0)


def basis_of(sampled, flipped):
    rows, rank = sampled.shape
    return pl.pallas_call(
        basis_kernel,
        grid=(rows // BLOCK,),
        out_shape=jax.ShapeDtypeStruct(sampled.shape, jnp.float32),
        in_specs=[pl.BlockSpec((BLOCK, rank), lambda i: (i, 0)), pl.BlockSpec((rank, rank), lambda i: (0, 0))],
        out_specs=pl.BlockSpec((BLOCK, rank), lambda i: (i, 0)),
        cost_estimate=pl.CostEstimate(flops=4 * 10**8, bytes_accessed=2 * 2**20, transcendentals=0),
        name="basis",
    )(sampled, flipped)


def project_kernel(inverse_ref, *refs):
    *pieces, projection_ref, cross_ref = refs
    own = own_block()
    height = cross_ref.shape[0] // BLOCKS
    at = 0
    for piece in pieces:
        for top in range(0, piece.shape[0], height):
            cross_ref[rows_of(at ^ own, height), :] = piece[top:top + height, :]
            at += 1
    inverse = split(inverse_ref[...])
    for left in range(0, cross_ref.shape[1], BLOCK):
        span = slice(left, left + BLOCK)
        projection_ref[:, span] = product(inverse, split(cross_ref[:, span]), 1, 0)


def project(inverse, pieces):
    rank = inverse.shape[0]
    depth = pieces[0].shape[1]
    return pl.pallas_call(
        project_kernel,
        out_shape=jax.ShapeDtypeStruct((rank, depth), jnp.float32),
        in_specs=[VMEM] * (1 + len(pieces)),
        out_specs=VMEM,
        scratch_shapes=[pltpu.VMEM((rank, depth), jnp.float32)],
        compiler_params=pltpu.CompilerParams(vmem_limit_bytes=16 * 2**20),
        cost_estimate=pl.CostEstimate(flops=4 * 10**8, bytes_accessed=2 * 2**20, transcendentals=0),
        name="project",
    )(inverse, *pieces)


def send(value, wide, narrow):
    mask = wide * lax.axis_size("narrow") + narrow
    pairs = [(source, source ^ mask) for source in range(lax.axis_size(AXES))]
    return lax.ppermute(value, AXES, pairs)


CORE = (1, 0)
PLANE = [(0, 1), (2, 0), (2, 1)]
LINE = [(4, 0), (8, 0), (12, 0)]


def spare_bits():
    wide = [(2**bit, 0) for bit in range(4, lax.axis_size("wide").bit_length() - 1)]
    narrow = [(0, 2**bit) for bit in range(1, lax.axis_size("narrow").bit_length() - 1)]
    return wide + narrow


def sum_gram(keep, other):
    half = keep + send(other, *CORE)
    for mask in [(0, 1), (2, 0), (4, 0), (8, 0)] + spare_bits():
        half = half + send(half, *mask)
    return half, send(half, *CORE)


def quarters(values):
    height = values[0].shape[0] // 4
    return [sum(value[at * height:(at + 1) * height] for value in values) for at in range(4)]


def scatter(values, masks):
    first, *rest = quarters(values)
    return [first] + [send(part, *mask) for part, mask in zip(rest, masks)]


def sum_cross(keep, other):
    values = scatter([keep, send(other, *CORE)], PLANE)
    values = scatter(values, LINE)
    own = sum(values)
    for mask in spare_bits():
        own = own + send(own, *mask)
    line = jnp.concatenate([own] + [send(own, *mask) for mask in LINE])
    plane = [line] + [send(line, *mask) for mask in PLANE]
    return plane + [send(part, *CORE) for part in plane]


def per_device(features, sketch):
    scale = (features.shape[0] * lax.axis_size(AXES)) ** 0.5
    size = sketch.shape[1]
    sampled, keep, other, gram_keep, gram_other = local_terms(features, sketch)
    gram = sum_gram(gram_keep, gram_other)
    cross = sum_cross(keep, other)
    state = gram
    for first in range(0, size, PANEL):
        state = factor_part(state[:2], size, scale, first, first + PANEL)
    inverse, factor, flipped = state
    return (basis_of(sampled, flipped), factor, project(inverse, cross))


def solution(mesh):
    rows = P(AXES, None)
    return jax.shard_map(
        per_device, mesh=mesh, in_specs=(rows, P()), out_specs=(rows, P(), P()), check_vma=False
    )
```

```python
import jax, jax.numpy as jnp
from jax import lax
from jax.experimental import pallas as pl
from jax.experimental.pallas import tpu as pltpu
from jax.sharding import PartitionSpec as P

GROUP = 8
LANES = 128
PANEL = 64
BLOCK = 256
BLOCKS = 32
AXES = ("wide", "narrow")
VMEM = pl.BlockSpec(memory_space=pltpu.VMEM)


def factor_panel(a_ref, factor_ref, scale, base, height, size):
    lane = lax.broadcasted_iota(jnp.int32, (GROUP, LANES), 1)
    sub = lax.broadcasted_iota(jnp.int32, (GROUP, LANES), 0)
    tiles = size // LANES
    for top in range(base, base + height, GROUP):
        groups = list(range(top, base + height, GROUP))
        home = top // LANES
        offset = top - home * LANES
        inside = (lane >= offset) & (lane < offset + GROUP)
        rows = {}
        for g in groups:
            for t in range(tiles):
                rows[g, t] = a_ref[g:g + GROUP, t * LANES:(t + 1) * LANES]
        diag = rows[top, home]
        col = {}
        for g in groups:
            for j in range(GROUP):
                at = rows[g, home][:, offset + j:offset + j + 1]
                col[g, j] = jnp.broadcast_to(at, (GROUP, LANES))
        one = {}
        for j in range(GROUP):
            for k in range(j, GROUP):
                one[k, j] = jnp.broadcast_to(col[top, j][k:k + 1, :], (GROUP, LANES))
        for g in groups:
            fresh = jnp.where(lane == sub + offset, 1.0, 0.0) if g == top else 0.0
            rows[g, home] = jnp.where(inside, fresh, rows[g, home])
        for j in range(GROUP):
            inv = lax.rsqrt(one[j, j])
            low = {k: one[k, j] * inv for k in range(j + 1, GROUP)}
            for k in range(j + 1, GROUP):
                for m in range(k, GROUP):
                    one[m, k] = one[m, k] - low[m] * low[k]
            scaled = {g: col[g, j] * inv for g in groups}
            for k in range(j + 1, GROUP):
                for g in groups:
                    col[g, k] = col[g, k] - scaled[g] * low[k]
            pivot = {t: jnp.broadcast_to(rows[top, t][j:j + 1, :], (GROUP, LANES)) * inv for t in range(tiles)}
            pivot_diag = jnp.broadcast_to(diag[j:j + 1, :], (GROUP, LANES)) * inv
            below = jnp.where(sub > j, scaled[top], 0.0)
            diag = jnp.where(sub == j, pivot_diag, diag - below * pivot_diag)
            for t in range(tiles):
                rows[top, t] = jnp.where(sub == j, pivot[t], rows[top, t] - below * pivot[t])
                for g in groups[1:]:
                    rows[g, t] = rows[g, t] - scaled[g] * pivot[t]
        for g in groups:
            for t in range(tiles):
                a_ref[g:g + GROUP, t * LANES:(t + 1) * LANES] = rows[g, t]
        for t in range(tiles):
            span = slice(t * LANES, (t + 1) * LANES)
            if t < home:
                factor_ref[top:top + GROUP, span] = jnp.zeros((GROUP, LANES), jnp.float32)
            elif t == home:
                factor_ref[top:top + GROUP, span] = jnp.where(lane >= sub + offset, diag / scale, 0.0)
            else:
                factor_ref[top:top + GROUP, span] = rows[top, t] / scale


def trailing(a_ref, base, height, size):
    end = base + height
    if end == size:
        return
    panel = a_ref[base:end, :]
    col = lax.broadcasted_iota(jnp.int32, (height, size), 1)
    row = lax.broadcasted_iota(jnp.int32, (height, size), 0) + base
    right = jnp.where((col <= row) | (col >= end), panel, 0.0)
    left = panel[:, end:]
    update = lax.dot_general(left, right, (((0,), (0,)), ((), ())), precision=lax.Precision.HIGHEST, preferred_element_type=jnp.float32)
    rest = a_ref[end:, :]
    at = lax.broadcasted_iota(jnp.int32, (size - end, size), 1)
    a_ref[end:, :] = jnp.where((at >= base) & (at < end), 0.0, rest) - update


def split(value):
    high = value.astype(jnp.bfloat16)
    return high, (value - high.astype(jnp.float32)).astype(jnp.bfloat16)


def product(left, right, left_dim, right_dim):
    dims = (((left_dim,), (right_dim,)), ((), ()))
    dot = lambda a, b: lax.dot_general(a, b, dims, preferred_element_type=jnp.float32)
    return dot(left[0], right[0]) + (dot(left[0], right[1]) + dot(left[1], right[0]))


def core_bit():
    return lax.rem(lax.axis_index("wide"), 2)


def own_block():
    wide, narrow = lax.axis_index("wide"), lax.axis_index("narrow")
    plane = lax.rem(narrow, 2) + 2 * lax.rem(wide // 2, 2)
    return 16 * lax.rem(wide, 2) + 4 * plane + lax.rem(wide // 4, 4)


def rows_of(block, height):
    return pl.ds(pl.multiple_of(block * height, GROUP), height)


def local_kernel(features_hbm, sketch_hbm, sampled_ref, keep_ref, send_ref, gram_keep_ref, gram_send_ref, features_ref, sketch_ref, high_ref, low_ref, flip_high_ref, flip_low_ref, cross_ref, packed_ref, sems):
    rows, depth = features_ref.shape
    rank = sketch_ref.shape[1]
    chunks = rows // BLOCK
    copies = [pltpu.make_async_copy(sketch_hbm, sketch_ref, sems.at[chunks])]
    for at in range(chunks):
        span = pl.ds(at * BLOCK, BLOCK)
        copies.append(pltpu.make_async_copy(features_hbm.at[span, :], features_ref.at[span, :], sems.at[at]))
    for copy in copies:
        copy.start()
    copies[0].wait()
    sketch = split(sketch_ref[...])
    gram = None
    for at in range(chunks):
        span = slice(at * BLOCK, (at + 1) * BLOCK)
        copies[1 + at].wait()
        features = split(features_ref[span, :])
        high_ref[span, :], low_ref[span, :] = features
        sampled = product(features, sketch, 1, 0)
        sampled_ref[span, :] = sampled
        flipped = split(sampled.T)
        flip_high_ref[:, span], flip_low_ref[:, span] = flipped
        term = product(flipped, split(sampled), 1, 0)
        gram = term if gram is None else gram + term
    packed_ref[:LANES, :] = gram[:LANES, :LANES]
    packed_ref[LANES:2 * LANES, :] = gram[:LANES, LANES:]
    packed_ref[2 * LANES:, :] = gram[LANES:, LANES:]
    half = packed_ref.shape[0] // 2
    core = core_bit()
    gram_keep_ref[...] = packed_ref[rows_of(core, half), :]
    gram_send_ref[...] = packed_ref[rows_of(1 - core, half), :]
    flipped = flip_high_ref[...], flip_low_ref[...]
    own = own_block()
    height = rank // BLOCKS
    for left in range(0, depth, BLOCK):
        span = slice(left, left + BLOCK)
        cross_ref[:, span] = product(flipped, (high_ref[:, span], low_ref[:, span]), 1, 0)
    for at in range(BLOCKS):
        block = cross_ref[rows_of(at ^ own, height), :]
        if at < BLOCKS // 2:
            keep_ref[at * height:(at + 1) * height, :] = block
        else:
            rest = at - BLOCKS // 2
            send_ref[rest * height:(rest + 1) * height, :] = block


def f32(*shape):
    return jax.ShapeDtypeStruct(shape, jnp.float32)


def local_terms(features, sketch):
    rows, depth = features.shape
    rank = sketch.shape[1]
    packed = 3 * LANES
    hbm = pl.BlockSpec(memory_space=pltpu.HBM)
    return pl.pallas_call(
        local_kernel,
        out_shape=(f32(rows, rank), f32(rank // 2, depth), f32(rank // 2, depth), f32(packed // 2, LANES), f32(packed // 2, LANES)),
        in_specs=[hbm, hbm],
        out_specs=(VMEM,) * 5,
        scratch_shapes=[
            pltpu.VMEM((rows, depth), jnp.float32), pltpu.VMEM((depth, rank), jnp.float32),
            pltpu.VMEM((rows, depth), jnp.bfloat16), pltpu.VMEM((rows, depth), jnp.bfloat16),
            pltpu.VMEM((rank, rows), jnp.bfloat16), pltpu.VMEM((rank, rows), jnp.bfloat16),
            pltpu.VMEM((rank, depth), jnp.float32), pltpu.VMEM((packed, LANES), jnp.float32),
            pltpu.SemaphoreType.DMA((rows // BLOCK + 1,)),
        ],
        compiler_params=pltpu.CompilerParams(vmem_limit_bytes=51 * 2**20),
        cost_estimate=pl.CostEstimate(flops=4 * 10**9, bytes_accessed=8 * 2**20, transcendentals=0),
        name="local_terms",
    )(features, sketch)


def stage_kernel(terms, *refs):
    cross, (gram_ref, gram_other_ref, gram_out_ref), outs = refs[:terms], refs[terms:terms + 3], refs[terms + 3:]
    gram_out_ref[...] = gram_ref[...] + gram_other_ref[...]
    height = outs[0].shape[0]
    for at, out_ref in enumerate(outs):
        span = slice(at * height, (at + 1) * height)
        out_ref[...] = sum(ref[span, :] for ref in cross)


def join_kernel(*refs):
    *cross, gram_ref, gram_other_ref, gram_out_ref, out_ref = refs
    gram_out_ref[...] = gram_ref[...] + gram_other_ref[...]
    top = 0
    for ref in cross:
        out_ref[top:top + ref.shape[0], :] = ref[...]
        top += ref.shape[0]


def stage(cross, gram, gram_other, pieces, join=False):
    height, depth = cross[0].shape
    outs = [f32(len(cross) * height, depth)] if join else [f32(height // pieces, depth)] * pieces
    kernel = join_kernel if join else lambda *refs: stage_kernel(len(cross), *refs)
    gram, *outs = pl.pallas_call(
        kernel,
        out_shape=(f32(*gram.shape), *outs),
        in_specs=[VMEM] * (len(cross) + 2),
        out_specs=(VMEM,) * (1 + len(outs)),
        compiler_params=pltpu.CompilerParams(vmem_limit_bytes=16 * 2**20),
        cost_estimate=pl.CostEstimate(flops=10**6, bytes_accessed=10**6, transcendentals=0),
        name="join" if join else "stage",
    )(*cross, gram, gram_other)
    return gram, outs


def factor_kernel(scale, first, last, *refs):
    if first == 0:
        keep_ref, other_ref, a_ref, factor_ref, packed_ref = refs
        half = keep_ref.shape[0]
        core = core_bit()
        packed_ref[rows_of(core, half), :] = keep_ref[...]
        packed_ref[rows_of(1 - core, half), :] = other_ref[...]
        a_ref[:LANES, :LANES] = packed_ref[:LANES, :]
        a_ref[:LANES, LANES:] = packed_ref[LANES:2 * LANES, :]
        a_ref[LANES:, :LANES] = jnp.zeros((LANES, LANES), jnp.float32)
        a_ref[LANES:, LANES:] = packed_ref[2 * LANES:, :]
    else:
        from_ref, upper_ref, a_ref, factor_ref, *flipped_ref = refs
        a_ref[...] = from_ref[...]
        factor_ref[:first, :] = upper_ref[:first, :]
    size = a_ref.shape[0]
    for base in range(first, last, PANEL):
        factor_panel(a_ref, factor_ref, scale, base, PANEL, size)
        trailing(a_ref, base, PANEL, size)
    if last == size:
        col = lax.broadcasted_iota(jnp.int32, (size, size), 1)
        row = lax.broadcasted_iota(jnp.int32, (size, size), 0)
        inverse = jnp.where(col <= row, a_ref[...], 0.0)
        a_ref[...] = inverse
        flipped_ref[0][...] = inverse.T * scale


def factor_part(operands, size, scale, first, last):
    square = jax.ShapeDtypeStruct((size, size), jnp.float32)
    outs = 3 if last == size else 2
    return pl.pallas_call(
        lambda *refs: factor_kernel(scale, first, last, *refs),
        out_shape=(square,) * outs,
        in_specs=[VMEM] * 2,
        out_specs=(VMEM,) * outs,
        scratch_shapes=[pltpu.VMEM((3 * LANES, LANES), jnp.float32)] if first == 0 else [],
        compiler_params=pltpu.CompilerParams(vmem_limit_bytes=16 * 2**20),
        cost_estimate=pl.CostEstimate(flops=12 * 10**9 * (last - first) // size, bytes_accessed=2**20, transcendentals=last - first),
        name="factor_part",
    )(*operands)


def basis_kernel(sampled_ref, flipped_ref, basis_ref):
    flipped = split(flipped_ref[...])
    for top in range(0, sampled_ref.shape[0], BLOCK):
        span = slice(top, top + BLOCK)
        basis_ref[span, :] = product(split(sampled_ref[span, :]), flipped, 1, 0)


def basis_of(sampled, flipped):
    return pl.pallas_call(
        basis_kernel,
        out_shape=f32(*sampled.shape),
        in_specs=[VMEM] * 2,
        out_specs=VMEM,
        compiler_params=pltpu.CompilerParams(vmem_limit_bytes=16 * 2**20),
        cost_estimate=pl.CostEstimate(flops=2 * 10**9, bytes_accessed=2 * 2**20, transcendentals=0),
        name="basis",
    )(sampled, flipped)


def project_kernel(inverse_ref, *refs):
    *pieces, projection_ref, cross_ref = refs
    own = own_block()
    height = cross_ref.shape[0] // BLOCKS
    at = 0
    for piece in pieces:
        for top in range(0, piece.shape[0], height):
            cross_ref[rows_of(at ^ own, height), :] = piece[top:top + height, :]
            at += 1
    inverse = split(inverse_ref[...])
    for left in range(0, cross_ref.shape[1], BLOCK):
        span = slice(left, left + BLOCK)
        projection_ref[:, span] = product(inverse, split(cross_ref[:, span]), 1, 0)


def project(inverse, pieces):
    rank = inverse.shape[0]
    depth = pieces[0].shape[1]
    return pl.pallas_call(
        project_kernel,
        out_shape=jax.ShapeDtypeStruct((rank, depth), jnp.float32),
        in_specs=[VMEM] * (1 + len(pieces)),
        out_specs=VMEM,
        scratch_shapes=[pltpu.VMEM((rank, depth), jnp.float32)],
        compiler_params=pltpu.CompilerParams(vmem_limit_bytes=16 * 2**20),
        cost_estimate=pl.CostEstimate(flops=4 * 10**8, bytes_accessed=2 * 2**20, transcendentals=0),
        name="project",
    )(inverse, *pieces)


def send(value, wide, narrow):
    mask = wide * lax.axis_size("narrow") + narrow
    pairs = [(source, source ^ mask) for source in range(lax.axis_size(AXES))]
    return lax.ppermute(value, AXES, pairs)


CORE = (1, 0)
PLANE = [(0, 1), (2, 0), (2, 1)]
LINE = [(4, 0), (8, 0), (12, 0)]


def spare_bits():
    wide = [(2**bit, 0) for bit in range(4, lax.axis_size("wide").bit_length() - 1)]
    narrow = [(0, 2**bit) for bit in range(1, lax.axis_size("narrow").bit_length() - 1)]
    return wide + narrow


def spread(parts, masks):
    first, *rest = parts
    return [first] + [send(part, *mask) for part, mask in zip(rest, masks)]


def sums_and_factors(keep, other, gram_keep, gram_other, factors):
    cross = [keep, send(other, *CORE)]
    gram, parts = stage(cross, gram_keep, send(gram_other, *CORE), 4)
    cross = spread(parts, PLANE)
    gram = gram + send(gram, *LINE[0])
    gram, parts = stage(cross, gram, send(gram, *LINE[1]), 4)
    cross = spread(parts, LINE)
    gram, (own,) = stage(cross, gram, send(gram, *PLANE[0]), 1)
    for mask in spare_bits():
        own = own + send(own, *mask)
        gram = gram + send(gram, *mask)
    line = [own] + [send(own, *mask) for mask in LINE]
    gram, (line,) = stage(line, gram, send(gram, *PLANE[1]), 1, join=True)
    plane = [line] + [send(line, *mask) for mask in PLANE]
    factors = factors((gram, send(gram, *CORE)))
    return plane + [send(part, *CORE) for part in plane], factors


def per_device(features, sketch):
    scale = (features.shape[0] * lax.axis_size(AXES)) ** 0.5
    size = sketch.shape[1]

    def factors(state):
        for first in range(0, size, PANEL):
            state = factor_part(state[:2], size, scale, first, first + PANEL)
        return state

    sampled, *terms = local_terms(features, sketch)
    cross, (inverse, factor, flipped) = sums_and_factors(*terms, factors)
    return (basis_of(sampled, flipped), factor, project(inverse, cross))


def solution(mesh):
    rows = P(AXES, None)
    return jax.shard_map(
        per_device, mesh=mesh, in_specs=(rows, P()), out_specs=(rows, P(), P()), check_vma=False
    )
```

```python
import jax, jax.numpy as jnp
from jax import lax
from jax.experimental import pallas as pl
from jax.experimental.pallas import tpu as pltpu
from jax.sharding import PartitionSpec as P

GROUP = 8
LANES = 128
PANEL = 64
BLOCK = 256
BLOCKS = 32
AXES = ("wide", "narrow")
VMEM = pl.BlockSpec(memory_space=pltpu.VMEM)


def factor_panel(a_ref, factor_ref, scale, base, height, size):
    lane = lax.broadcasted_iota(jnp.int32, (GROUP, LANES), 1)
    sub = lax.broadcasted_iota(jnp.int32, (GROUP, LANES), 0)
    tiles = size // LANES
    for top in range(base, base + height, GROUP):
        groups = list(range(top, base + height, GROUP))
        home = top // LANES
        offset = top - home * LANES
        inside = (lane >= offset) & (lane < offset + GROUP)
        rows = {}
        for g in groups:
            for t in range(tiles):
                rows[g, t] = a_ref[g:g + GROUP, t * LANES:(t + 1) * LANES]
        diag = rows[top, home]
        col = {}
        for g in groups:
            for j in range(GROUP):
                at = rows[g, home][:, offset + j:offset + j + 1]
                col[g, j] = jnp.broadcast_to(at, (GROUP, LANES))
        one = {}
        for j in range(GROUP):
            for k in range(j, GROUP):
                one[k, j] = jnp.broadcast_to(col[top, j][k:k + 1, :], (GROUP, LANES))
        for g in groups:
            fresh = jnp.where(lane == sub + offset, 1.0, 0.0) if g == top else 0.0
            rows[g, home] = jnp.where(inside, fresh, rows[g, home])
        for j in range(GROUP):
            inv = lax.rsqrt(one[j, j])
            low = {k: one[k, j] * inv for k in range(j + 1, GROUP)}
            for k in range(j + 1, GROUP):
                for m in range(k, GROUP):
                    one[m, k] = one[m, k] - low[m] * low[k]
            scaled = {g: col[g, j] * inv for g in groups}
            for k in range(j + 1, GROUP):
                for g in groups:
                    col[g, k] = col[g, k] - scaled[g] * low[k]
            pivot = {t: jnp.broadcast_to(rows[top, t][j:j + 1, :], (GROUP, LANES)) * inv for t in range(tiles)}
            pivot_diag = jnp.broadcast_to(diag[j:j + 1, :], (GROUP, LANES)) * inv
            below = jnp.where(sub > j, scaled[top], 0.0)
            diag = jnp.where(sub == j, pivot_diag, diag - below * pivot_diag)
            for t in range(tiles):
                rows[top, t] = jnp.where(sub == j, pivot[t], rows[top, t] - below * pivot[t])
                for g in groups[1:]:
                    rows[g, t] = rows[g, t] - scaled[g] * pivot[t]
        for g in groups:
            for t in range(tiles):
                a_ref[g:g + GROUP, t * LANES:(t + 1) * LANES] = rows[g, t]
        for t in range(tiles):
            span = slice(t * LANES, (t + 1) * LANES)
            if t < home:
                factor_ref[top:top + GROUP, span] = jnp.zeros((GROUP, LANES), jnp.float32)
            elif t == home:
                factor_ref[top:top + GROUP, span] = jnp.where(lane >= sub + offset, diag / scale, 0.0)
            else:
                factor_ref[top:top + GROUP, span] = rows[top, t] / scale


def trailing(a_ref, base, height, size):
    end = base + height
    if end == size:
        return
    panel = a_ref[base:end, :]
    col = lax.broadcasted_iota(jnp.int32, (height, size), 1)
    row = lax.broadcasted_iota(jnp.int32, (height, size), 0) + base
    right = jnp.where((col <= row) | (col >= end), panel, 0.0)
    left = panel[:, end:]
    update = lax.dot_general(left, right, (((0,), (0,)), ((), ())), precision=lax.Precision.HIGHEST, preferred_element_type=jnp.float32)
    rest = a_ref[end:, :]
    at = lax.broadcasted_iota(jnp.int32, (size - end, size), 1)
    a_ref[end:, :] = jnp.where((at >= base) & (at < end), 0.0, rest) - update


def split(value):
    high = value.astype(jnp.bfloat16)
    return high, (value - high.astype(jnp.float32)).astype(jnp.bfloat16)


def product(left, right, left_dim, right_dim):
    dims = (((left_dim,), (right_dim,)), ((), ()))
    dot = lambda a, b: lax.dot_general(a, b, dims, preferred_element_type=jnp.float32)
    return dot(left[0], right[0]) + (dot(left[0], right[1]) + dot(left[1], right[0]))


def core_bit():
    return lax.rem(lax.axis_index("wide"), 2)


def own_block():
    wide, narrow = lax.axis_index("wide"), lax.axis_index("narrow")
    plane = lax.rem(narrow, 2) + 2 * lax.rem(wide // 2, 2)
    return 16 * lax.rem(wide, 2) + 4 * plane + lax.rem(wide // 4, 4)


def rows_of(block, height):
    return pl.ds(pl.multiple_of(block * height, GROUP), height)


def stacked_product(left_ref, left_span, rank, high, low):
    both = lax.dot(left_ref[:, left_span], high, preferred_element_type=jnp.float32)
    return both[:rank, :] + (both[rank:, :] + lax.dot(left_ref[:rank, left_span], low, preferred_element_type=jnp.float32))


def local_kernel(features_hbm, sketch_hbm, sampled_ref, keep_ref, send_ref, gram_keep_ref, gram_send_ref, features_ref, sketch_ref, pair_ref, high_ref, low_ref, flip_ref, cross_ref, packed_ref, sems):
    rows, depth = features_ref.shape
    rank = sketch_ref.shape[1]
    chunks = rows // BLOCK
    copies = [pltpu.make_async_copy(sketch_hbm, sketch_ref, sems.at[chunks])]
    for at in range(chunks):
        span = pl.ds(at * BLOCK, BLOCK)
        copies.append(pltpu.make_async_copy(features_hbm.at[span, :], features_ref.at[span, :], sems.at[at]))
    for copy in copies:
        copy.start()
    copies[0].wait()
    pair_ref[:, :rank], pair_ref[:, rank:] = split(sketch_ref[...])
    gram = None
    for at in range(chunks):
        span = slice(at * BLOCK, (at + 1) * BLOCK)
        copies[1 + at].wait()
        high, low = split(features_ref[span, :])
        high_ref[span, :], low_ref[span, :] = high, low
        both = lax.dot(high, pair_ref[...], preferred_element_type=jnp.float32)
        sampled = both[:, :rank] + (both[:, rank:] + lax.dot(low, pair_ref[:, :rank], preferred_element_type=jnp.float32))
        sampled_ref[span, :] = sampled
        flip_ref[:rank, span], flip_ref[rank:, span] = split(sampled.T)
        term = stacked_product(flip_ref, span, rank, *split(sampled))
        gram = term if gram is None else gram + term
    packed_ref[:LANES, :] = gram[:LANES, :LANES]
    packed_ref[LANES:2 * LANES, :] = gram[:LANES, LANES:]
    packed_ref[2 * LANES:, :] = gram[LANES:, LANES:]
    half = packed_ref.shape[0] // 2
    core = core_bit()
    gram_keep_ref[...] = packed_ref[rows_of(core, half), :]
    gram_send_ref[...] = packed_ref[rows_of(1 - core, half), :]
    own = own_block()
    height = rank // BLOCKS
    for left in range(0, depth, 2 * BLOCK):
        span = slice(left, left + 2 * BLOCK)
        cross_ref[:, span] = stacked_product(flip_ref, slice(None), rank, high_ref[:, span], low_ref[:, span])
    for at in range(BLOCKS):
        block = cross_ref[rows_of(at ^ own, height), :]
        if at < BLOCKS // 2:
            keep_ref[at * height:(at + 1) * height, :] = block
        else:
            rest = at - BLOCKS // 2
            send_ref[rest * height:(rest + 1) * height, :] = block


def f32(*shape):
    return jax.ShapeDtypeStruct(shape, jnp.float32)


def local_terms(features, sketch):
    rows, depth = features.shape
    rank = sketch.shape[1]
    packed = 3 * LANES
    hbm = pl.BlockSpec(memory_space=pltpu.HBM)
    return pl.pallas_call(
        local_kernel,
        out_shape=(f32(rows, rank), f32(rank // 2, depth), f32(rank // 2, depth), f32(packed // 2, LANES), f32(packed // 2, LANES)),
        in_specs=[hbm, hbm],
        out_specs=(VMEM,) * 5,
        scratch_shapes=[
            pltpu.VMEM((rows, depth), jnp.float32), pltpu.VMEM((depth, rank), jnp.float32),
            pltpu.VMEM((depth, 2 * rank), jnp.bfloat16),
            pltpu.VMEM((rows, depth), jnp.bfloat16), pltpu.VMEM((rows, depth), jnp.bfloat16),
            pltpu.VMEM((2 * rank, rows), jnp.bfloat16),
            pltpu.VMEM((rank, depth), jnp.float32), pltpu.VMEM((packed, LANES), jnp.float32),
            pltpu.SemaphoreType.DMA((rows // BLOCK + 1,)),
        ],
        compiler_params=pltpu.CompilerParams(vmem_limit_bytes=51 * 2**20),
        cost_estimate=pl.CostEstimate(flops=4 * 10**9, bytes_accessed=8 * 2**20, transcendentals=0),
        name="local_terms",
    )(features, sketch)


def stage_kernel(terms, *refs):
    cross, (gram_ref, gram_other_ref, gram_out_ref), outs = refs[:terms], refs[terms:terms + 3], refs[terms + 3:]
    gram_out_ref[...] = gram_ref[...] + gram_other_ref[...]
    height = outs[0].shape[0]
    for at, out_ref in enumerate(outs):
        span = slice(at * height, (at + 1) * height)
        out_ref[...] = sum(ref[span, :] for ref in cross)


def join_kernel(*refs):
    *cross, _, out_ref = refs
    top = 0
    for ref in cross:
        out_ref[top:top + ref.shape[0], :] = ref[...]
        top += ref.shape[0]


def stage(cross, gram, gram_other, pieces):
    height, depth = cross[0].shape
    gram, *outs = pl.pallas_call(
        lambda *refs: stage_kernel(len(cross), *refs),
        out_shape=(f32(*gram.shape), *[f32(height // pieces, depth)] * pieces),
        in_specs=[VMEM] * (len(cross) + 2),
        out_specs=(VMEM,) * (1 + pieces),
        compiler_params=pltpu.CompilerParams(vmem_limit_bytes=16 * 2**20),
        cost_estimate=pl.CostEstimate(flops=10**6, bytes_accessed=10**6, transcendentals=0),
        name="stage",
    )(*cross, gram, gram_other)
    return gram, outs


def add_after(gram, other, after):
    def kernel(gram_ref, other_ref, _, out_ref):
        out_ref[...] = gram_ref[...] + other_ref[...]

    return pl.pallas_call(
        kernel,
        out_shape=f32(*gram.shape),
        in_specs=[VMEM, VMEM, pl.BlockSpec(memory_space=pl.ANY)],
        out_specs=VMEM,
        compiler_params=pltpu.CompilerParams(vmem_limit_bytes=16 * 2**20),
        cost_estimate=pl.CostEstimate(flops=10**6, bytes_accessed=10**6, transcendentals=0),
        name="add_after",
    )(gram, other, after)


def join(cross, after):
    height, depth = cross[0].shape
    return pl.pallas_call(
        join_kernel,
        out_shape=f32(len(cross) * height, depth),
        in_specs=[VMEM] * len(cross) + [pl.BlockSpec(memory_space=pl.ANY)],
        out_specs=VMEM,
        compiler_params=pltpu.CompilerParams(vmem_limit_bytes=16 * 2**20),
        cost_estimate=pl.CostEstimate(flops=10**6, bytes_accessed=10**6, transcendentals=0),
        name="join",
    )(*cross, after)


def factor_kernel(scale, first, last, after, *refs):
    refs = refs[:2] + refs[2 + after:]
    if first == 0:
        keep_ref, other_ref, a_ref, factor_ref, packed_ref = refs
        half = keep_ref.shape[0]
        core = core_bit()
        packed_ref[rows_of(core, half), :] = keep_ref[...]
        packed_ref[rows_of(1 - core, half), :] = other_ref[...]
        a_ref[:LANES, :LANES] = packed_ref[:LANES, :]
        a_ref[:LANES, LANES:] = packed_ref[LANES:2 * LANES, :]
        a_ref[LANES:, :LANES] = jnp.zeros((LANES, LANES), jnp.float32)
        a_ref[LANES:, LANES:] = packed_ref[2 * LANES:, :]
    else:
        from_ref, upper_ref, a_ref, factor_ref, *flipped_ref = refs
        a_ref[...] = from_ref[...]
        factor_ref[:first, :] = upper_ref[:first, :]
    size = a_ref.shape[0]
    for base in range(first, last, PANEL):
        factor_panel(a_ref, factor_ref, scale, base, PANEL, size)
        trailing(a_ref, base, PANEL, size)
    if last == size:
        col = lax.broadcasted_iota(jnp.int32, (size, size), 1)
        row = lax.broadcasted_iota(jnp.int32, (size, size), 0)
        inverse = jnp.where(col <= row, a_ref[...], 0.0)
        a_ref[...] = inverse
        flipped_ref[0][...] = inverse.T * scale


def factor_part(operands, size, scale, first, last, after=()):
    square = jax.ShapeDtypeStruct((size, size), jnp.float32)
    outs = 3 if last == size else 2
    return pl.pallas_call(
        lambda *refs: factor_kernel(scale, first, last, len(after), *refs),
        out_shape=(square,) * outs,
        in_specs=[VMEM] * 2 + [pl.BlockSpec(memory_space=pl.ANY)] * len(after),
        out_specs=(VMEM,) * outs,
        scratch_shapes=[pltpu.VMEM((3 * LANES, LANES), jnp.float32)] if first == 0 else [],
        compiler_params=pltpu.CompilerParams(vmem_limit_bytes=16 * 2**20),
        cost_estimate=pl.CostEstimate(flops=12 * 10**9 * (last - first) // size, bytes_accessed=2**20, transcendentals=last - first),
        name="factor_part",
    )(*operands, *after)


def basis_kernel(sampled_ref, flipped_ref, basis_ref):
    flipped = split(flipped_ref[...])
    for top in range(0, sampled_ref.shape[0], BLOCK):
        span = slice(top, top + BLOCK)
        basis_ref[span, :] = product(split(sampled_ref[span, :]), flipped, 1, 0)


def basis_of(sampled, flipped):
    return pl.pallas_call(
        basis_kernel,
        out_shape=f32(*sampled.shape),
        in_specs=[VMEM] * 2,
        out_specs=VMEM,
        compiler_params=pltpu.CompilerParams(vmem_limit_bytes=16 * 2**20),
        cost_estimate=pl.CostEstimate(flops=2 * 10**9, bytes_accessed=2 * 2**20, transcendentals=0),
        name="basis",
    )(sampled, flipped)


def project_kernel(inverse_ref, *refs):
    *pieces, projection_ref, cross_ref = refs
    own = own_block()
    height = cross_ref.shape[0] // BLOCKS
    at = 0
    for piece in pieces:
        for top in range(0, piece.shape[0], height):
            cross_ref[rows_of(at ^ own, height), :] = piece[top:top + height, :]
            at += 1
    inverse = split(inverse_ref[...])
    for left in range(0, cross_ref.shape[1], BLOCK):
        span = slice(left, left + BLOCK)
        projection_ref[:, span] = product(inverse, split(cross_ref[:, span]), 1, 0)


def project(inverse, pieces):
    rank = inverse.shape[0]
    depth = pieces[0].shape[1]
    return pl.pallas_call(
        project_kernel,
        out_shape=jax.ShapeDtypeStruct((rank, depth), jnp.float32),
        in_specs=[VMEM] * (1 + len(pieces)),
        out_specs=VMEM,
        scratch_shapes=[pltpu.VMEM((rank, depth), jnp.float32)],
        compiler_params=pltpu.CompilerParams(vmem_limit_bytes=16 * 2**20),
        cost_estimate=pl.CostEstimate(flops=4 * 10**8, bytes_accessed=2 * 2**20, transcendentals=0),
        name="project",
    )(inverse, *pieces)


def send(value, wide, narrow):
    mask = wide * lax.axis_size("narrow") + narrow
    pairs = [(source, source ^ mask) for source in range(lax.axis_size(AXES))]
    return lax.ppermute(value, AXES, pairs)


CORE = (1, 0)
PLANE = [(0, 1), (2, 0), (2, 1)]
LINE = [(4, 0), (8, 0), (12, 0)]


def spare_bits():
    wide = [(2**bit, 0) for bit in range(4, lax.axis_size("wide").bit_length() - 1)]
    narrow = [(0, 2**bit) for bit in range(1, lax.axis_size("narrow").bit_length() - 1)]
    return wide + narrow


def spread(parts, masks):
    first, *rest = parts
    return [first] + [send(part, *mask) for part, mask in zip(rest, masks)]


def per_device(features, sketch):
    scale = (features.shape[0] * lax.axis_size(AXES)) ** 0.5
    size = sketch.shape[1]
    sampled, keep, other, gram, gram_other = local_terms(features, sketch)
    cross = [keep, send(other, *CORE)]
    gram, parts = stage(cross, gram, send(gram_other, *CORE), 4)
    cross = spread(parts, PLANE)
    gram = gram + send(gram, *LINE[0])
    gram, parts = stage(cross, gram, send(gram, *LINE[1]), 4)
    cross = spread(parts, LINE)
    gram, (own,) = stage(cross, gram, send(gram, *PLANE[0]), 1)
    for mask in spare_bits():
        own = own + send(own, *mask)
        gram = gram + send(gram, *mask)
    line = [own] + [send(own, *mask) for mask in LINE]
    gram = add_after(gram, send(gram, *PLANE[1]), line[1])
    state = factor_part((gram, send(gram, *CORE)), size, scale, 0, PANEL)
    line = join(line, state[0])
    plane = [line] + [send(line, *mask) for mask in PLANE]
    after = (line,)
    for first in range(PANEL, size, PANEL):
        state = factor_part(state[:2], size, scale, first, first + PANEL, after)
        after = ()
    inverse, factor, flipped = state
    cross = plane + [send(part, *CORE) for part in plane]
    return (basis_of(sampled, flipped), factor, project(inverse, cross))


def solution(mesh):
    rows = P(AXES, None)
    return jax.shard_map(
        per_device, mesh=mesh, in_specs=(rows, P()), out_specs=(rows, P(), P()), check_vma=False
    )
```

```python
import jax, jax.numpy as jnp
from jax import lax
from jax.experimental import pallas as pl
from jax.experimental.pallas import tpu as pltpu
from jax.sharding import PartitionSpec as P

GROUP = 8
LANES = 128
PANEL = 64
BLOCK = 256
BLOCKS = 32
AXES = ("wide", "narrow")
VMEM = pl.BlockSpec(memory_space=pltpu.VMEM)


def factor_panel(a_ref, factor_ref, scale, base, height, size):
    lane = lax.broadcasted_iota(jnp.int32, (GROUP, LANES), 1)
    sub = lax.broadcasted_iota(jnp.int32, (GROUP, LANES), 0)
    tiles = size // LANES
    for top in range(base, base + height, GROUP):
        groups = list(range(top, base + height, GROUP))
        home = top // LANES
        offset = top - home * LANES
        inside = (lane >= offset) & (lane < offset + GROUP)
        rows = {}
        for g in groups:
            for t in range(tiles):
                rows[g, t] = a_ref[g:g + GROUP, t * LANES:(t + 1) * LANES]
        diag = rows[top, home]
        col = {}
        for g in groups:
            for j in range(GROUP):
                at = rows[g, home][:, offset + j:offset + j + 1]
                col[g, j] = jnp.broadcast_to(at, (GROUP, LANES))
        one = {}
        for j in range(GROUP):
            for k in range(j, GROUP):
                one[k, j] = jnp.broadcast_to(col[top, j][k:k + 1, :], (GROUP, LANES))
        for g in groups:
            fresh = jnp.where(lane == sub + offset, 1.0, 0.0) if g == top else 0.0
            rows[g, home] = jnp.where(inside, fresh, rows[g, home])
        for j in range(GROUP):
            inv = lax.rsqrt(one[j, j])
            low = {k: one[k, j] * inv for k in range(j + 1, GROUP)}
            for k in range(j + 1, GROUP):
                for m in range(k, GROUP):
                    one[m, k] = one[m, k] - low[m] * low[k]
            scaled = {g: col[g, j] * inv for g in groups}
            for k in range(j + 1, GROUP):
                for g in groups:
                    col[g, k] = col[g, k] - scaled[g] * low[k]
            pivot = {t: jnp.broadcast_to(rows[top, t][j:j + 1, :], (GROUP, LANES)) * inv for t in range(tiles)}
            pivot_diag = jnp.broadcast_to(diag[j:j + 1, :], (GROUP, LANES)) * inv
            below = jnp.where(sub > j, scaled[top], 0.0)
            diag = jnp.where(sub == j, pivot_diag, diag - below * pivot_diag)
            for t in range(tiles):
                rows[top, t] = jnp.where(sub == j, pivot[t], rows[top, t] - below * pivot[t])
                for g in groups[1:]:
                    rows[g, t] = rows[g, t] - scaled[g] * pivot[t]
        for g in groups:
            for t in range(tiles):
                a_ref[g:g + GROUP, t * LANES:(t + 1) * LANES] = rows[g, t]
        for t in range(tiles):
            span = slice(t * LANES, (t + 1) * LANES)
            if t < home:
                factor_ref[top:top + GROUP, span] = jnp.zeros((GROUP, LANES), jnp.float32)
            elif t == home:
                factor_ref[top:top + GROUP, span] = jnp.where(lane >= sub + offset, diag / scale, 0.0)
            else:
                factor_ref[top:top + GROUP, span] = rows[top, t] / scale


def trailing(a_ref, base, height, size):
    end = base + height
    if end == size:
        return
    panel = a_ref[base:end, :]
    col = lax.broadcasted_iota(jnp.int32, (height, size), 1)
    row = lax.broadcasted_iota(jnp.int32, (height, size), 0) + base
    right = jnp.where((col <= row) | (col >= end), panel, 0.0)
    left = panel[:, end:]
    update = lax.dot_general(left, right, (((0,), (0,)), ((), ())), precision=lax.Precision.HIGHEST, preferred_element_type=jnp.float32)
    rest = a_ref[end:, :]
    at = lax.broadcasted_iota(jnp.int32, (size - end, size), 1)
    a_ref[end:, :] = jnp.where((at >= base) & (at < end), 0.0, rest) - update


def split(value):
    high = value.astype(jnp.bfloat16)
    return high, (value - high.astype(jnp.float32)).astype(jnp.bfloat16)


def product(left, right, left_dim, right_dim):
    dims = (((left_dim,), (right_dim,)), ((), ()))
    dot = lambda a, b: lax.dot_general(a, b, dims, preferred_element_type=jnp.float32)
    return dot(left[0], right[0]) + (dot(left[0], right[1]) + dot(left[1], right[0]))


def own_block():
    wide, narrow = lax.axis_index("wide"), lax.axis_index("narrow")
    plane = lax.rem(narrow, 2) + 2 * lax.rem(wide // 2, 2)
    return 16 * lax.rem(wide, 2) + 4 * plane + lax.rem(wide // 4, 4)


def rows_of(block, height):
    return pl.ds(pl.multiple_of(block * height, GROUP), height)


def arrange_kernel(cross_ref, gram_ref, keep_ref, send_ref):
    own = own_block()
    depth = cross_ref.shape[1]
    height = cross_ref.shape[0] // BLOCKS
    for at in range(BLOCKS):
        rows = rows_of(at ^ own, height)
        out_ref = keep_ref if at < BLOCKS // 2 else send_ref
        top = at % (BLOCKS // 2) * height
        out_ref[top:top + height, :depth] = cross_ref[rows, :]
        out_ref[top:top + height, depth:] = gram_ref[rows, :]


def f32(*shape):
    return jax.ShapeDtypeStruct(shape, jnp.float32)


def call(kernel, name, outs, *operands, after=(), flops=10**6):
    return pl.pallas_call(
        lambda *refs: kernel(*refs[:len(operands)], *refs[len(operands) + len(after):]),
        out_shape=outs,
        in_specs=[VMEM] * len(operands) + [pl.BlockSpec(memory_space=pl.ANY)] * len(after),
        out_specs=jax.tree.map(lambda _: VMEM, outs),
        compiler_params=pltpu.CompilerParams(vmem_limit_bytes=16 * 2**20),
        cost_estimate=pl.CostEstimate(flops=flops, bytes_accessed=10**6, transcendentals=0),
        name=name,
    )(*operands, *after)


def core_sum_kernel(keep_ref, other_ref, *outs):
    height = outs[0].shape[0]
    for at, out_ref in enumerate(outs):
        span = slice(at * height, (at + 1) * height)
        out_ref[...] = keep_ref[span, :] + other_ref[span, :]


def plane_sum_kernel(depth, *refs):
    parts, outs = refs[:4], refs[4:]
    height = outs[0].shape[0]
    for at, out_ref in enumerate(outs):
        span = slice(at * height, (at + 1) * height)
        total = sum(part[span, :] for part in parts)
        out_ref[:, :depth] = total[:, :depth]
        rank = total.shape[1] - depth
        for to_ref in outs:
            left = depth + at * rank
            to_ref[:, left:left + rank] = total[:, depth:]


def line_sum_kernel(depth, *refs):
    parts, (own_ref, gram_ref) = refs[:4], refs[4:]
    own_ref[...] = sum(part[:, :depth] for part in parts)
    rank = gram_ref.shape[1]
    height = own_ref.shape[0]
    for at in range(4):
        pieces = [part[:, depth + (at ^ sender) * rank:depth + (at ^ sender) * rank + rank] for sender, part in enumerate(parts)]
        gram_ref[at * height:(at + 1) * height, :] = sum(pieces)


def join_kernel(*refs):
    *parts, out_ref, gram_ref = refs
    for to_ref, pieces in ((out_ref, parts[:4]), (gram_ref, parts[4:])):
        top = 0
        for piece in pieces:
            to_ref[top:top + piece.shape[0], :] = piece[...]
            top += piece.shape[0]


def factor_kernel(scale, first, last, after, *refs):
    refs = refs[:2] + refs[2 + after:]
    if first == 0:
        *halves, a_ref, factor_ref = refs
        own = own_block()
        height = a_ref.shape[0] // BLOCKS
        for at in range(BLOCKS):
            half_ref = halves[at // (BLOCKS // 2)]
            top = at % (BLOCKS // 2) * height
            a_ref[rows_of(at ^ own, height), :] = half_ref[top:top + height, :]
    else:
        from_ref, upper_ref, a_ref, factor_ref, *flipped_ref = refs
        a_ref[...] = from_ref[...]
        factor_ref[:first, :] = upper_ref[:first, :]
    size = a_ref.shape[0]
    for base in range(first, last, PANEL):
        factor_panel(a_ref, factor_ref, scale, base, PANEL, size)
        trailing(a_ref, base, PANEL, size)
    if last == size:
        col = lax.broadcasted_iota(jnp.int32, (size, size), 1)
        row = lax.broadcasted_iota(jnp.int32, (size, size), 0)
        inverse = jnp.where(col <= row, a_ref[...], 0.0)
        a_ref[...] = inverse
        flipped_ref[0][...] = inverse.T * scale


def factor_part(operands, size, scale, first, last, after=()):
    square = jax.ShapeDtypeStruct((size, size), jnp.float32)
    outs = 3 if last == size else 2
    return pl.pallas_call(
        lambda *refs: factor_kernel(scale, first, last, len(after), *refs),
        out_shape=(square,) * outs,
        in_specs=[VMEM] * 2 + [pl.BlockSpec(memory_space=pl.ANY)] * len(after),
        out_specs=(VMEM,) * outs,
        compiler_params=pltpu.CompilerParams(vmem_limit_bytes=16 * 2**20),
        cost_estimate=pl.CostEstimate(flops=12 * 10**9 * (last - first) // size, bytes_accessed=2**20, transcendentals=last - first),
        name="factor_part",
    )(*operands, *after)


def basis_kernel(sampled_ref, flipped_ref, basis_ref):
    flipped = split(flipped_ref[...])
    for top in range(0, sampled_ref.shape[1], BLOCK):
        span = slice(top, top + BLOCK)
        basis_ref[span, :] = product(split(sampled_ref[:, span].T), flipped, 1, 0)


def basis_of(sampled, flipped):
    return pl.pallas_call(
        basis_kernel,
        out_shape=f32(*sampled.shape[::-1]),
        in_specs=[VMEM] * 2,
        out_specs=VMEM,
        compiler_params=pltpu.CompilerParams(vmem_limit_bytes=16 * 2**20),
        cost_estimate=pl.CostEstimate(flops=2 * 10**9, bytes_accessed=2 * 2**20, transcendentals=0),
        name="basis",
    )(sampled, flipped)


def project_kernel(inverse_ref, *refs):
    *pieces, projection_ref, cross_ref = refs
    own = own_block()
    height = cross_ref.shape[0] // BLOCKS
    at = 0
    for piece in pieces:
        for top in range(0, piece.shape[0], height):
            cross_ref[rows_of(at ^ own, height), :] = piece[top:top + height, :]
            at += 1
    inverse = split(inverse_ref[...])
    for left in range(0, cross_ref.shape[1], BLOCK):
        span = slice(left, left + BLOCK)
        projection_ref[:, span] = product(inverse, split(cross_ref[:, span]), 1, 0)


def project(inverse, pieces):
    rank = inverse.shape[0]
    depth = pieces[0].shape[1]
    return pl.pallas_call(
        project_kernel,
        out_shape=jax.ShapeDtypeStruct((rank, depth), jnp.float32),
        in_specs=[VMEM] * (1 + len(pieces)),
        out_specs=VMEM,
        scratch_shapes=[pltpu.VMEM((rank, depth), jnp.float32)],
        compiler_params=pltpu.CompilerParams(vmem_limit_bytes=16 * 2**20),
        cost_estimate=pl.CostEstimate(flops=4 * 10**8, bytes_accessed=2 * 2**20, transcendentals=0),
        name="project",
    )(inverse, *pieces)


def send(value, wide, narrow):
    mask = wide * lax.axis_size("narrow") + narrow
    pairs = [(source, source ^ mask) for source in range(lax.axis_size(AXES))]
    return lax.ppermute(value, AXES, pairs)


CORE = (1, 0)
PLANE = [(0, 1), (2, 0), (2, 1)]
LINE = [(4, 0), (8, 0), (12, 0)]


def spare_bits():
    wide = [(2**bit, 0) for bit in range(4, lax.axis_size("wide").bit_length() - 1)]
    narrow = [(0, 2**bit) for bit in range(1, lax.axis_size("narrow").bit_length() - 1)]
    return wide + narrow


def spread(parts, masks):
    first, *rest = parts
    return [first] + [send(part, *mask) for part, mask in zip(rest, masks)]


def per_device(features, sketch):
    scale = (features.shape[0] * lax.axis_size(AXES)) ** 0.5
    size = sketch.shape[1]
    depth = features.shape[1]
    dot = lambda a, b, dims: lax.dot_general(a, b, ((dims[:1], dims[1:]), ((), ())), precision=lax.Precision.HIGH, preferred_element_type=jnp.float32)
    sampled = dot(sketch, features, (0, 1))
    cross = dot(sampled, features, (1, 0))
    gram = dot(sampled, sampled, (1, 1))
    half = f32(size // 2, depth + size)
    keep, other = call(arrange_kernel, "arrange", (half, half), cross, gram)
    height = size // BLOCKS
    parts = call(core_sum_kernel, "core_sum", (f32(4 * height, depth + size),) * 4, keep, send(other, *CORE))
    parts = call(lambda *refs: plane_sum_kernel(depth, *refs), "plane_sum", (f32(height, depth + 4 * size),) * 4, *spread(parts, PLANE))
    own, gram = call(lambda *refs: line_sum_kernel(depth, *refs), "line_sum", (f32(height, depth), f32(4 * height, size)), *spread(parts, LINE))
    for mask in spare_bits():
        own = own + send(own, *mask)
        gram = gram + send(gram, *mask)
    line = [own] + [send(own, *mask) for mask in LINE]
    gram = [gram] + [send(gram, *mask) for mask in PLANE]
    line, gram = call(join_kernel, "join", (f32(4 * height, depth), f32(16 * height, size)), *line, *gram)
    plane = [line] + [send(line, *mask) for mask in PLANE]
    state = (gram, send(gram, *CORE))
    after = (line,)
    for first in range(0, size, PANEL):
        state = factor_part(state[:2], size, scale, first, first + PANEL, after)
        after = ()
    inverse, factor, flipped = state
    cross = plane + [send(part, *CORE) for part in plane]
    return (basis_of(sampled, flipped), factor, project(inverse, cross))


def solution(mesh):
    rows = P(AXES, None)
    return jax.shard_map(
        per_device, mesh=mesh, in_specs=(rows, P()), out_specs=(rows, P(), P()), check_vma=False
    )
```

```python
import jax, jax.numpy as jnp
from jax import lax
from jax.experimental import pallas as pl
from jax.experimental.pallas import tpu as pltpu
from jax.sharding import PartitionSpec as P

GROUP = 8
LANES = 128
PANEL = 64
BLOCK = 256
BLOCKS = 32
AXES = ("wide", "narrow")
VMEM = pl.BlockSpec(memory_space=pltpu.VMEM)


def factor_panel(a_ref, factor_ref, base, height, size):
    lane = lax.broadcasted_iota(jnp.int32, (GROUP, LANES), 1)
    sub = lax.broadcasted_iota(jnp.int32, (GROUP, LANES), 0)
    tiles = size // LANES
    spread = lambda value: jnp.broadcast_to(value, (GROUP, LANES))
    rows = {}
    for g in range(base, base + height, GROUP):
        for t in range(tiles):
            rows[g, t] = a_ref[g:g + GROUP, t * LANES:(t + 1) * LANES]
    for top in range(base, base + height, GROUP):
        groups = list(range(top, base + height, GROUP))
        home = top // LANES
        offset = top - home * LANES
        inside = (lane >= offset) & (lane < offset + GROUP)
        diag = rows[top, home]
        col, one = {}, {}
        for j in range(GROUP):
            for g in groups:
                col[g, j] = spread(rows[g, home][:, offset + j:offset + j + 1])
            for k in range(j, GROUP):
                one[k, j] = spread(col[top, j][k:k + 1, :])
        for g in groups:
            fresh = jnp.where(lane == sub + offset, 1.0, 0.0) if g == top else 0.0
            rows[g, home] = jnp.where(inside, fresh, rows[g, home])
        for j in range(0, GROUP, 2):
            a, b, c = one[j, j], one[j + 1, j], one[j + 1, j + 1]
            first = lax.rsqrt(a)
            both = first * lax.rsqrt(a * c - b * b)
            cross = b * first
            second = a * both
            low = {}
            for k in range(j + 2, GROUP):
                low[k] = one[k, j] * first, (a * one[k, j + 1] - b * one[k, j]) * both
            for k in range(j + 2, GROUP):
                for m in range(k, GROUP):
                    one[m, k] = one[m, k] - (low[m][0] * low[k][0] + low[m][1] * low[k][1])
            scaled = {}
            for g in groups:
                scaled[g] = col[g, j] * first, (a * col[g, j + 1] - b * col[g, j]) * both
            for k in range(j + 2, GROUP):
                for g in groups:
                    col[g, k] = col[g, k] - (scaled[g][0] * low[k][0] + scaled[g][1] * low[k][1])
            below = [jnp.where(sub > j + 1, part, 0.0) for part in scaled[top]]

            def pivots(value):
                upper = spread(value[j:j + 1, :]) * first
                return upper, (spread(value[j + 1:j + 2, :]) - cross * upper) * second

            def replaced(value, upper, lower):
                value = value - (below[0] * upper + below[1] * lower)
                return jnp.where(sub == j, upper, jnp.where(sub == j + 1, lower, value))

            diag = replaced(diag, *pivots(diag))
            for t in range(tiles):
                upper, lower = pivots(rows[top, t])
                rows[top, t] = replaced(rows[top, t], upper, lower)
                for g in groups[1:]:
                    rows[g, t] = rows[g, t] - (scaled[g][0] * upper + scaled[g][1] * lower)
        for t in range(tiles):
            span = slice(t * LANES, (t + 1) * LANES)
            a_ref[top:top + GROUP, span] = rows[top, t]
            if t < home:
                factor_ref[top:top + GROUP, span] = jnp.zeros((GROUP, LANES), jnp.float32)
            elif t == home:
                factor_ref[top:top + GROUP, span] = jnp.where(lane >= sub + offset, diag, 0.0)
            else:
                factor_ref[top:top + GROUP, span] = rows[top, t]


def trailing(a_ref, base, height, size):
    end = base + height
    if end == size:
        return
    panel = a_ref[base:end, :]
    col = lax.broadcasted_iota(jnp.int32, (height, size), 1)
    row = lax.broadcasted_iota(jnp.int32, (height, size), 0) + base
    right = jnp.where((col <= row) | (col >= end), panel, 0.0)
    left = panel[:, end:]
    update = lax.dot_general(left, right, (((0,), (0,)), ((), ())), precision=lax.Precision.HIGHEST, preferred_element_type=jnp.float32)
    rest = a_ref[end:, :]
    at = lax.broadcasted_iota(jnp.int32, (size - end, size), 1)
    a_ref[end:, :] = jnp.where((at >= base) & (at < end), 0.0, rest) - update


def factorize(a_ref, factor_ref):
    size = a_ref.shape[0]
    col = lax.broadcasted_iota(jnp.int32, (size, size), 1)
    row = lax.broadcasted_iota(jnp.int32, (size, size), 0)
    largest = jnp.max(jnp.where(col == row, a_ref[...], 0.0), axis=(0, 1), keepdims=True)
    shrink = lax.rsqrt(largest)
    a_ref[...] = a_ref[...] * shrink * shrink
    for base in range(0, size, PANEL):
        factor_panel(a_ref, factor_ref, base, PANEL, size)
        trailing(a_ref, base, PANEL, size)
    return jnp.where(col <= row, a_ref[...], 0.0) * shrink, largest * shrink


def split(value):
    high = value.astype(jnp.bfloat16)
    return high, (value - high.astype(jnp.float32)).astype(jnp.bfloat16)


def product(left, right, left_dim, right_dim):
    dims = (((left_dim,), (right_dim,)), ((), ()))
    dot = lambda a, b: lax.dot_general(a, b, dims, preferred_element_type=jnp.float32)
    return dot(left[0], right[0]) + (dot(left[0], right[1]) + dot(left[1], right[0]))


def core_bit():
    return lax.rem(lax.axis_index("wide"), 2)


def own_block():
    wide, narrow = lax.axis_index("wide"), lax.axis_index("narrow")
    plane = lax.rem(narrow, 2) + 2 * lax.rem(wide // 2, 2)
    return 16 * lax.rem(wide, 2) + 4 * plane + lax.rem(wide // 4, 4)


def rows_of(block, height):
    return pl.ds(pl.multiple_of(block * height, GROUP), height)


def local_kernel(features_hbm, sketch_hbm, sampled_ref, keep_ref, send_ref, gram_keep_ref, gram_send_ref, features_ref, sketch_ref, high_ref, low_ref, flip_high_ref, flip_low_ref, cross_ref, packed_ref, sems):
    rows, depth = features_ref.shape
    rank = sketch_ref.shape[1]
    chunks = rows // BLOCK
    copies = [pltpu.make_async_copy(sketch_hbm, sketch_ref, sems.at[chunks])]
    for at in range(chunks):
        span = pl.ds(at * BLOCK, BLOCK)
        copies.append(pltpu.make_async_copy(features_hbm.at[span, :], features_ref.at[span, :], sems.at[at]))
    for copy in copies:
        copy.start()
    copies[0].wait()
    sketch = split(sketch_ref[...])
    gram = None
    step = rows // 2
    for top in range(0, rows, step):
        span = slice(top, top + step)
        for at in range(top // BLOCK, (top + step) // BLOCK):
            copies[1 + at].wait()
        features = split(features_ref[span, :])
        high_ref[span, :], low_ref[span, :] = features
        sampled = product(features, sketch, 1, 0)
        sampled_ref[span, :] = sampled
        flipped = split(sampled.T)
        flip_high_ref[:, span], flip_low_ref[:, span] = flipped
        term = product(flipped, split(sampled), 1, 0)
        gram = term if gram is None else gram + term
    packed_ref[:LANES, :] = gram[:LANES, :LANES]
    packed_ref[LANES:2 * LANES, :] = gram[:LANES, LANES:]
    packed_ref[2 * LANES:, :] = gram[LANES:, LANES:]
    half = packed_ref.shape[0] // 2
    core = core_bit()
    gram_keep_ref[...] = packed_ref[rows_of(core, half), :]
    gram_send_ref[...] = packed_ref[rows_of(1 - core, half), :]
    flipped = flip_high_ref[...], flip_low_ref[...]
    own = own_block()
    height = rank // BLOCKS
    cross_ref[...] = product(flipped, (high_ref[...], low_ref[...]), 1, 0)
    for at in range(BLOCKS):
        block = cross_ref[rows_of(at ^ own, height), :]
        if at < BLOCKS // 2:
            keep_ref[at * height:(at + 1) * height, :] = block
        else:
            rest = at - BLOCKS // 2
            send_ref[rest * height:(rest + 1) * height, :] = block


def f32(*shape):
    return jax.ShapeDtypeStruct(shape, jnp.float32)


def local_terms(features, sketch):
    rows, depth = features.shape
    rank = sketch.shape[1]
    packed = 3 * LANES
    hbm = pl.BlockSpec(memory_space=pltpu.HBM)
    return pl.pallas_call(
        local_kernel,
        out_shape=(f32(rows, rank), f32(rank // 2, depth), f32(rank // 2, depth), f32(packed // 2, LANES), f32(packed // 2, LANES)),
        in_specs=[hbm, hbm],
        out_specs=(VMEM,) * 5,
        scratch_shapes=[
            pltpu.VMEM((rows, depth), jnp.float32), pltpu.VMEM((depth, rank), jnp.float32),
            pltpu.VMEM((rows, depth), jnp.bfloat16), pltpu.VMEM((rows, depth), jnp.bfloat16),
            pltpu.VMEM((rank, rows), jnp.bfloat16), pltpu.VMEM((rank, rows), jnp.bfloat16),
            pltpu.VMEM((rank, depth), jnp.float32), pltpu.VMEM((packed, LANES), jnp.float32),
            pltpu.SemaphoreType.DMA((rows // BLOCK + 1,)),
        ],
        compiler_params=pltpu.CompilerParams(vmem_limit_bytes=51 * 2**20),
        cost_estimate=pl.CostEstimate(flops=4 * 10**9, bytes_accessed=8 * 2**20, transcendentals=0),
        name="local_terms",
    )(features, sketch)


def stage_kernel(terms, *refs):
    cross, (gram_ref, gram_other_ref, gram_out_ref), outs = refs[:terms], refs[terms:terms + 3], refs[terms + 3:]
    gram_out_ref[...] = gram_ref[...] + gram_other_ref[...]
    height = outs[0].shape[0]
    for at, out_ref in enumerate(outs):
        span = slice(at * height, (at + 1) * height)
        out_ref[...] = sum(ref[span, :] for ref in cross)


def join_kernel(*refs):
    *cross, gram_ref, gram_other_ref, gram_out_ref, out_ref = refs
    gram_out_ref[...] = gram_ref[...] + gram_other_ref[...]
    top = 0
    for ref in cross:
        out_ref[top:top + ref.shape[0], :] = ref[...]
        top += ref.shape[0]


def stage(cross, gram, gram_other, pieces, join=False):
    height, depth = cross[0].shape
    outs = [f32(len(cross) * height, depth)] if join else [f32(height // pieces, depth)] * pieces
    kernel = join_kernel if join else lambda *refs: stage_kernel(len(cross), *refs)
    gram, *outs = pl.pallas_call(
        kernel,
        out_shape=(f32(*gram.shape), *outs),
        in_specs=[VMEM] * (len(cross) + 2),
        out_specs=(VMEM,) * (1 + len(outs)),
        compiler_params=pltpu.CompilerParams(vmem_limit_bytes=16 * 2**20),
        cost_estimate=pl.CostEstimate(flops=10**6, bytes_accessed=10**6, transcendentals=0),
        name="join" if join else "stage",
    )(*cross, gram, gram_other)
    return gram, outs


def factor_kernel(scale, keep_ref, other_ref, inverse_ref, flipped_ref, factor_ref, a_ref, packed_ref):
    half = keep_ref.shape[0]
    core = core_bit()
    packed_ref[rows_of(core, half), :] = keep_ref[...]
    packed_ref[rows_of(1 - core, half), :] = other_ref[...]
    a_ref[:LANES, :LANES] = packed_ref[:LANES, :]
    a_ref[:LANES, LANES:] = packed_ref[LANES:2 * LANES, :]
    a_ref[LANES:, :LANES] = jnp.zeros((LANES, LANES), jnp.float32)
    a_ref[LANES:, LANES:] = packed_ref[2 * LANES:, :]
    inverse, grow = factorize(a_ref, factor_ref)
    inverse_ref[...] = inverse
    flipped_ref[...] = inverse.T * scale
    factor_ref[...] = factor_ref[...] * (grow / scale)


def factor(keep, other, size, scale):
    return pl.pallas_call(
        lambda *refs: factor_kernel(scale, *refs),
        out_shape=(f32(size, size),) * 3,
        in_specs=[VMEM] * 2,
        out_specs=(VMEM,) * 3,
        scratch_shapes=[pltpu.VMEM((size, size), jnp.float32), pltpu.VMEM((3 * LANES, LANES), jnp.float32)],
        compiler_params=pltpu.CompilerParams(vmem_limit_bytes=16 * 2**20),
        cost_estimate=pl.CostEstimate(flops=10 * 10**9, bytes_accessed=2**20, transcendentals=size),
        name="factor",
    )(keep, other)


def basis_kernel(sampled_ref, flipped_ref, basis_ref):
    flipped = split(flipped_ref[...])
    for top in range(0, sampled_ref.shape[0], BLOCK):
        span = slice(top, top + BLOCK)
        basis_ref[span, :] = product(split(sampled_ref[span, :]), flipped, 1, 0)


def basis_of(sampled, flipped):
    return pl.pallas_call(
        basis_kernel,
        out_shape=f32(*sampled.shape),
        in_specs=[VMEM] * 2,
        out_specs=VMEM,
        compiler_params=pltpu.CompilerParams(vmem_limit_bytes=16 * 2**20),
        cost_estimate=pl.CostEstimate(flops=2 * 10**9, bytes_accessed=2 * 2**20, transcendentals=0),
        name="basis",
    )(sampled, flipped)


def project_kernel(inverse_ref, *refs):
    *pieces, projection_ref, cross_ref = refs
    own = own_block()
    height = cross_ref.shape[0] // BLOCKS
    at = 0
    for piece in pieces:
        for top in range(0, piece.shape[0], height):
            cross_ref[rows_of(at ^ own, height), :] = piece[top:top + height, :]
            at += 1
    inverse = split(inverse_ref[...])
    for left in range(0, cross_ref.shape[1], BLOCK):
        span = slice(left, left + BLOCK)
        projection_ref[:, span] = product(inverse, split(cross_ref[:, span]), 1, 0)


def project(inverse, pieces):
    rank = inverse.shape[0]
    depth = pieces[0].shape[1]
    return pl.pallas_call(
        project_kernel,
        out_shape=jax.ShapeDtypeStruct((rank, depth), jnp.float32),
        in_specs=[VMEM] * (1 + len(pieces)),
        out_specs=VMEM,
        scratch_shapes=[pltpu.VMEM((rank, depth), jnp.float32)],
        compiler_params=pltpu.CompilerParams(vmem_limit_bytes=16 * 2**20),
        cost_estimate=pl.CostEstimate(flops=4 * 10**8, bytes_accessed=2 * 2**20, transcendentals=0),
        name="project",
    )(inverse, *pieces)


def send(value, wide, narrow):
    mask = wide * lax.axis_size("narrow") + narrow
    pairs = [(source, source ^ mask) for source in range(lax.axis_size(AXES))]
    return lax.ppermute(value, AXES, pairs)


CORE = (1, 0)
PLANE = [(0, 1), (2, 0), (2, 1)]
LINE = [(4, 0), (8, 0), (12, 0)]


def spare_bits():
    wide = [(2**bit, 0) for bit in range(4, lax.axis_size("wide").bit_length() - 1)]
    narrow = [(0, 2**bit) for bit in range(1, lax.axis_size("narrow").bit_length() - 1)]
    return wide + narrow


def spread(parts, masks):
    first, *rest = parts
    return [first] + [send(part, *mask) for part, mask in zip(rest, masks)]


def sums_and_factors(keep, other, gram_keep, gram_other, factors):
    cross = [keep, send(other, *CORE)]
    gram, parts = stage(cross, gram_keep, send(gram_other, *CORE), 4)
    cross = spread(parts, PLANE)
    gram = gram + send(gram, *LINE[0])
    gram, parts = stage(cross, gram, send(gram, *LINE[1]), 4)
    cross = spread(parts, LINE)
    gram, (own,) = stage(cross, gram, send(gram, *PLANE[0]), 1)
    for mask in spare_bits():
        own = own + send(own, *mask)
        gram = gram + send(gram, *mask)
    line = [own] + [send(own, *mask) for mask in LINE]
    gram, (line,) = stage(line, gram, send(gram, *PLANE[1]), 1, join=True)
    plane = [line] + [send(line, *mask) for mask in PLANE]
    factors = factors(gram, send(gram, *CORE))
    return plane + [send(part, *CORE) for part in plane], factors


def per_device(features, sketch):
    scale = (features.shape[0] * lax.axis_size(AXES)) ** 0.5
    size = sketch.shape[1]

    sampled, *terms = local_terms(features, sketch)
    cross, (inverse, flipped, upper) = sums_and_factors(*terms, lambda *halves: factor(*halves, size, scale))
    return (basis_of(sampled, flipped), upper, project(inverse, cross))


def solution(mesh):
    rows = P(AXES, None)
    return jax.shard_map(
        per_device, mesh=mesh, in_specs=(rows, P()), out_specs=(rows, P(), P()), check_vma=False
    )
```

```python
import jax, jax.numpy as jnp
from jax import lax
from jax.experimental import pallas as pl
from jax.experimental.pallas import tpu as pltpu
from jax.sharding import PartitionSpec as P

GROUP = 8
LANES = 128
PANEL = 64
BLOCK = 256
BLOCKS = 32
AXES = ("wide", "narrow")
VMEM = pl.BlockSpec(memory_space=pltpu.VMEM)


def factor_panel(a_ref, factor_ref, buffer_ref, base, height, size):
    lane = lax.broadcasted_iota(jnp.int32, (GROUP, LANES), 1)
    sub = lax.broadcasted_iota(jnp.int32, (GROUP, LANES), 0)
    tiles = size // LANES
    spread = lambda value: jnp.broadcast_to(value, (GROUP, LANES))

    def spread_row(slot, k):
        return spread(buffer_ref[slot * GROUP + k:slot * GROUP + k + 1, :])

    def keep(value, slot):
        buffer_ref[slot * GROUP:(slot + 1) * GROUP, :] = value

    rows = {}
    for g in range(base, base + height, GROUP):
        for t in range(tiles):
            rows[g, t] = a_ref[g:g + GROUP, t * LANES:(t + 1) * LANES]
    for top in range(base, base + height, GROUP):
        groups = list(range(top, base + height, GROUP))
        home = top // LANES
        offset = top - home * LANES
        inside = (lane >= offset) & (lane < offset + GROUP)
        diag = rows[top, home]
        bank = top // GROUP % 2 * 20
        col, one = {}, {}
        for j in range(GROUP):
            for g in groups:
                col[g, j] = spread(rows[g, home][:, offset + j:offset + j + 1])
            keep(col[top, j], bank + j)
            for k in range(j, GROUP):
                one[k, j] = spread_row(bank + j, k)
        for g in groups:
            fresh = jnp.where(lane == sub + offset, 1.0, 0.0) if g == top else 0.0
            rows[g, home] = jnp.where(inside, fresh, rows[g, home])
        for j in range(0, GROUP, 2):
            a, b, c = one[j, j], one[j + 1, j], one[j + 1, j + 1]
            first = lax.rsqrt(a)
            both = first * lax.rsqrt(a * c - b * b)
            cross = b * first
            second = a * both
            low = {}
            for k in range(j + 2, GROUP):
                low[k] = one[k, j] * first, (a * one[k, j + 1] - b * one[k, j]) * both
            for k in range(j + 2, GROUP):
                for m in range(k, GROUP):
                    one[m, k] = one[m, k] - (low[m][0] * low[k][0] + low[m][1] * low[k][1])
            scaled = {}
            for g in groups:
                scaled[g] = col[g, j] * first, (a * col[g, j + 1] - b * col[g, j]) * both
            for k in range(j + 2, GROUP):
                for g in groups:
                    col[g, k] = col[g, k] - (scaled[g][0] * low[k][0] + scaled[g][1] * low[k][1])
            below = [jnp.where(sub > j + 1, part, 0.0) for part in scaled[top]]

            def pivots(value, slot):
                slot = bank + GROUP + 3 * (j // 2) + slot
                keep(value, slot)
                upper = spread_row(slot, j) * first
                return upper, (spread_row(slot, j + 1) - cross * upper) * second

            def replaced(value, upper, lower):
                value = value - (below[0] * upper + below[1] * lower)
                return jnp.where(sub == j, upper, jnp.where(sub == j + 1, lower, value))

            diag = replaced(diag, *pivots(diag, 2))
            for t in range(tiles):
                upper, lower = pivots(rows[top, t], t)
                rows[top, t] = replaced(rows[top, t], upper, lower)
                for g in groups[1:]:
                    rows[g, t] = rows[g, t] - (scaled[g][0] * upper + scaled[g][1] * lower)
        for t in range(tiles):
            span = slice(t * LANES, (t + 1) * LANES)
            a_ref[top:top + GROUP, span] = rows[top, t]
            if t < home:
                factor_ref[top:top + GROUP, span] = jnp.zeros((GROUP, LANES), jnp.float32)
            elif t == home:
                factor_ref[top:top + GROUP, span] = jnp.where(lane >= sub + offset, diag, 0.0)
            else:
                factor_ref[top:top + GROUP, span] = rows[top, t]


def trailing(a_ref, base, height, size):
    end = base + height
    if end == size:
        return
    panel = a_ref[base:end, :]
    col = lax.broadcasted_iota(jnp.int32, (height, size), 1)
    row = lax.broadcasted_iota(jnp.int32, (height, size), 0) + base
    right = jnp.where((col <= row) | (col >= end), panel, 0.0)
    left = panel[:, end:]
    update = lax.dot_general(left, right, (((0,), (0,)), ((), ())), precision=lax.Precision.HIGHEST, preferred_element_type=jnp.float32)
    rest = a_ref[end:, :]
    at = lax.broadcasted_iota(jnp.int32, (size - end, size), 1)
    a_ref[end:, :] = jnp.where((at >= base) & (at < end), 0.0, rest) - update


def factorize(a_ref, factor_ref, buffer_ref):
    size = a_ref.shape[0]
    col = lax.broadcasted_iota(jnp.int32, (size, size), 1)
    row = lax.broadcasted_iota(jnp.int32, (size, size), 0)
    largest = jnp.max(jnp.where(col == row, a_ref[...], 0.0), axis=(0, 1), keepdims=True)
    shrink = lax.rsqrt(largest)
    a_ref[...] = a_ref[...] * shrink * shrink
    for base in range(0, size, PANEL):
        factor_panel(a_ref, factor_ref, buffer_ref, base, PANEL, size)
        trailing(a_ref, base, PANEL, size)
    return jnp.where(col <= row, a_ref[...], 0.0) * shrink, largest * shrink


def split(value):
    high = value.astype(jnp.bfloat16)
    return high, (value - high.astype(jnp.float32)).astype(jnp.bfloat16)


def product(left, right, left_dim, right_dim):
    dims = (((left_dim,), (right_dim,)), ((), ()))
    dot = lambda a, b: lax.dot_general(a, b, dims, preferred_element_type=jnp.float32)
    return dot(left[0], right[0]) + (dot(left[0], right[1]) + dot(left[1], right[0]))


def core_bit():
    return lax.rem(lax.axis_index("wide"), 2)


def own_block():
    wide, narrow = lax.axis_index("wide"), lax.axis_index("narrow")
    plane = lax.rem(narrow, 2) + 2 * lax.rem(wide // 2, 2)
    return 16 * lax.rem(wide, 2) + 4 * plane + lax.rem(wide // 4, 4)


def rows_of(block, height):
    return pl.ds(pl.multiple_of(block * height, GROUP), height)


def local_kernel(features_hbm, sketch_hbm, sampled_ref, keep_ref, send_ref, gram_keep_ref, gram_send_ref, features_ref, sketch_ref, cross_ref, packed_ref, sems):
    rows, depth = features_ref.shape
    rank = sketch_ref.shape[1]
    chunks = rows // BLOCK
    copies = [pltpu.make_async_copy(sketch_hbm, sketch_ref, sems.at[chunks])]
    for at in range(chunks):
        span = pl.ds(at * BLOCK, BLOCK)
        copies.append(pltpu.make_async_copy(features_hbm.at[span, :], features_ref.at[span, :], sems.at[at]))
    for copy in copies:
        copy.start()
    copies[0].wait()
    sketch = split(sketch_ref[...])
    gram = None
    for at in range(chunks):
        span = slice(at * BLOCK, (at + 1) * BLOCK)
        copies[1 + at].wait()
        features = split(features_ref[span, :])
        sampled = product(features, sketch, 1, 0)
        sampled_ref[span, :] = sampled
        flipped = split(sampled.T)
        term = product(flipped, split(sampled), 1, 0)
        gram = term if gram is None else gram + term
        for left in range(0, depth, BLOCK):
            columns = slice(left, left + BLOCK)
            term = product(flipped, [part[:, columns] for part in features], 1, 0)
            cross_ref[:, columns] = term if at == 0 else cross_ref[:, columns] + term
    packed_ref[:LANES, :] = gram[:LANES, :LANES]
    packed_ref[LANES:2 * LANES, :] = gram[:LANES, LANES:]
    packed_ref[2 * LANES:, :] = gram[LANES:, LANES:]
    half = packed_ref.shape[0] // 2
    core = core_bit()
    gram_keep_ref[...] = packed_ref[rows_of(core, half), :]
    gram_send_ref[...] = packed_ref[rows_of(1 - core, half), :]
    own = own_block()
    height = rank // BLOCKS
    for at in range(BLOCKS):
        block = cross_ref[rows_of(at ^ own, height), :]
        if at < BLOCKS // 2:
            keep_ref[at * height:(at + 1) * height, :] = block
        else:
            rest = at - BLOCKS // 2
            send_ref[rest * height:(rest + 1) * height, :] = block


def f32(*shape):
    return jax.ShapeDtypeStruct(shape, jnp.float32)


def local_terms(features, sketch):
    rows, depth = features.shape
    rank = sketch.shape[1]
    packed = 3 * LANES
    hbm = pl.BlockSpec(memory_space=pltpu.HBM)
    return pl.pallas_call(
        local_kernel,
        out_shape=(f32(rows, rank), f32(rank // 2, depth), f32(rank // 2, depth), f32(packed // 2, LANES), f32(packed // 2, LANES)),
        in_specs=[hbm, hbm],
        out_specs=(VMEM,) * 5,
        scratch_shapes=[
            pltpu.VMEM((rows, depth), jnp.float32), pltpu.VMEM((depth, rank), jnp.float32),
            pltpu.VMEM((rank, depth), jnp.float32), pltpu.VMEM((packed, LANES), jnp.float32),
            pltpu.SemaphoreType.DMA((rows // BLOCK + 1,)),
        ],
        compiler_params=pltpu.CompilerParams(vmem_limit_bytes=51 * 2**20),
        cost_estimate=pl.CostEstimate(flops=4 * 10**9, bytes_accessed=8 * 2**20, transcendentals=0),
        name="local_terms",
    )(features, sketch)


def stage_kernel(terms, *refs):
    cross, (gram_ref, gram_other_ref, gram_out_ref), outs = refs[:terms], refs[terms:terms + 3], refs[terms + 3:]
    gram_out_ref[...] = gram_ref[...] + gram_other_ref[...]
    height = outs[0].shape[0]
    for at, out_ref in enumerate(outs):
        span = slice(at * height, (at + 1) * height)
        out_ref[...] = sum(ref[span, :] for ref in cross)


def join_kernel(*refs):
    *cross, gram_ref, gram_other_ref, gram_out_ref, out_ref = refs
    gram_out_ref[...] = gram_ref[...] + gram_other_ref[...]
    top = 0
    for ref in cross:
        out_ref[top:top + ref.shape[0], :] = ref[...]
        top += ref.shape[0]


def stage(cross, gram, gram_other, pieces, join=False):
    height, depth = cross[0].shape
    outs = [f32(len(cross) * height, depth)] if join else [f32(height // pieces, depth)] * pieces
    kernel = join_kernel if join else lambda *refs: stage_kernel(len(cross), *refs)
    gram, *outs = pl.pallas_call(
        kernel,
        out_shape=(f32(*gram.shape), *outs),
        in_specs=[VMEM] * (len(cross) + 2),
        out_specs=(VMEM,) * (1 + len(outs)),
        compiler_params=pltpu.CompilerParams(vmem_limit_bytes=16 * 2**20),
        cost_estimate=pl.CostEstimate(flops=10**6, bytes_accessed=10**6, transcendentals=0),
        name="join" if join else "stage",
    )(*cross, gram, gram_other)
    return gram, outs


def factor_kernel(scale, keep_ref, other_ref, inverse_ref, flipped_ref, factor_ref, a_ref, packed_ref, buffer_ref):
    half = keep_ref.shape[0]
    core = core_bit()
    packed_ref[rows_of(core, half), :] = keep_ref[...]
    packed_ref[rows_of(1 - core, half), :] = other_ref[...]
    a_ref[:LANES, :LANES] = packed_ref[:LANES, :]
    a_ref[:LANES, LANES:] = packed_ref[LANES:2 * LANES, :]
    a_ref[LANES:, :LANES] = jnp.zeros((LANES, LANES), jnp.float32)
    a_ref[LANES:, LANES:] = packed_ref[2 * LANES:, :]
    inverse, grow = factorize(a_ref, factor_ref, buffer_ref)
    inverse_ref[...] = inverse
    flipped_ref[...] = inverse.T * scale
    factor_ref[...] = factor_ref[...] * (grow / scale)


def factor(keep, other, size, scale):
    return pl.pallas_call(
        lambda *refs: factor_kernel(scale, *refs),
        out_shape=(f32(size, size),) * 3,
        in_specs=[VMEM] * 2,
        out_specs=(VMEM,) * 3,
        scratch_shapes=[pltpu.VMEM((size, size), jnp.float32), pltpu.VMEM((3 * LANES, LANES), jnp.float32), pltpu.VMEM((40 * GROUP, LANES), jnp.float32)],
        compiler_params=pltpu.CompilerParams(vmem_limit_bytes=16 * 2**20),
        cost_estimate=pl.CostEstimate(flops=10 * 10**9, bytes_accessed=2**20, transcendentals=size),
        name="factor",
    )(keep, other)


def basis_kernel(sampled_ref, flipped_ref, basis_ref):
    flipped = split(flipped_ref[...])
    for top in range(0, sampled_ref.shape[0], BLOCK):
        span = slice(top, top + BLOCK)
        basis_ref[span, :] = product(split(sampled_ref[span, :]), flipped, 1, 0)


def basis_of(sampled, flipped):
    return pl.pallas_call(
        basis_kernel,
        out_shape=f32(*sampled.shape),
        in_specs=[VMEM] * 2,
        out_specs=VMEM,
        compiler_params=pltpu.CompilerParams(vmem_limit_bytes=16 * 2**20),
        cost_estimate=pl.CostEstimate(flops=2 * 10**9, bytes_accessed=2 * 2**20, transcendentals=0),
        name="basis",
    )(sampled, flipped)


def project_kernel(inverse_ref, *refs):
    *pieces, projection_ref, cross_ref = refs
    own = own_block()
    height = cross_ref.shape[0] // BLOCKS
    at = 0
    for piece in pieces:
        for top in range(0, piece.shape[0], height):
            cross_ref[rows_of(at ^ own, height), :] = piece[top:top + height, :]
            at += 1
    inverse = split(inverse_ref[...])
    for left in range(0, cross_ref.shape[1], BLOCK):
        span = slice(left, left + BLOCK)
        projection_ref[:, span] = product(inverse, split(cross_ref[:, span]), 1, 0)


def project(inverse, pieces):
    rank = inverse.shape[0]
    depth = pieces[0].shape[1]
    return pl.pallas_call(
        project_kernel,
        out_shape=jax.ShapeDtypeStruct((rank, depth), jnp.float32),
        in_specs=[VMEM] * (1 + len(pieces)),
        out_specs=VMEM,
        scratch_shapes=[pltpu.VMEM((rank, depth), jnp.float32)],
        compiler_params=pltpu.CompilerParams(vmem_limit_bytes=16 * 2**20),
        cost_estimate=pl.CostEstimate(flops=4 * 10**8, bytes_accessed=2 * 2**20, transcendentals=0),
        name="project",
    )(inverse, *pieces)


def send(value, wide, narrow):
    mask = wide * lax.axis_size("narrow") + narrow
    pairs = [(source, source ^ mask) for source in range(lax.axis_size(AXES))]
    return lax.ppermute(value, AXES, pairs)


CORE = (1, 0)
PLANE = [(0, 1), (2, 0), (2, 1)]
LINE = [(4, 0), (8, 0), (12, 0)]


def spare_bits():
    wide = [(2**bit, 0) for bit in range(4, lax.axis_size("wide").bit_length() - 1)]
    narrow = [(0, 2**bit) for bit in range(1, lax.axis_size("narrow").bit_length() - 1)]
    return wide + narrow


def spread(parts, masks):
    first, *rest = parts
    return [first] + [send(part, *mask) for part, mask in zip(rest, masks)]


def sums_and_factors(keep, other, gram_keep, gram_other, factors):
    cross = [keep, send(other, *CORE)]
    gram, parts = stage(cross, gram_keep, send(gram_other, *CORE), 4)
    cross = spread(parts, PLANE)
    gram = gram + send(gram, *LINE[0])
    gram, parts = stage(cross, gram, send(gram, *LINE[1]), 4)
    cross = spread(parts, LINE)
    gram, (own,) = stage(cross, gram, send(gram, *PLANE[0]), 1)
    for mask in spare_bits():
        own = own + send(own, *mask)
        gram = gram + send(gram, *mask)
    line = [own] + [send(own, *mask) for mask in LINE]
    gram, (line,) = stage(line, gram, send(gram, *PLANE[1]), 1, join=True)
    plane = [line] + [send(line, *mask) for mask in PLANE]
    factors = factors(gram, send(gram, *CORE))
    return plane + [send(part, *CORE) for part in plane], factors


def per_device(features, sketch):
    scale = (features.shape[0] * lax.axis_size(AXES)) ** 0.5
    size = sketch.shape[1]

    sampled, *terms = local_terms(features, sketch)
    cross, (inverse, flipped, upper) = sums_and_factors(*terms, lambda *halves: factor(*halves, size, scale))
    return (basis_of(sampled, flipped), upper, project(inverse, cross))


def solution(mesh):
    rows = P(AXES, None)
    return jax.shard_map(
        per_device, mesh=mesh, in_specs=(rows, P()), out_specs=(rows, P(), P()), check_vma=False
    )
```

```python
import jax, jax.numpy as jnp
from jax import lax
from jax.experimental import pallas as pl
from jax.experimental.pallas import tpu as pltpu
from jax.sharding import PartitionSpec as P

GROUP = 8
LANES = 128
PANEL = 64
BLOCK = 256
BLOCKS = 32
AXES = ("wide", "narrow")
VMEM = pl.BlockSpec(memory_space=pltpu.VMEM)


def factor_panel(a_ref, factor_ref, buffer_ref, base, height, size):
    lane = lax.broadcasted_iota(jnp.int32, (GROUP, LANES), 1)
    sub = lax.broadcasted_iota(jnp.int32, (GROUP, LANES), 0)
    tiles = size // LANES
    spread = lambda value: jnp.broadcast_to(value, (GROUP, LANES))

    def spread_row(slot, k):
        return spread(buffer_ref[slot * GROUP + k:slot * GROUP + k + 1, :])

    def keep(value, slot):
        buffer_ref[slot * GROUP:(slot + 1) * GROUP, :] = value

    rows = {}
    for g in range(base, base + height, GROUP):
        for t in range(tiles):
            rows[g, t] = a_ref[g:g + GROUP, t * LANES:(t + 1) * LANES]
    for top in range(base, base + height, GROUP):
        groups = list(range(top, base + height, GROUP))
        home = top // LANES
        offset = top - home * LANES
        inside = (lane >= offset) & (lane < offset + GROUP)
        diag = rows[top, home]
        bank = top // GROUP % 2 * 20
        col, one = {}, {}
        for j in range(GROUP):
            for g in groups:
                col[g, j] = spread(rows[g, home][:, offset + j:offset + j + 1])
            keep(col[top, j], bank + j)
            for k in range(j, GROUP):
                one[k, j] = spread_row(bank + j, k)
        for g in groups:
            fresh = jnp.where(lane == sub + offset, 1.0, 0.0) if g == top else 0.0
            rows[g, home] = jnp.where(inside, fresh, rows[g, home])
        for j in range(0, GROUP, 2):
            a, b, c = one[j, j], one[j + 1, j], one[j + 1, j + 1]
            first = lax.rsqrt(a)
            both = first * lax.rsqrt(a * c - b * b)
            cross = b * first
            second = a * both
            low = {}
            for k in range(j + 2, GROUP):
                low[k] = one[k, j] * first, (a * one[k, j + 1] - b * one[k, j]) * both
            for k in range(j + 2, GROUP):
                for m in range(k, GROUP):
                    one[m, k] = one[m, k] - (low[m][0] * low[k][0] + low[m][1] * low[k][1])
            scaled = {}
            for g in groups:
                scaled[g] = col[g, j] * first, (a * col[g, j + 1] - b * col[g, j]) * both
            for k in range(j + 2, GROUP):
                for g in groups:
                    col[g, k] = col[g, k] - (scaled[g][0] * low[k][0] + scaled[g][1] * low[k][1])
            below = [jnp.where(sub > j + 1, part, 0.0) for part in scaled[top]]

            def pivots(value, slot):
                slot = bank + GROUP + 3 * (j // 2) + slot
                keep(value, slot)
                upper = spread_row(slot, j) * first
                return upper, (spread_row(slot, j + 1) - cross * upper) * second

            def replaced(value, upper, lower):
                value = value - (below[0] * upper + below[1] * lower)
                return jnp.where(sub == j, upper, jnp.where(sub == j + 1, lower, value))

            diag = replaced(diag, *pivots(diag, 2))
            for t in range(tiles):
                upper, lower = pivots(rows[top, t], t)
                rows[top, t] = replaced(rows[top, t], upper, lower)
                for g in groups[1:]:
                    rows[g, t] = rows[g, t] - (scaled[g][0] * upper + scaled[g][1] * lower)
        for t in range(tiles):
            span = slice(t * LANES, (t + 1) * LANES)
            a_ref[top:top + GROUP, span] = rows[top, t]
            if t < home:
                factor_ref[top:top + GROUP, span] = jnp.zeros((GROUP, LANES), jnp.float32)
            elif t == home:
                factor_ref[top:top + GROUP, span] = jnp.where(lane >= sub + offset, diag, 0.0)
            else:
                factor_ref[top:top + GROUP, span] = rows[top, t]


def trailing(a_ref, base, height, size):
    end = base + height
    if end == size:
        return
    panel = a_ref[base:end, :]
    col = lax.broadcasted_iota(jnp.int32, (height, size), 1)
    row = lax.broadcasted_iota(jnp.int32, (height, size), 0) + base
    right = jnp.where((col <= row) | (col >= end), panel, 0.0)
    left = panel[:, end:]
    update = lax.dot_general(left, right, (((0,), (0,)), ((), ())), precision=lax.Precision.HIGHEST, preferred_element_type=jnp.float32)
    rest = a_ref[end:, :]
    at = lax.broadcasted_iota(jnp.int32, (size - end, size), 1)
    a_ref[end:, :] = jnp.where((at >= base) & (at < end), 0.0, rest) - update


def normalize(a_ref):
    size = a_ref.shape[0]
    col = lax.broadcasted_iota(jnp.int32, (size, size), 1)
    row = lax.broadcasted_iota(jnp.int32, (size, size), 0)
    largest = jnp.max(jnp.where(col == row, a_ref[...], 0.0), axis=(0, 1), keepdims=True)
    shrink = lax.rsqrt(largest)
    a_ref[...] = a_ref[...] * shrink * shrink
    return shrink, largest * shrink


def eliminate(a_ref, factor_ref, buffer_ref, first, last):
    size = a_ref.shape[0]
    for base in range(first, last, PANEL):
        factor_panel(a_ref, factor_ref, buffer_ref, base, PANEL, size)
        trailing(a_ref, base, PANEL, size)


def split(value):
    high = value.astype(jnp.bfloat16)
    return high, (value - high.astype(jnp.float32)).astype(jnp.bfloat16)


def product(left, right, left_dim, right_dim):
    dims = (((left_dim,), (right_dim,)), ((), ()))
    dot = lambda a, b: lax.dot_general(a, b, dims, preferred_element_type=jnp.float32)
    return dot(left[0], right[0]) + (dot(left[0], right[1]) + dot(left[1], right[0]))


def core_bit():
    return lax.rem(lax.axis_index("wide"), 2)


def own_block():
    wide, narrow = lax.axis_index("wide"), lax.axis_index("narrow")
    plane = lax.rem(narrow, 2) + 2 * lax.rem(wide // 2, 2)
    return 16 * lax.rem(wide, 2) + 4 * plane + lax.rem(wide // 4, 4)


def rows_of(block, height):
    return pl.ds(pl.multiple_of(block * height, GROUP), height)


def local_kernel(features_hbm, sketch_hbm, sampled_ref, keep_ref, send_ref, gram_keep_ref, gram_send_ref, features_ref, sketch_ref, high_ref, low_ref, flip_high_ref, flip_low_ref, cross_ref, packed_ref, sems):
    rows, depth = features_ref.shape
    rank = sketch_ref.shape[1]
    chunks = rows // BLOCK
    copies = [pltpu.make_async_copy(sketch_hbm, sketch_ref, sems.at[chunks])]
    for at in range(chunks):
        span = pl.ds(at * BLOCK, BLOCK)
        copies.append(pltpu.make_async_copy(features_hbm.at[span, :], features_ref.at[span, :], sems.at[at]))
    for copy in copies:
        copy.start()
    copies[0].wait()
    sketch = split(sketch_ref[...])
    gram = None
    for at in range(chunks):
        span = slice(at * BLOCK, (at + 1) * BLOCK)
        copies[1 + at].wait()
        features = split(features_ref[span, :])
        high_ref[span, :], low_ref[span, :] = features
        sampled = product(features, sketch, 1, 0)
        sampled_ref[span, :] = sampled
        flipped = split(sampled.T)
        flip_high_ref[:, span], flip_low_ref[:, span] = flipped
        term = product(flipped, split(sampled), 1, 0)
        gram = term if gram is None else gram + term
    packed_ref[:LANES, :] = gram[:LANES, :LANES]
    packed_ref[LANES:2 * LANES, :] = gram[:LANES, LANES:]
    packed_ref[2 * LANES:, :] = gram[LANES:, LANES:]
    half = packed_ref.shape[0] // 2
    core = core_bit()
    gram_keep_ref[...] = packed_ref[rows_of(core, half), :]
    gram_send_ref[...] = packed_ref[rows_of(1 - core, half), :]
    flipped = flip_high_ref[...], flip_low_ref[...]
    own = own_block()
    height = rank // BLOCKS
    for left in range(0, depth, BLOCK):
        span = slice(left, left + BLOCK)
        cross_ref[:, span] = product(flipped, (high_ref[:, span], low_ref[:, span]), 1, 0)
    for at in range(BLOCKS):
        block = cross_ref[rows_of(at ^ own, height), :]
        if at < BLOCKS // 2:
            keep_ref[at * height:(at + 1) * height, :] = block
        else:
            rest = at - BLOCKS // 2
            send_ref[rest * height:(rest + 1) * height, :] = block


def f32(*shape):
    return jax.ShapeDtypeStruct(shape, jnp.float32)


def local_terms(features, sketch):
    rows, depth = features.shape
    rank = sketch.shape[1]
    packed = 3 * LANES
    hbm = pl.BlockSpec(memory_space=pltpu.HBM)
    return pl.pallas_call(
        local_kernel,
        out_shape=(f32(rows, rank), f32(rank // 2, depth), f32(rank // 2, depth), f32(packed // 2, LANES), f32(packed // 2, LANES)),
        in_specs=[hbm, hbm],
        out_specs=(VMEM,) * 5,
        scratch_shapes=[
            pltpu.VMEM((rows, depth), jnp.float32), pltpu.VMEM((depth, rank), jnp.float32),
            pltpu.VMEM((rows, depth), jnp.bfloat16), pltpu.VMEM((rows, depth), jnp.bfloat16),
            pltpu.VMEM((rank, rows), jnp.bfloat16), pltpu.VMEM((rank, rows), jnp.bfloat16),
            pltpu.VMEM((rank, depth), jnp.float32), pltpu.VMEM((packed, LANES), jnp.float32),
            pltpu.SemaphoreType.DMA((rows // BLOCK + 1,)),
        ],
        compiler_params=pltpu.CompilerParams(vmem_limit_bytes=51 * 2**20),
        cost_estimate=pl.CostEstimate(flops=4 * 10**9, bytes_accessed=8 * 2**20, transcendentals=0),
        name="local_terms",
    )(features, sketch)


def call(kernel, name, outs, *operands, after=(), scratch=(), flops=10**6):
    return pl.pallas_call(
        lambda *refs: kernel(*refs[:len(operands)], *refs[len(operands) + len(after):]),
        out_shape=outs,
        in_specs=[VMEM] * len(operands) + [pl.BlockSpec(memory_space=pl.ANY)] * len(after),
        out_specs=jax.tree.map(lambda _: VMEM, outs),
        scratch_shapes=list(scratch),
        compiler_params=pltpu.CompilerParams(vmem_limit_bytes=16 * 2**20),
        cost_estimate=pl.CostEstimate(flops=flops, bytes_accessed=10**6, transcendentals=0),
        name=name,
    )(*operands, *after)


def sum_kernel(order, terms, *refs):
    cross, (gram_ref, gram_other_ref), outs = refs[:terms], refs[terms:terms + 2], refs[terms + 2:]
    outs[0][...] = gram_ref[...] + gram_other_ref[...]
    at = 0
    for out_ref in outs[1:]:
        for top in range(0, out_ref.shape[0], GROUP):
            span = slice(order[at] * GROUP, (order[at] + 1) * GROUP)
            out_ref[top:top + GROUP, :] = sum(ref[span, :] for ref in cross)
            at += 1


def sums(cross, gram, gram_other, pieces, order=None):
    height, depth = cross[0].shape
    order = order or tuple(range(height // GROUP))
    outs = (f32(*gram.shape), *[f32(height // pieces, depth)] * pieces)
    kernel = lambda *refs: sum_kernel(order, len(cross), *refs)
    gram, *outs = call(kernel, "sums", outs, *cross, gram, gram_other)
    return gram, outs


def weave_kernel(*refs):
    *parts, out_ref = refs
    for top in range(0, out_ref.shape[0], GROUP):
        block = top // GROUP
        at = block // len(parts) * GROUP
        out_ref[top:top + GROUP, :] = parts[block % len(parts)][at:at + GROUP, :]


def weave(parts, after=()):
    height, depth = parts[0].shape
    return call(weave_kernel, "weave", f32(len(parts) * height, depth), *parts, after=after)


def first_half_kernel(keep_ref, other_ref, a_ref, factor_ref, norm_ref, packed_ref, buffer_ref):
    half = keep_ref.shape[0]
    core = core_bit()
    packed_ref[rows_of(core, half), :] = keep_ref[...]
    packed_ref[rows_of(1 - core, half), :] = other_ref[...]
    a_ref[:LANES, :LANES] = packed_ref[:LANES, :]
    a_ref[:LANES, LANES:] = packed_ref[LANES:2 * LANES, :]
    a_ref[LANES:, :LANES] = jnp.zeros((LANES, LANES), jnp.float32)
    a_ref[LANES:, LANES:] = packed_ref[2 * LANES:, :]
    shrink, grow = normalize(a_ref)
    norm_ref[:GROUP, :] = jnp.broadcast_to(shrink, (GROUP, LANES))
    norm_ref[GROUP:, :] = jnp.broadcast_to(grow, (GROUP, LANES))
    eliminate(a_ref, factor_ref, buffer_ref, 0, a_ref.shape[0] // 2)


def second_half_kernel(scale, from_ref, upper_ref, norm_ref, inverse_ref, flipped_ref, factor_ref, a_ref, buffer_ref):
    size = a_ref.shape[0]
    a_ref[...] = from_ref[...]
    eliminate(a_ref, factor_ref, buffer_ref, size // 2, size)
    shrink, grow = norm_ref[:1, :1], norm_ref[GROUP:GROUP + 1, :1] / scale
    factor_ref[:size // 2, :] = upper_ref[:size // 2, :] * grow
    factor_ref[size // 2:, :] = factor_ref[size // 2:, :] * grow
    col = lax.broadcasted_iota(jnp.int32, (size, size), 1)
    row = lax.broadcasted_iota(jnp.int32, (size, size), 0)
    inverse = jnp.where(col <= row, a_ref[...], 0.0) * shrink
    inverse_ref[...] = inverse
    flipped_ref[...] = inverse.T * scale


def first_half(keep, other, size, after):
    square = f32(size, size)
    scratch = pltpu.VMEM((3 * LANES, LANES), jnp.float32), pltpu.VMEM((40 * GROUP, LANES), jnp.float32)
    return call(first_half_kernel, "first_half", (square, square, f32(2 * GROUP, LANES)), keep, other, after=after, scratch=scratch, flops=5 * 10**9)


def second_half(state, size, scale, after):
    square = f32(size, size)
    scratch = pltpu.VMEM((size, size), jnp.float32), pltpu.VMEM((40 * GROUP, LANES), jnp.float32)
    kernel = lambda *refs: second_half_kernel(scale, *refs)
    return call(kernel, "second_half", (square, square, square), *state, after=after, scratch=scratch, flops=5 * 10**9)


def basis_kernel(sampled_ref, flipped_ref, basis_ref):
    flipped = split(flipped_ref[...])
    for top in range(0, sampled_ref.shape[0], BLOCK):
        span = slice(top, top + BLOCK)
        basis_ref[span, :] = product(split(sampled_ref[span, :]), flipped, 1, 0)


def basis_of(sampled, flipped):
    return pl.pallas_call(
        basis_kernel,
        out_shape=f32(*sampled.shape),
        in_specs=[VMEM] * 2,
        out_specs=VMEM,
        compiler_params=pltpu.CompilerParams(vmem_limit_bytes=16 * 2**20),
        cost_estimate=pl.CostEstimate(flops=2 * 10**9, bytes_accessed=2 * 2**20, transcendentals=0),
        name="basis",
    )(sampled, flipped)


def project_kernel(inverse_ref, *refs):
    *pieces, projection_ref, cross_ref = refs
    own = own_block()
    height = cross_ref.shape[0] // BLOCKS
    at = 0
    for piece in pieces:
        for top in range(0, piece.shape[0], height):
            cross_ref[rows_of(at ^ own, height), :] = piece[top:top + height, :]
            at += 1
    inverse = split(inverse_ref[...])
    for left in range(0, cross_ref.shape[1], BLOCK):
        span = slice(left, left + BLOCK)
        projection_ref[:, span] = product(inverse, split(cross_ref[:, span]), 1, 0)


def project(inverse, pieces):
    rank = inverse.shape[0]
    depth = pieces[0].shape[1]
    return pl.pallas_call(
        project_kernel,
        out_shape=jax.ShapeDtypeStruct((rank, depth), jnp.float32),
        in_specs=[VMEM] * (1 + len(pieces)),
        out_specs=VMEM,
        scratch_shapes=[pltpu.VMEM((rank, depth), jnp.float32)],
        compiler_params=pltpu.CompilerParams(vmem_limit_bytes=16 * 2**20),
        cost_estimate=pl.CostEstimate(flops=4 * 10**8, bytes_accessed=2 * 2**20, transcendentals=0),
        name="project",
    )(inverse, *pieces)


def send(value, wide, narrow):
    mask = wide * lax.axis_size("narrow") + narrow
    pairs = [(source, source ^ mask) for source in range(lax.axis_size(AXES))]
    return lax.ppermute(value, AXES, pairs)


CORE = (1, 0)
PLANE = [(0, 1), (2, 0), (2, 1)]
NEAR, FAR = (4, 0), (8, 0)


def spare_bits():
    wide = [(2**bit, 0) for bit in range(4, lax.axis_size("wide").bit_length() - 1)]
    narrow = [(0, 2**bit) for bit in range(1, lax.axis_size("narrow").bit_length() - 1)]
    return wide + narrow


def spread(parts, masks):
    first, *rest = parts
    return [first] + [send(part, *mask) for part, mask in zip(rest, masks)]


def per_device(features, sketch):
    scale = (features.shape[0] * lax.axis_size(AXES)) ** 0.5
    size = sketch.shape[1]
    sampled, keep, other, gram, gram_other = local_terms(features, sketch)
    cross = [keep, send(other, *CORE)]
    gram, parts = sums(cross, gram, send(gram_other, *CORE), 4)
    cross = spread(parts, PLANE)
    gram = gram + send(gram, *NEAR)
    gram, (keep, other) = sums(cross, gram, send(gram, *FAR), 2, (0, 2, 1, 3))
    gram, (keep, other) = sums([keep, send(other, *NEAR)], gram, send(gram, *PLANE[0]), 2)
    gram, (own,) = sums([keep, send(other, *FAR)], gram, send(gram, *PLANE[1]), 1)
    for mask in spare_bits():
        own = own + send(own, *mask)
        gram = gram + send(gram, *mask)
    pair = weave([own, send(own, *FAR)])
    state = first_half(gram, send(gram, *CORE), size, (pair,))
    line = weave([pair, send(pair, *NEAR)], state[:1])
    plane = [line] + [send(line, *mask) for mask in PLANE]
    inverse, flipped, factor = second_half(state, size, scale, (line,))
    cross = plane + [send(part, *CORE) for part in plane]
    return (basis_of(sampled, flipped), factor, project(inverse, cross))


def solution(mesh):
    rows = P(AXES, None)
    return jax.shard_map(
        per_device, mesh=mesh, in_specs=(rows, P()), out_specs=(rows, P(), P()), check_vma=False
    )
```

```python
import jax, jax.numpy as jnp
from jax import lax
from jax.experimental import pallas as pl
from jax.experimental.pallas import tpu as pltpu
from jax.sharding import PartitionSpec as P

GROUP = 8
LANES = 128
PANEL = 64
BLOCK = 256
BLOCKS = 32
AXES = ("wide", "narrow")
VMEM = pl.BlockSpec(memory_space=pltpu.VMEM)


def factor_panel(a_ref, factor_ref, buffer_ref, base, height, size):
    lane = lax.broadcasted_iota(jnp.int32, (GROUP, LANES), 1)
    sub = lax.broadcasted_iota(jnp.int32, (GROUP, LANES), 0)
    tiles = size // LANES
    spread = lambda value: jnp.broadcast_to(value, (GROUP, LANES))

    def spread_row(slot, k):
        return spread(buffer_ref[slot * GROUP + k:slot * GROUP + k + 1, :])

    def keep(value, slot):
        buffer_ref[slot * GROUP:(slot + 1) * GROUP, :] = value

    rows = {}
    for g in range(base, base + height, GROUP):
        for t in range(tiles):
            rows[g, t] = a_ref[g:g + GROUP, t * LANES:(t + 1) * LANES]
    for top in range(base, base + height, GROUP):
        groups = list(range(top, base + height, GROUP))
        home = top // LANES
        offset = top - home * LANES
        inside = (lane >= offset) & (lane < offset + GROUP)
        diag = rows[top, home]
        bank = top // GROUP % 2 * 20
        col, one = {}, {}
        for j in range(GROUP):
            for g in groups:
                col[g, j] = spread(rows[g, home][:, offset + j:offset + j + 1])
            keep(col[top, j], bank + j)
            for k in range(j, GROUP):
                one[k, j] = spread_row(bank + j, k)
        for g in groups:
            fresh = jnp.where(lane == sub + offset, 1.0, 0.0) if g == top else 0.0
            rows[g, home] = jnp.where(inside, fresh, rows[g, home])
        for j in range(0, GROUP, 2):
            a, b, c = one[j, j], one[j + 1, j], one[j + 1, j + 1]
            first = lax.rsqrt(a)
            both = first * lax.rsqrt(a * c - b * b)
            cross = b * first
            second = a * both
            low = {}
            for k in range(j + 2, GROUP):
                low[k] = one[k, j] * first, (a * one[k, j + 1] - b * one[k, j]) * both
            for k in range(j + 2, GROUP):
                for m in range(k, GROUP):
                    one[m, k] = one[m, k] - (low[m][0] * low[k][0] + low[m][1] * low[k][1])
            scaled = {}
            for g in groups:
                scaled[g] = col[g, j] * first, (a * col[g, j + 1] - b * col[g, j]) * both
            for k in range(j + 2, GROUP):
                for g in groups:
                    col[g, k] = col[g, k] - (scaled[g][0] * low[k][0] + scaled[g][1] * low[k][1])
            below = [jnp.where(sub > j + 1, part, 0.0) for part in scaled[top]]

            def pivots(value, slot):
                slot = bank + GROUP + 3 * (j // 2) + slot
                keep(value, slot)
                upper = spread_row(slot, j) * first
                return upper, (spread_row(slot, j + 1) - cross * upper) * second

            def replaced(value, upper, lower):
                value = value - (below[0] * upper + below[1] * lower)
                return jnp.where(sub == j, upper, jnp.where(sub == j + 1, lower, value))

            diag = replaced(diag, *pivots(diag, 2))
            for t in range(tiles):
                upper, lower = pivots(rows[top, t], t)
                rows[top, t] = replaced(rows[top, t], upper, lower)
                for g in groups[1:]:
                    rows[g, t] = rows[g, t] - (scaled[g][0] * upper + scaled[g][1] * lower)
        for t in range(tiles):
            span = slice(t * LANES, (t + 1) * LANES)
            a_ref[top:top + GROUP, span] = rows[top, t]
            if t < home:
                factor_ref[top:top + GROUP, span] = jnp.zeros((GROUP, LANES), jnp.float32)
            elif t == home:
                factor_ref[top:top + GROUP, span] = jnp.where(lane >= sub + offset, diag, 0.0)
            else:
                factor_ref[top:top + GROUP, span] = rows[top, t]


def trailing(a_ref, base, height, size):
    end = base + height
    if end == size:
        return
    panel = a_ref[base:end, :]
    col = lax.broadcasted_iota(jnp.int32, (height, size), 1)
    row = lax.broadcasted_iota(jnp.int32, (height, size), 0) + base
    right = jnp.where((col <= row) | (col >= end), panel, 0.0)
    left = panel[:, end:]
    update = lax.dot_general(left, right, (((0,), (0,)), ((), ())), precision=lax.Precision.HIGHEST, preferred_element_type=jnp.float32)
    rest = a_ref[end:, :]
    at = lax.broadcasted_iota(jnp.int32, (size - end, size), 1)
    a_ref[end:, :] = jnp.where((at >= base) & (at < end), 0.0, rest) - update


def normalize(a_ref):
    size = a_ref.shape[0]
    col = lax.broadcasted_iota(jnp.int32, (size, size), 1)
    row = lax.broadcasted_iota(jnp.int32, (size, size), 0)
    largest = jnp.max(jnp.where(col == row, a_ref[...], 0.0), axis=(0, 1), keepdims=True)
    shrink = lax.rsqrt(largest)
    a_ref[...] = a_ref[...] * shrink * shrink
    return shrink, largest * shrink


def eliminate(a_ref, factor_ref, buffer_ref, first, last):
    size = a_ref.shape[0]
    for base in range(first, last, PANEL):
        factor_panel(a_ref, factor_ref, buffer_ref, base, PANEL, size)
        trailing(a_ref, base, PANEL, size)


def split(value):
    high = value.astype(jnp.bfloat16)
    return high, (value - high.astype(jnp.float32)).astype(jnp.bfloat16)


def product(left, right, left_dim, right_dim):
    dims = (((left_dim,), (right_dim,)), ((), ()))
    dot = lambda a, b: lax.dot_general(a, b, dims, preferred_element_type=jnp.float32)
    return dot(left[0], right[0]) + (dot(left[0], right[1]) + dot(left[1], right[0]))


def core_bit():
    return lax.rem(lax.axis_index("wide"), 2)


def own_block():
    wide, narrow = lax.axis_index("wide"), lax.axis_index("narrow")
    plane = lax.rem(narrow, 2) + 2 * lax.rem(wide // 2, 2)
    return 16 * lax.rem(wide, 2) + 4 * plane + lax.rem(wide // 4, 4)


def rows_of(block, height):
    return pl.ds(pl.multiple_of(block * height, GROUP), height)


def local_kernel(features_hbm, sketch_hbm, sampled_ref, keep_ref, send_ref, gram_keep_ref, gram_send_ref, features_ref, sketch_ref, high_ref, low_ref, flip_high_ref, flip_low_ref, cross_ref, packed_ref, sems):
    rows, depth = features_ref.shape
    rank = sketch_ref.shape[1]
    chunks = rows // BLOCK
    copies = [pltpu.make_async_copy(sketch_hbm, sketch_ref, sems.at[chunks])]
    for at in range(chunks):
        span = pl.ds(at * BLOCK, BLOCK)
        copies.append(pltpu.make_async_copy(features_hbm.at[span, :], features_ref.at[span, :], sems.at[at]))
    for copy in copies:
        copy.start()
    copies[0].wait()
    sketch = split(sketch_ref[...])
    gram = None
    for at in range(chunks):
        span = slice(at * BLOCK, (at + 1) * BLOCK)
        copies[1 + at].wait()
        features = split(features_ref[span, :])
        high_ref[span, :], low_ref[span, :] = features
        sampled = product(features, sketch, 1, 0)
        sampled_ref[span, :] = sampled
        flipped = split(sampled.T)
        flip_high_ref[:, span], flip_low_ref[:, span] = flipped
        term = product(flipped, split(sampled), 1, 0)
        gram = term if gram is None else gram + term
    packed_ref[:LANES, :] = gram[:LANES, :LANES]
    packed_ref[LANES:2 * LANES, :] = gram[:LANES, LANES:]
    packed_ref[2 * LANES:, :] = gram[LANES:, LANES:]
    half = packed_ref.shape[0] // 2
    core = core_bit()
    gram_keep_ref[...] = packed_ref[rows_of(core, half), :]
    gram_send_ref[...] = packed_ref[rows_of(1 - core, half), :]
    flipped = flip_high_ref[...], flip_low_ref[...]
    own = own_block()
    height = rank // BLOCKS
    for left in range(0, depth, BLOCK):
        span = slice(left, left + BLOCK)
        cross_ref[:, span] = product(flipped, (high_ref[:, span], low_ref[:, span]), 1, 0)
    for at in range(BLOCKS):
        block = cross_ref[rows_of(at ^ own, height), :]
        if at < BLOCKS // 2:
            keep_ref[at * height:(at + 1) * height, :] = block
        else:
            rest = at - BLOCKS // 2
            send_ref[rest * height:(rest + 1) * height, :] = block


def f32(*shape):
    return jax.ShapeDtypeStruct(shape, jnp.float32)


def local_terms(features, sketch):
    rows, depth = features.shape
    rank = sketch.shape[1]
    packed = 3 * LANES
    hbm = pl.BlockSpec(memory_space=pltpu.HBM)
    return pl.pallas_call(
        local_kernel,
        out_shape=(f32(rows, rank), f32(rank // 2, depth), f32(rank // 2, depth), f32(packed // 2, LANES), f32(packed // 2, LANES)),
        in_specs=[hbm, hbm],
        out_specs=(VMEM,) * 5,
        scratch_shapes=[
            pltpu.VMEM((rows, depth), jnp.float32), pltpu.VMEM((depth, rank), jnp.float32),
            pltpu.VMEM((rows, depth), jnp.bfloat16), pltpu.VMEM((rows, depth), jnp.bfloat16),
            pltpu.VMEM((rank, rows), jnp.bfloat16), pltpu.VMEM((rank, rows), jnp.bfloat16),
            pltpu.VMEM((rank, depth), jnp.float32), pltpu.VMEM((packed, LANES), jnp.float32),
            pltpu.SemaphoreType.DMA((rows // BLOCK + 1,)),
        ],
        compiler_params=pltpu.CompilerParams(vmem_limit_bytes=51 * 2**20),
        cost_estimate=pl.CostEstimate(flops=4 * 10**9, bytes_accessed=8 * 2**20, transcendentals=0),
        name="local_terms",
    )(features, sketch)


def call(kernel, name, outs, *operands, after=(), scratch=(), flops=10**6):
    return pl.pallas_call(
        lambda *refs: kernel(*refs[:len(operands)], *refs[len(operands) + len(after):]),
        out_shape=outs,
        in_specs=[VMEM] * len(operands) + [pl.BlockSpec(memory_space=pl.ANY)] * len(after),
        out_specs=jax.tree.map(lambda _: VMEM, outs),
        scratch_shapes=list(scratch),
        compiler_params=pltpu.CompilerParams(vmem_limit_bytes=16 * 2**20),
        cost_estimate=pl.CostEstimate(flops=flops, bytes_accessed=10**6, transcendentals=0),
        name=name,
    )(*operands, *after)


def sum_kernel(masks, *refs):
    cross, outs = refs[:len(masks)], refs[len(masks):]
    at = 0
    for out_ref in outs:
        for top in range(0, out_ref.shape[0], GROUP):
            blocks = [ref[(at ^ mask) * GROUP:(at ^ mask) * GROUP + GROUP, :] for ref, mask in zip(cross, masks)]
            out_ref[top:top + GROUP, :] = sum(blocks)
            at += 1


def sums(cross, pieces=1, masks=None, after=()):
    height, depth = cross[0].shape
    masks = masks or (0,) * len(cross)
    outs = (f32(height // pieces, depth),) * pieces
    return call(lambda *refs: sum_kernel(masks, *refs), "sums", outs, *cross, after=after)


def add_kernel(left_ref, right_ref, out_ref):
    out_ref[...] = left_ref[...] + right_ref[...]


def add(left, right, after):
    return call(add_kernel, "add", f32(*left.shape), left, right, after=after)


def first_part_kernel(keep_ref, other_ref, a_ref, factor_ref, norm_ref, packed_ref, buffer_ref):
    half = keep_ref.shape[0]
    core = core_bit()
    packed_ref[rows_of(core, half), :] = keep_ref[...]
    packed_ref[rows_of(1 - core, half), :] = other_ref[...]
    a_ref[:LANES, :LANES] = packed_ref[:LANES, :]
    a_ref[:LANES, LANES:] = packed_ref[LANES:2 * LANES, :]
    a_ref[LANES:, :LANES] = jnp.zeros((LANES, LANES), jnp.float32)
    a_ref[LANES:, LANES:] = packed_ref[2 * LANES:, :]
    shrink, grow = normalize(a_ref)
    norm_ref[:GROUP, :] = jnp.broadcast_to(shrink, (GROUP, LANES))
    norm_ref[GROUP:, :] = jnp.broadcast_to(grow, (GROUP, LANES))
    eliminate(a_ref, factor_ref, buffer_ref, 0, PANEL)


def middle_part_kernel(first, from_ref, upper_ref, a_ref, factor_ref, buffer_ref):
    a_ref[...] = from_ref[...]
    factor_ref[:first, :] = upper_ref[:first, :]
    eliminate(a_ref, factor_ref, buffer_ref, first, first + PANEL)


def last_part_kernel(scale, first, from_ref, upper_ref, norm_ref, inverse_ref, flipped_ref, factor_ref, a_ref, buffer_ref):
    size = a_ref.shape[0]
    a_ref[...] = from_ref[...]
    eliminate(a_ref, factor_ref, buffer_ref, first, size)
    shrink, grow = norm_ref[:1, :1], norm_ref[GROUP:GROUP + 1, :1] / scale
    factor_ref[:first, :] = upper_ref[:first, :] * grow
    factor_ref[first:, :] = factor_ref[first:, :] * grow
    col = lax.broadcasted_iota(jnp.int32, (size, size), 1)
    row = lax.broadcasted_iota(jnp.int32, (size, size), 0)
    inverse = jnp.where(col <= row, a_ref[...], 0.0) * shrink
    inverse_ref[...] = inverse
    flipped_ref[...] = inverse.T * scale


def buffers(*shapes):
    return [pltpu.VMEM(shape, jnp.float32) for shape in (*shapes, (40 * GROUP, LANES))]


def first_part(keep, other, size, after):
    outs = f32(size, size), f32(size, size), f32(2 * GROUP, LANES)
    return call(first_part_kernel, "first_part", outs, keep, other, after=after, scratch=buffers((3 * LANES, LANES)), flops=10**6)


def middle_part(state, size, first, after):
    kernel = lambda *refs: middle_part_kernel(first, *refs)
    return call(kernel, "middle_part", (f32(size, size),) * 2, *state, after=after, scratch=buffers(), flops=3 * 10**9)


def last_part(state, size, scale, first, after):
    kernel = lambda *refs: last_part_kernel(scale, first, *refs)
    return call(kernel, "last_part", (f32(size, size),) * 3, *state, after=after, scratch=buffers((size, size)), flops=3 * 10**9)


def basis_kernel(sampled_ref, flipped_ref, basis_ref):
    flipped = split(flipped_ref[...])
    for top in range(0, sampled_ref.shape[0], BLOCK):
        span = slice(top, top + BLOCK)
        basis_ref[span, :] = product(split(sampled_ref[span, :]), flipped, 1, 0)


def basis_of(sampled, flipped):
    return pl.pallas_call(
        basis_kernel,
        out_shape=f32(*sampled.shape),
        in_specs=[VMEM] * 2,
        out_specs=VMEM,
        compiler_params=pltpu.CompilerParams(vmem_limit_bytes=16 * 2**20),
        cost_estimate=pl.CostEstimate(flops=2 * 10**9, bytes_accessed=2 * 2**20, transcendentals=0),
        name="basis",
    )(sampled, flipped)


def project_kernel(inverse_ref, *refs):
    *pieces, projection_ref, cross_ref = refs
    own = own_block()
    height = cross_ref.shape[0] // BLOCKS
    at = 0
    for piece in pieces:
        for top in range(0, piece.shape[0], height):
            cross_ref[rows_of(at ^ own, height), :] = piece[top:top + height, :]
            at += 1
    inverse = split(inverse_ref[...])
    for left in range(0, cross_ref.shape[1], BLOCK):
        span = slice(left, left + BLOCK)
        projection_ref[:, span] = product(inverse, split(cross_ref[:, span]), 1, 0)


def project(inverse, pieces):
    rank = inverse.shape[0]
    depth = pieces[0].shape[1]
    return pl.pallas_call(
        project_kernel,
        out_shape=jax.ShapeDtypeStruct((rank, depth), jnp.float32),
        in_specs=[VMEM] * (1 + len(pieces)),
        out_specs=VMEM,
        scratch_shapes=[pltpu.VMEM((rank, depth), jnp.float32)],
        compiler_params=pltpu.CompilerParams(vmem_limit_bytes=16 * 2**20),
        cost_estimate=pl.CostEstimate(flops=4 * 10**8, bytes_accessed=2 * 2**20, transcendentals=0),
        name="project",
    )(inverse, *pieces)


def send(value, wide, narrow):
    mask = wide * lax.axis_size("narrow") + narrow
    pairs = [(source, source ^ mask) for source in range(lax.axis_size(AXES))]
    return lax.ppermute(value, AXES, pairs)


CORE = (1, 0)
PLANE = [(0, 1), (2, 0), (2, 1)]
NEAR, FAR = (4, 0), (8, 0)


def spare_bits():
    wide = [(2**bit, 0) for bit in range(4, lax.axis_size("wide").bit_length() - 1)]
    narrow = [(0, 2**bit) for bit in range(1, lax.axis_size("narrow").bit_length() - 1)]
    return wide + narrow


def spread(parts, masks):
    first, *rest = parts
    return [first] + [send(part, *mask) for part, mask in zip(rest, masks)]


def per_device(features, sketch):
    scale = (features.shape[0] * lax.axis_size(AXES)) ** 0.5
    size = sketch.shape[1]
    sampled, keep, other, gram, gram_other = local_terms(features, sketch)
    gram_other = send(gram_other, *CORE)
    parts = sums([keep, send(other, *CORE)], 4, after=(gram_other,))
    cross = spread(parts, PLANE)
    gram = add(gram, gram_other, parts[-1:])
    gram = gram + send(gram, *NEAR)
    gram_other = send(gram, *FAR)
    (line,) = sums(cross, after=(gram_other,))
    gram = add(gram, gram_other, (line,))
    gram_other = send(gram, *PLANE[0])
    (line,) = sums([line, send(line, *NEAR)], masks=(0, 1), after=(gram_other,))
    gram = add(gram, gram_other, (line,))
    gram = gram + send(gram, *PLANE[1])
    for mask in spare_bits():
        line = line + send(line, *mask)
        gram = gram + send(gram, *mask)
    *state, norm = first_part(gram, send(gram, *CORE), size, ())
    (line,) = sums([line, send(line, *FAR)], masks=(0, 2), after=state[:1])
    plane = [line] + [send(line, *mask) for mask in PLANE]
    state = middle_part(state, size, PANEL, (line,))
    state = middle_part(state, size, 2 * PANEL, ())
    inverse, flipped, factor = last_part((*state, norm), size, scale, 3 * PANEL, ())
    cross = plane + [send(part, *CORE) for part in plane]
    return (basis_of(sampled, flipped), factor, project(inverse, cross))


def solution(mesh):
    rows = P(AXES, None)
    return jax.shard_map(
        per_device, mesh=mesh, in_specs=(rows, P()), out_specs=(rows, P(), P()), check_vma=False
    )
```

```python
import jax, jax.numpy as jnp
from jax import lax
from jax.experimental import pallas as pl
from jax.experimental.pallas import tpu as pltpu
from jax.sharding import PartitionSpec as P

GROUP = 8
LANES = 128
PANEL = 64
BLOCK = 256
BLOCKS = 32
AXES = ("wide", "narrow")
VMEM = pl.BlockSpec(memory_space=pltpu.VMEM)


def factor_panel(a_ref, factor_ref, buffer_ref, base, height, size):
    lane = lax.broadcasted_iota(jnp.int32, (GROUP, LANES), 1)
    sub = lax.broadcasted_iota(jnp.int32, (GROUP, LANES), 0)
    tiles = size // LANES
    spread = lambda value: jnp.broadcast_to(value, (GROUP, LANES))

    def spread_row(slot, k):
        return spread(buffer_ref[slot * GROUP + k:slot * GROUP + k + 1, :])

    def keep(value, slot):
        buffer_ref[slot * GROUP:(slot + 1) * GROUP, :] = value

    rows = {}
    for g in range(base, base + height, GROUP):
        for t in range(tiles):
            rows[g, t] = a_ref[g:g + GROUP, t * LANES:(t + 1) * LANES]
    for top in range(base, base + height, GROUP):
        groups = list(range(top, base + height, GROUP))
        home = top // LANES
        offset = top - home * LANES
        inside = (lane >= offset) & (lane < offset + GROUP)
        diag = rows[top, home]
        bank = top // GROUP % 2 * 20
        col, one = {}, {}
        for j in range(GROUP):
            for g in groups:
                col[g, j] = spread(rows[g, home][:, offset + j:offset + j + 1])
            keep(col[top, j], bank + j)
            for k in range(j, GROUP):
                one[k, j] = spread_row(bank + j, k)
        for g in groups:
            fresh = jnp.where(lane == sub + offset, 1.0, 0.0) if g == top else 0.0
            rows[g, home] = jnp.where(inside, fresh, rows[g, home])
        for j in range(0, GROUP, 2):
            a, b, c = one[j, j], one[j + 1, j], one[j + 1, j + 1]
            first = lax.rsqrt(a)
            both = first * lax.rsqrt(a * c - b * b)
            cross = b * first
            second = a * both
            low = {}
            for k in range(j + 2, GROUP):
                low[k] = one[k, j] * first, (a * one[k, j + 1] - b * one[k, j]) * both
            for k in range(j + 2, GROUP):
                for m in range(k, GROUP):
                    one[m, k] = one[m, k] - (low[m][0] * low[k][0] + low[m][1] * low[k][1])
            scaled = {}
            for g in groups:
                scaled[g] = col[g, j] * first, (a * col[g, j + 1] - b * col[g, j]) * both
            for k in range(j + 2, GROUP):
                for g in groups:
                    col[g, k] = col[g, k] - (scaled[g][0] * low[k][0] + scaled[g][1] * low[k][1])
            below = [jnp.where(sub > j + 1, part, 0.0) for part in scaled[top]]

            def pivots(value, slot):
                slot = bank + GROUP + 3 * (j // 2) + slot
                keep(value, slot)
                upper = spread_row(slot, j) * first
                return upper, (spread_row(slot, j + 1) - cross * upper) * second

            def replaced(value, upper, lower):
                value = value - (below[0] * upper + below[1] * lower)
                return jnp.where(sub == j, upper, jnp.where(sub == j + 1, lower, value))

            diag = replaced(diag, *pivots(diag, 2))
            for t in range(tiles):
                upper, lower = pivots(rows[top, t], t)
                rows[top, t] = replaced(rows[top, t], upper, lower)
                for g in groups[1:]:
                    rows[g, t] = rows[g, t] - (scaled[g][0] * upper + scaled[g][1] * lower)
        for t in range(tiles):
            span = slice(t * LANES, (t + 1) * LANES)
            a_ref[top:top + GROUP, span] = rows[top, t]
            if t < home:
                factor_ref[top:top + GROUP, span] = jnp.zeros((GROUP, LANES), jnp.float32)
            elif t == home:
                factor_ref[top:top + GROUP, span] = jnp.where(lane >= sub + offset, diag, 0.0)
            else:
                factor_ref[top:top + GROUP, span] = rows[top, t]


def trailing(a_ref, base, height, size):
    end = base + height
    if end == size:
        return
    panel = a_ref[base:end, :]
    col = lax.broadcasted_iota(jnp.int32, (height, size), 1)
    row = lax.broadcasted_iota(jnp.int32, (height, size), 0) + base
    right = jnp.where((col <= row) | (col >= end), panel, 0.0)
    left = panel[:, end:]
    update = lax.dot_general(left, right, (((0,), (0,)), ((), ())), precision=lax.Precision.HIGHEST, preferred_element_type=jnp.float32)
    rest = a_ref[end:, :]
    at = lax.broadcasted_iota(jnp.int32, (size - end, size), 1)
    a_ref[end:, :] = jnp.where((at >= base) & (at < end), 0.0, rest) - update


def normalize(a_ref):
    size = a_ref.shape[0]
    col = lax.broadcasted_iota(jnp.int32, (size, size), 1)
    row = lax.broadcasted_iota(jnp.int32, (size, size), 0)
    largest = jnp.max(jnp.where(col == row, a_ref[...], 0.0), axis=(0, 1), keepdims=True)
    shrink = lax.rsqrt(largest)
    a_ref[...] = a_ref[...] * shrink * shrink
    return shrink, largest * shrink


def eliminate(a_ref, factor_ref, buffer_ref, first, last):
    size = a_ref.shape[0]
    for base in range(first, last, PANEL):
        factor_panel(a_ref, factor_ref, buffer_ref, base, PANEL, size)
        trailing(a_ref, base, PANEL, size)


def split(value):
    high = value.astype(jnp.bfloat16)
    return high, (value - high.astype(jnp.float32)).astype(jnp.bfloat16)


def product(left, right, left_dim, right_dim):
    dims = (((left_dim,), (right_dim,)), ((), ()))
    dot = lambda a, b: lax.dot_general(a, b, dims, preferred_element_type=jnp.float32)
    return dot(left[0], right[0]) + (dot(left[0], right[1]) + dot(left[1], right[0]))


def core_bit():
    return lax.rem(lax.axis_index("wide"), 2)


def own_block():
    wide, narrow = lax.axis_index("wide"), lax.axis_index("narrow")
    plane = lax.rem(narrow, 2) + 2 * lax.rem(wide // 2, 2)
    return 16 * lax.rem(wide, 2) + 4 * plane + lax.rem(wide // 4, 4)


def rows_of(block, height):
    return pl.ds(pl.multiple_of(block * height, GROUP), height)


def local_kernel(features_hbm, sketch_hbm, sampled_ref, keep_ref, send_ref, gram_keep_ref, gram_send_ref, features_ref, sketch_ref, pair_ref, high_ref, low_ref, flip_high_ref, flip_low_ref, cross_ref, packed_ref, sems):
    rows, depth = features_ref.shape
    rank = sketch_ref.shape[1]
    chunks = rows // BLOCK
    copies = [pltpu.make_async_copy(sketch_hbm, sketch_ref, sems.at[chunks])]
    for at in range(chunks):
        span = pl.ds(at * BLOCK, BLOCK)
        copies.append(pltpu.make_async_copy(features_hbm.at[span, :], features_ref.at[span, :], sems.at[at]))
    for copy in copies:
        copy.start()
    copies[0].wait()
    pair_ref[:, :rank], pair_ref[:, rank:] = split(sketch_ref[...])
    gram = None
    for at in range(chunks):
        span = slice(at * BLOCK, (at + 1) * BLOCK)
        copies[1 + at].wait()
        features = split(features_ref[span, :])
        high_ref[span, :], low_ref[span, :] = features
        both = lax.dot(features[0], pair_ref[...], preferred_element_type=jnp.float32)
        sampled = both[:, :rank] + (both[:, rank:] + lax.dot(features[1], pair_ref[:, :rank], preferred_element_type=jnp.float32))
        sampled_ref[span, :] = sampled
        flipped = split(sampled.T)
        flip_high_ref[:, span], flip_low_ref[:, span] = flipped
        term = product(flipped, split(sampled), 1, 0)
        gram = term if gram is None else gram + term
    packed_ref[:LANES, :] = gram[:LANES, :LANES]
    packed_ref[LANES:2 * LANES, :] = gram[:LANES, LANES:]
    packed_ref[2 * LANES:, :] = gram[LANES:, LANES:]
    half = packed_ref.shape[0] // 2
    core = core_bit()
    gram_keep_ref[...] = packed_ref[rows_of(core, half), :]
    gram_send_ref[...] = packed_ref[rows_of(1 - core, half), :]
    flipped = flip_high_ref[...], flip_low_ref[...]
    own = own_block()
    height = rank // BLOCKS
    for left in range(0, depth, BLOCK):
        span = slice(left, left + BLOCK)
        cross_ref[:, span] = product(flipped, (high_ref[:, span], low_ref[:, span]), 1, 0)
    for at in range(BLOCKS):
        block = cross_ref[rows_of(at ^ own, height), :]
        if at < BLOCKS // 2:
            keep_ref[at * height:(at + 1) * height, :] = block
        else:
            rest = at - BLOCKS // 2
            send_ref[rest * height:(rest + 1) * height, :] = block


def f32(*shape):
    return jax.ShapeDtypeStruct(shape, jnp.float32)


def local_terms(features, sketch):
    rows, depth = features.shape
    rank = sketch.shape[1]
    packed = 3 * LANES
    hbm = pl.BlockSpec(memory_space=pltpu.HBM)
    return pl.pallas_call(
        local_kernel,
        out_shape=(f32(rows, rank), f32(rank // 2, depth), f32(rank // 2, depth), f32(packed // 2, LANES), f32(packed // 2, LANES)),
        in_specs=[hbm, hbm],
        out_specs=(VMEM,) * 5,
        scratch_shapes=[
            pltpu.VMEM((rows, depth), jnp.float32), pltpu.VMEM((depth, rank), jnp.float32),
            pltpu.VMEM((depth, 2 * rank), jnp.bfloat16),
            pltpu.VMEM((rows, depth), jnp.bfloat16), pltpu.VMEM((rows, depth), jnp.bfloat16),
            pltpu.VMEM((rank, rows), jnp.bfloat16), pltpu.VMEM((rank, rows), jnp.bfloat16),
            pltpu.VMEM((rank, depth), jnp.float32), pltpu.VMEM((packed, LANES), jnp.float32),
            pltpu.SemaphoreType.DMA((rows // BLOCK + 1,)),
        ],
        compiler_params=pltpu.CompilerParams(vmem_limit_bytes=51 * 2**20),
        cost_estimate=pl.CostEstimate(flops=4 * 10**9, bytes_accessed=8 * 2**20, transcendentals=0),
        name="local_terms",
    )(features, sketch)


def call(kernel, name, outs, *operands, after=(), scratch=(), flops=10**6):
    return pl.pallas_call(
        lambda *refs: kernel(*refs[:len(operands)], *refs[len(operands) + len(after):]),
        out_shape=outs,
        in_specs=[VMEM] * len(operands) + [pl.BlockSpec(memory_space=pl.ANY)] * len(after),
        out_specs=jax.tree.map(lambda _: VMEM, outs),
        scratch_shapes=list(scratch),
        compiler_params=pltpu.CompilerParams(vmem_limit_bytes=16 * 2**20),
        cost_estimate=pl.CostEstimate(flops=flops, bytes_accessed=10**6, transcendentals=0),
        name=name,
    )(*operands, *after)


def sum_kernel(masks, *refs):
    cross, outs = refs[:len(masks)], refs[len(masks):]
    at = 0
    for out_ref in outs:
        for top in range(0, out_ref.shape[0], GROUP):
            blocks = [ref[(at ^ mask) * GROUP:(at ^ mask) * GROUP + GROUP, :] for ref, mask in zip(cross, masks)]
            out_ref[top:top + GROUP, :] = sum(blocks)
            at += 1


def sums(cross, pieces=1, masks=None, after=()):
    height, depth = cross[0].shape
    masks = masks or (0,) * len(cross)
    outs = (f32(height // pieces, depth),) * pieces
    return call(lambda *refs: sum_kernel(masks, *refs), "sums", outs, *cross, after=after)


def add_kernel(left_ref, right_ref, out_ref):
    out_ref[...] = left_ref[...] + right_ref[...]


def add(left, right, after):
    return call(add_kernel, "add", f32(*left.shape), left, right, after=after)


def first_part_kernel(keep_ref, other_ref, a_ref, factor_ref, norm_ref, packed_ref, buffer_ref):
    half = keep_ref.shape[0]
    core = core_bit()
    packed_ref[rows_of(core, half), :] = keep_ref[...]
    packed_ref[rows_of(1 - core, half), :] = other_ref[...]
    a_ref[:LANES, :LANES] = packed_ref[:LANES, :]
    a_ref[:LANES, LANES:] = packed_ref[LANES:2 * LANES, :]
    a_ref[LANES:, :LANES] = jnp.zeros((LANES, LANES), jnp.float32)
    a_ref[LANES:, LANES:] = packed_ref[2 * LANES:, :]
    shrink, grow = normalize(a_ref)
    norm_ref[:GROUP, :] = jnp.broadcast_to(shrink, (GROUP, LANES))
    norm_ref[GROUP:, :] = jnp.broadcast_to(grow, (GROUP, LANES))
    eliminate(a_ref, factor_ref, buffer_ref, 0, PANEL)


def middle_part_kernel(first, from_ref, upper_ref, a_ref, factor_ref, buffer_ref):
    a_ref[...] = from_ref[...]
    factor_ref[:first, :] = upper_ref[:first, :]
    eliminate(a_ref, factor_ref, buffer_ref, first, first + PANEL)


def last_part_kernel(scale, first, from_ref, upper_ref, norm_ref, inverse_ref, flipped_ref, factor_ref, a_ref, buffer_ref):
    size = a_ref.shape[0]
    a_ref[...] = from_ref[...]
    eliminate(a_ref, factor_ref, buffer_ref, first, size)
    shrink, grow = norm_ref[:1, :1], norm_ref[GROUP:GROUP + 1, :1] / scale
    factor_ref[:first, :] = upper_ref[:first, :] * grow
    factor_ref[first:, :] = factor_ref[first:, :] * grow
    col = lax.broadcasted_iota(jnp.int32, (size, size), 1)
    row = lax.broadcasted_iota(jnp.int32, (size, size), 0)
    inverse = jnp.where(col <= row, a_ref[...], 0.0) * shrink
    inverse_ref[...] = inverse
    flipped_ref[...] = inverse.T * scale


def buffers(*shapes):
    return [pltpu.VMEM(shape, jnp.float32) for shape in (*shapes, (40 * GROUP, LANES))]


def first_part(keep, other, size, after):
    outs = f32(size, size), f32(size, size), f32(2 * GROUP, LANES)
    return call(first_part_kernel, "first_part", outs, keep, other, after=after, scratch=buffers((3 * LANES, LANES)), flops=10**6)


def middle_part(state, size, first, after):
    kernel = lambda *refs: middle_part_kernel(first, *refs)
    return call(kernel, "middle_part", (f32(size, size),) * 2, *state, after=after, scratch=buffers(), flops=3 * 10**9)


def last_part(state, size, scale, first, after):
    kernel = lambda *refs: last_part_kernel(scale, first, *refs)
    return call(kernel, "last_part", (f32(size, size),) * 3, *state, after=after, scratch=buffers((size, size)), flops=3 * 10**9)


def basis_kernel(sampled_ref, flipped_ref, basis_ref):
    flipped = split(flipped_ref[...])
    for top in range(0, sampled_ref.shape[0], BLOCK):
        span = slice(top, top + BLOCK)
        basis_ref[span, :] = product(split(sampled_ref[span, :]), flipped, 1, 0)


def basis_of(sampled, flipped):
    return pl.pallas_call(
        basis_kernel,
        out_shape=f32(*sampled.shape),
        in_specs=[VMEM] * 2,
        out_specs=VMEM,
        compiler_params=pltpu.CompilerParams(vmem_limit_bytes=16 * 2**20),
        cost_estimate=pl.CostEstimate(flops=2 * 10**9, bytes_accessed=2 * 2**20, transcendentals=0),
        name="basis",
    )(sampled, flipped)


def project_kernel(inverse_ref, *refs):
    *pieces, projection_ref, cross_ref = refs
    own = own_block()
    height = cross_ref.shape[0] // BLOCKS
    at = 0
    for piece in pieces:
        for top in range(0, piece.shape[0], height):
            cross_ref[rows_of(at ^ own, height), :] = piece[top:top + height, :]
            at += 1
    inverse = split(inverse_ref[...])
    for left in range(0, cross_ref.shape[1], BLOCK):
        span = slice(left, left + BLOCK)
        projection_ref[:, span] = product(inverse, split(cross_ref[:, span]), 1, 0)


def project(inverse, pieces):
    rank = inverse.shape[0]
    depth = pieces[0].shape[1]
    return pl.pallas_call(
        project_kernel,
        out_shape=jax.ShapeDtypeStruct((rank, depth), jnp.float32),
        in_specs=[VMEM] * (1 + len(pieces)),
        out_specs=VMEM,
        scratch_shapes=[pltpu.VMEM((rank, depth), jnp.float32)],
        compiler_params=pltpu.CompilerParams(vmem_limit_bytes=16 * 2**20),
        cost_estimate=pl.CostEstimate(flops=4 * 10**8, bytes_accessed=2 * 2**20, transcendentals=0),
        name="project",
    )(inverse, *pieces)


def send(value, wide, narrow):
    mask = wide * lax.axis_size("narrow") + narrow
    pairs = [(source, source ^ mask) for source in range(lax.axis_size(AXES))]
    return lax.ppermute(value, AXES, pairs)


CORE = (1, 0)
PLANE = [(0, 1), (2, 0), (2, 1)]
NEAR, FAR = (4, 0), (8, 0)


def spare_bits():
    wide = [(2**bit, 0) for bit in range(4, lax.axis_size("wide").bit_length() - 1)]
    narrow = [(0, 2**bit) for bit in range(1, lax.axis_size("narrow").bit_length() - 1)]
    return wide + narrow


def spread(parts, masks):
    first, *rest = parts
    return [first] + [send(part, *mask) for part, mask in zip(rest, masks)]


def per_device(features, sketch):
    scale = (features.shape[0] * lax.axis_size(AXES)) ** 0.5
    size = sketch.shape[1]
    sampled, keep, other, gram, gram_other = local_terms(features, sketch)
    gram_other = send(gram_other, *CORE)
    parts = sums([keep, send(other, *CORE)], 4, after=(gram_other,))
    cross = spread(parts, PLANE)
    gram = add(gram, gram_other, parts[-1:])
    gram = gram + send(gram, *NEAR)
    gram_other = send(gram, *FAR)
    (line,) = sums(cross)
    gram = add(gram, gram_other, (line,))
    gram_other = send(gram, *PLANE[0])
    (line,) = sums([line, send(line, *NEAR)], masks=(0, 1))
    gram = add(gram, gram_other, (line,))
    gram = gram + send(gram, *PLANE[1])
    for mask in spare_bits():
        line = line + send(line, *mask)
        gram = gram + send(gram, *mask)
    *state, norm = first_part(gram, send(gram, *CORE), size, ())
    (line,) = sums([line, send(line, *FAR)], masks=(0, 2), after=state[:1])
    plane = [line] + [send(line, *mask) for mask in PLANE]
    state = middle_part(state, size, PANEL, (line,))
    state = middle_part(state, size, 2 * PANEL, ())
    inverse, flipped, factor = last_part((*state, norm), size, scale, 3 * PANEL, ())
    cross = plane + [send(part, *CORE) for part in plane]
    return (basis_of(sampled, flipped), factor, project(inverse, cross))


def solution(mesh):
    rows = P(AXES, None)
    return jax.shard_map(
        per_device, mesh=mesh, in_specs=(rows, P()), out_specs=(rows, P(), P()), check_vma=False
    )
```

```python
import jax, jax.numpy as jnp
from jax import lax
from jax.experimental import pallas as pl
from jax.experimental.pallas import tpu as pltpu
from jax.sharding import PartitionSpec as P

GROUP = 8
LANES = 128
PANEL = 64
BLOCK = 256
BLOCKS = 32
AXES = ("wide", "narrow")
VMEM = pl.BlockSpec(memory_space=pltpu.VMEM)


def factor_panel(a_ref, factor_ref, buffer_ref, base, height, size):
    lane = lax.broadcasted_iota(jnp.int32, (GROUP, LANES), 1)
    sub = lax.broadcasted_iota(jnp.int32, (GROUP, LANES), 0)
    tiles = size // LANES
    spread = lambda value: jnp.broadcast_to(value, (GROUP, LANES))

    def spread_row(slot, k):
        return spread(buffer_ref[slot * GROUP + k:slot * GROUP + k + 1, :])

    def keep(value, slot):
        buffer_ref[slot * GROUP:(slot + 1) * GROUP, :] = value

    rows = {}
    for g in range(base, base + height, GROUP):
        for t in range(tiles):
            rows[g, t] = a_ref[g:g + GROUP, t * LANES:(t + 1) * LANES]
    for top in range(base, base + height, GROUP):
        groups = list(range(top, base + height, GROUP))
        home = top // LANES
        offset = top - home * LANES
        inside = (lane >= offset) & (lane < offset + GROUP)
        diag = rows[top, home]
        bank = top // GROUP % 2 * 20
        col, one = {}, {}
        for j in range(GROUP):
            for g in groups:
                col[g, j] = spread(rows[g, home][:, offset + j:offset + j + 1])
            keep(col[top, j], bank + j)
            for k in range(j, GROUP):
                one[k, j] = spread_row(bank + j, k)
        for g in groups:
            fresh = jnp.where(lane == sub + offset, 1.0, 0.0) if g == top else 0.0
            rows[g, home] = jnp.where(inside, fresh, rows[g, home])
        for j in range(0, GROUP, 2):
            a, b, c = one[j, j], one[j + 1, j], one[j + 1, j + 1]
            first = lax.rsqrt(a)
            both = first * lax.rsqrt(a * c - b * b)
            cross = b * first
            second = a * both
            low = {}
            for k in range(j + 2, GROUP):
                low[k] = one[k, j] * first, (a * one[k, j + 1] - b * one[k, j]) * both
            for k in range(j + 2, GROUP):
                for m in range(k, GROUP):
                    one[m, k] = one[m, k] - (low[m][0] * low[k][0] + low[m][1] * low[k][1])
            scaled = {}
            for g in groups:
                scaled[g] = col[g, j] * first, (a * col[g, j + 1] - b * col[g, j]) * both
            for k in range(j + 2, GROUP):
                for g in groups:
                    col[g, k] = col[g, k] - (scaled[g][0] * low[k][0] + scaled[g][1] * low[k][1])
            below = [jnp.where(sub > j + 1, part, 0.0) for part in scaled[top]]

            def pivots(value, slot):
                slot = bank + GROUP + 3 * (j // 2) + slot
                keep(value, slot)
                upper = spread_row(slot, j) * first
                return upper, (spread_row(slot, j + 1) - cross * upper) * second

            def replaced(value, upper, lower):
                value = value - (below[0] * upper + below[1] * lower)
                return jnp.where(sub == j, upper, jnp.where(sub == j + 1, lower, value))

            diag = replaced(diag, *pivots(diag, 2))
            for t in range(tiles):
                upper, lower = pivots(rows[top, t], t)
                rows[top, t] = replaced(rows[top, t], upper, lower)
                for g in groups[1:]:
                    rows[g, t] = rows[g, t] - (scaled[g][0] * upper + scaled[g][1] * lower)
        for t in range(tiles):
            span = slice(t * LANES, (t + 1) * LANES)
            a_ref[top:top + GROUP, span] = rows[top, t]
            if t < home:
                factor_ref[top:top + GROUP, span] = jnp.zeros((GROUP, LANES), jnp.float32)
            elif t == home:
                factor_ref[top:top + GROUP, span] = jnp.where(lane >= sub + offset, diag, 0.0)
            else:
                factor_ref[top:top + GROUP, span] = rows[top, t]


def trailing(a_ref, base, height, size):
    end = base + height
    if end == size:
        return
    panel = a_ref[base:end, :]
    col = lax.broadcasted_iota(jnp.int32, (height, size), 1)
    row = lax.broadcasted_iota(jnp.int32, (height, size), 0) + base
    right = jnp.where((col <= row) | (col >= end), panel, 0.0)
    left = panel[:, end:]
    update = lax.dot_general(left, right, (((0,), (0,)), ((), ())), precision=lax.Precision.HIGHEST, preferred_element_type=jnp.float32)
    rest = a_ref[end:, :]
    at = lax.broadcasted_iota(jnp.int32, (size - end, size), 1)
    a_ref[end:, :] = jnp.where((at >= base) & (at < end), 0.0, rest) - update


def normalize(a_ref):
    size = a_ref.shape[0]
    col = lax.broadcasted_iota(jnp.int32, (size, size), 1)
    row = lax.broadcasted_iota(jnp.int32, (size, size), 0)
    largest = jnp.max(jnp.where(col == row, a_ref[...], 0.0), axis=(0, 1), keepdims=True)
    shrink = lax.rsqrt(largest)
    a_ref[...] = a_ref[...] * shrink * shrink
    return shrink, largest * shrink


def eliminate(a_ref, factor_ref, buffer_ref, first, last):
    size = a_ref.shape[0]
    for base in range(first, last, PANEL):
        factor_panel(a_ref, factor_ref, buffer_ref, base, PANEL, size)
        trailing(a_ref, base, PANEL, size)


def split(value):
    high = value.astype(jnp.bfloat16)
    return high, (value - high.astype(jnp.float32)).astype(jnp.bfloat16)


def product(left, right, left_dim, right_dim):
    dims = (((left_dim,), (right_dim,)), ((), ()))
    dot = lambda a, b: lax.dot_general(a, b, dims, preferred_element_type=jnp.float32)
    return dot(left[0], right[0]) + (dot(left[0], right[1]) + dot(left[1], right[0]))


def core_bit():
    return lax.rem(lax.axis_index("wide"), 2)


def own_block():
    wide, narrow = lax.axis_index("wide"), lax.axis_index("narrow")
    plane = lax.rem(narrow, 2) + 2 * lax.rem(wide // 2, 2)
    return 16 * lax.rem(wide, 2) + 4 * plane + lax.rem(wide // 4, 4)


def rows_of(block, height):
    return pl.ds(pl.multiple_of(block * height, GROUP), height)


def local_kernel(features_hbm, sketch_hbm, sampled_ref, keep_ref, send_ref, gram_keep_ref, gram_send_ref, features_ref, sketch_ref, pair_ref, high_ref, low_ref, flip_high_ref, flip_low_ref, cross_ref, packed_ref, sems):
    rows, depth = features_ref.shape
    rank = sketch_ref.shape[1]
    chunks = rows // BLOCK
    copies = [pltpu.make_async_copy(sketch_hbm, sketch_ref, sems.at[chunks])]
    for at in range(chunks):
        span = pl.ds(at * BLOCK, BLOCK)
        copies.append(pltpu.make_async_copy(features_hbm.at[span, :], features_ref.at[span, :], sems.at[at]))
    for copy in copies:
        copy.start()
    copies[0].wait()
    pair_ref[:, :rank], pair_ref[:, rank:] = split(sketch_ref[...])
    gram = None
    for at in range(chunks):
        span = slice(at * BLOCK, (at + 1) * BLOCK)
        copies[1 + at].wait()
        features = split(features_ref[span, :])
        high_ref[span, :], low_ref[span, :] = features
        both = lax.dot(features[0], pair_ref[...], preferred_element_type=jnp.float32)
        sampled = both[:, :rank] + (both[:, rank:] + lax.dot(features[1], pair_ref[:, :rank], preferred_element_type=jnp.float32))
        sampled_ref[span, :] = sampled
        flipped = split(sampled.T)
        flip_high_ref[:, span], flip_low_ref[:, span] = flipped
        term = product(flipped, split(sampled), 1, 0)
        gram = term if gram is None else gram + term
    packed_ref[:LANES, :] = gram[:LANES, :LANES]
    packed_ref[LANES:2 * LANES, :] = gram[:LANES, LANES:]
    packed_ref[2 * LANES:, :] = gram[LANES:, LANES:]
    half = packed_ref.shape[0] // 2
    core = core_bit()
    gram_keep_ref[...] = packed_ref[rows_of(core, half), :]
    gram_send_ref[...] = packed_ref[rows_of(1 - core, half), :]
    flipped = flip_high_ref[...], flip_low_ref[...]
    own = own_block()
    height = rank // BLOCKS
    for left in range(0, depth, BLOCK):
        span = slice(left, left + BLOCK)
        cross_ref[:, span] = product(flipped, (high_ref[:, span], low_ref[:, span]), 1, 0)
    for at in range(BLOCKS):
        block = cross_ref[rows_of(at ^ own, height), :]
        if at < BLOCKS // 2:
            keep_ref[at * height:(at + 1) * height, :] = block
        else:
            rest = at - BLOCKS // 2
            send_ref[rest * height:(rest + 1) * height, :] = block


def f32(*shape):
    return jax.ShapeDtypeStruct(shape, jnp.float32)


def local_terms(features, sketch):
    rows, depth = features.shape
    rank = sketch.shape[1]
    packed = 3 * LANES
    hbm = pl.BlockSpec(memory_space=pltpu.HBM)
    return pl.pallas_call(
        local_kernel,
        out_shape=(f32(rows, rank), f32(rank // 2, depth), f32(rank // 2, depth), f32(packed // 2, LANES), f32(packed // 2, LANES)),
        in_specs=[hbm, hbm],
        out_specs=(VMEM,) * 5,
        scratch_shapes=[
            pltpu.VMEM((rows, depth), jnp.float32), pltpu.VMEM((depth, rank), jnp.float32),
            pltpu.VMEM((depth, 2 * rank), jnp.bfloat16),
            pltpu.VMEM((rows, depth), jnp.bfloat16), pltpu.VMEM((rows, depth), jnp.bfloat16),
            pltpu.VMEM((rank, rows), jnp.bfloat16), pltpu.VMEM((rank, rows), jnp.bfloat16),
            pltpu.VMEM((rank, depth), jnp.float32), pltpu.VMEM((packed, LANES), jnp.float32),
            pltpu.SemaphoreType.DMA((rows // BLOCK + 1,)),
        ],
        compiler_params=pltpu.CompilerParams(vmem_limit_bytes=51 * 2**20),
        cost_estimate=pl.CostEstimate(flops=4 * 10**9, bytes_accessed=8 * 2**20, transcendentals=0),
        name="local_terms",
    )(features, sketch)


def call(kernel, name, outs, *operands, after=(), scratch=(), flops=10**6):
    return pl.pallas_call(
        lambda *refs: kernel(*refs[:len(operands)], *refs[len(operands) + len(after):]),
        out_shape=outs,
        in_specs=[VMEM] * len(operands) + [pl.BlockSpec(memory_space=pl.ANY)] * len(after),
        out_specs=jax.tree.map(lambda _: VMEM, outs),
        scratch_shapes=list(scratch),
        compiler_params=pltpu.CompilerParams(vmem_limit_bytes=16 * 2**20),
        cost_estimate=pl.CostEstimate(flops=flops, bytes_accessed=10**6, transcendentals=0),
        name=name,
    )(*operands, *after)


def sum_kernel(masks, *refs):
    cross, outs = refs[:len(masks)], refs[len(masks):]
    at = 0
    for out_ref in outs:
        for top in range(0, out_ref.shape[0], GROUP):
            blocks = [ref[(at ^ mask) * GROUP:(at ^ mask) * GROUP + GROUP, :] for ref, mask in zip(cross, masks)]
            out_ref[top:top + GROUP, :] = sum(blocks)
            at += 1


def sums(cross, pieces=1, masks=None, after=()):
    height, depth = cross[0].shape
    masks = masks or (0,) * len(cross)
    outs = (f32(height // pieces, depth),) * pieces
    return call(lambda *refs: sum_kernel(masks, *refs), "sums", outs, *cross, after=after)


def add_kernel(*refs):
    *terms, out_ref = refs
    out_ref[...] = sum(term[...] for term in terms)


def add(terms, after):
    return call(add_kernel, "add", f32(*terms[0].shape), *terms, after=after)


def first_part_kernel(keep_ref, other_ref, a_ref, factor_ref, norm_ref, packed_ref, buffer_ref):
    half = keep_ref.shape[0]
    core = core_bit()
    packed_ref[rows_of(core, half), :] = keep_ref[...]
    packed_ref[rows_of(1 - core, half), :] = other_ref[...]
    a_ref[:LANES, :LANES] = packed_ref[:LANES, :]
    a_ref[:LANES, LANES:] = packed_ref[LANES:2 * LANES, :]
    a_ref[LANES:, :LANES] = jnp.zeros((LANES, LANES), jnp.float32)
    a_ref[LANES:, LANES:] = packed_ref[2 * LANES:, :]
    shrink, grow = normalize(a_ref)
    norm_ref[:GROUP, :] = jnp.broadcast_to(shrink, (GROUP, LANES))
    norm_ref[GROUP:, :] = jnp.broadcast_to(grow, (GROUP, LANES))
    eliminate(a_ref, factor_ref, buffer_ref, 0, PANEL)


def last_part_kernel(scale, first, from_ref, upper_ref, norm_ref, inverse_ref, flipped_ref, factor_ref, a_ref, buffer_ref):
    size = a_ref.shape[0]
    a_ref[...] = from_ref[...]
    eliminate(a_ref, factor_ref, buffer_ref, first, size)
    shrink, grow = norm_ref[:1, :1], norm_ref[GROUP:GROUP + 1, :1] / scale
    factor_ref[:first, :] = upper_ref[:first, :] * grow
    factor_ref[first:, :] = factor_ref[first:, :] * grow
    col = lax.broadcasted_iota(jnp.int32, (size, size), 1)
    row = lax.broadcasted_iota(jnp.int32, (size, size), 0)
    inverse = jnp.where(col <= row, a_ref[...], 0.0) * shrink
    inverse_ref[...] = inverse
    flipped_ref[...] = inverse.T * scale


def buffers(*shapes):
    return [pltpu.VMEM(shape, jnp.float32) for shape in (*shapes, (40 * GROUP, LANES))]


def first_part(keep, other, size, after):
    outs = f32(size, size), f32(size, size), f32(2 * GROUP, LANES)
    return call(first_part_kernel, "first_part", outs, keep, other, after=after, scratch=buffers((3 * LANES, LANES)), flops=10**6)


def last_part(state, size, scale, first, after):
    kernel = lambda *refs: last_part_kernel(scale, first, *refs)
    return call(kernel, "last_part", (f32(size, size),) * 3, *state, after=after, scratch=buffers((size, size)), flops=3 * 10**9)


def copy_out(block_ref, out_hbm, span, sem):
    copy = pltpu.make_async_copy(block_ref.at[span], out_hbm.at[span], sem)
    copy.start()
    return copy


def basis_kernel(sampled_ref, flipped_ref, basis_hbm, basis_ref, sems):
    flipped = split(flipped_ref[...])
    copies = []
    for at in range(sampled_ref.shape[0] // BLOCK):
        span = slice(at * BLOCK, (at + 1) * BLOCK)
        basis_ref[span, :] = product(split(sampled_ref[span, :]), flipped, 1, 0)
        copies.append(copy_out(basis_ref, basis_hbm, (pl.ds(at * BLOCK, BLOCK), slice(None)), sems.at[at]))
    for copy in copies:
        copy.wait()


def streamed(kernel, name, out, operands, scratch, flops):
    blocks = max(out.shape) // BLOCK
    return pl.pallas_call(
        kernel,
        out_shape=out,
        in_specs=[VMEM] * len(operands),
        out_specs=pl.BlockSpec(memory_space=pl.ANY),
        scratch_shapes=[pltpu.VMEM(out.shape, jnp.float32), *scratch, pltpu.SemaphoreType.DMA((blocks,))],
        compiler_params=pltpu.CompilerParams(vmem_limit_bytes=16 * 2**20),
        cost_estimate=pl.CostEstimate(flops=flops, bytes_accessed=2 * 2**20, transcendentals=0),
        name=name,
    )(*operands)


def basis_of(sampled, flipped):
    return streamed(basis_kernel, "basis", f32(*sampled.shape), (sampled, flipped), (), 2 * 10**9)


def project_kernel(inverse_ref, *refs):
    *pieces, projection_hbm, projection_ref, cross_ref, sems = refs
    own = own_block()
    height = cross_ref.shape[0] // BLOCKS
    at = 0
    for piece in pieces:
        for top in range(0, piece.shape[0], height):
            cross_ref[rows_of(at ^ own, height), :] = piece[top:top + height, :]
            at += 1
    inverse = split(inverse_ref[...])
    copies = []
    for at in range(cross_ref.shape[1] // BLOCK):
        span = slice(at * BLOCK, (at + 1) * BLOCK)
        projection_ref[:, span] = product(inverse, split(cross_ref[:, span]), 1, 0)
        copies.append(copy_out(projection_ref, projection_hbm, (slice(None), pl.ds(at * BLOCK, BLOCK)), sems.at[at]))
    for copy in copies:
        copy.wait()


def project(inverse, pieces):
    rank, depth = inverse.shape[0], pieces[0].shape[1]
    scratch = (pltpu.VMEM((rank, depth), jnp.float32),)
    return streamed(project_kernel, "project", f32(rank, depth), (inverse, *pieces), scratch, 4 * 10**8)


def send(value, wide, narrow):
    mask = wide * lax.axis_size("narrow") + narrow
    pairs = [(source, source ^ mask) for source in range(lax.axis_size(AXES))]
    return lax.ppermute(value, AXES, pairs)


CORE = (1, 0)
PLANE = [(0, 1), (2, 0), (2, 1)]
NEAR, FAR = (4, 0), (8, 0)


def spare_bits():
    wide = [(2**bit, 0) for bit in range(4, lax.axis_size("wide").bit_length() - 1)]
    narrow = [(0, 2**bit) for bit in range(1, lax.axis_size("narrow").bit_length() - 1)]
    return wide + narrow


def spread(parts, masks):
    first, *rest = parts
    return [first] + [send(part, *mask) for part, mask in zip(rest, masks)]


def per_device(features, sketch):
    scale = (features.shape[0] * lax.axis_size(AXES)) ** 0.5
    size = sketch.shape[1]
    sampled, keep, other, gram, gram_other = local_terms(features, sketch)
    gram_other = send(gram_other, *CORE)
    parts = sums([keep, send(other, *CORE)], 4, after=(gram_other,))
    cross = spread(parts, PLANE)
    gram = add([gram, gram_other], parts[-1:])
    gram = gram + send(gram, *NEAR)
    gram_other = send(gram, *FAR)
    (line,) = sums(cross)
    gram = add([gram, gram_other], (line,))
    grams = [gram] + [send(gram, *mask) for mask in PLANE]
    (line,) = sums([line, send(line, *NEAR)], masks=(0, 1))
    gram = add(grams, (line,))
    for mask in spare_bits():
        line = line + send(line, *mask)
        gram = gram + send(gram, *mask)
    *state, norm = first_part(gram, send(gram, *CORE), size, ())
    (line,) = sums([line, send(line, *FAR)], masks=(0, 2), after=state[:1])
    plane = [line] + [send(line, *mask) for mask in PLANE]
    inverse, flipped, factor = last_part((*state, norm), size, scale, PANEL, (line,))
    cross = plane + [send(part, *CORE) for part in plane]
    return (basis_of(sampled, flipped), factor, project(inverse, cross))


def solution(mesh):
    rows = P(AXES, None)
    return jax.shard_map(
        per_device, mesh=mesh, in_specs=(rows, P()), out_specs=(rows, P(), P()), check_vma=False
    )
```

```python
import jax, jax.numpy as jnp
from jax import lax
from jax.experimental import pallas as pl
from jax.experimental.pallas import tpu as pltpu
from jax.sharding import PartitionSpec as P

GROUP = 8
LANES = 128
PANEL = 64
BLOCK = 256
BLOCKS = 32
AXES = ("wide", "narrow")
VMEM = pl.BlockSpec(memory_space=pltpu.VMEM)


def factor_panel(a_ref, factor_ref, buffer_ref, base, height, size):
    lane = lax.broadcasted_iota(jnp.int32, (GROUP, LANES), 1)
    sub = lax.broadcasted_iota(jnp.int32, (GROUP, LANES), 0)
    tiles = size // LANES
    spread = lambda value: jnp.broadcast_to(value, (GROUP, LANES))

    def spread_row(slot, k):
        return spread(buffer_ref[slot * GROUP + k:slot * GROUP + k + 1, :])

    def keep(value, slot):
        buffer_ref[slot * GROUP:(slot + 1) * GROUP, :] = value

    rows = {}
    for g in range(base, base + height, GROUP):
        for t in range(tiles):
            rows[g, t] = a_ref[g:g + GROUP, t * LANES:(t + 1) * LANES]
    for top in range(base, base + height, GROUP):
        groups = list(range(top, base + height, GROUP))
        home = top // LANES
        offset = top - home * LANES
        inside = (lane >= offset) & (lane < offset + GROUP)
        diag = rows[top, home]
        bank = top // GROUP % 2 * 20
        col, one = {}, {}
        for j in range(GROUP):
            for g in groups:
                col[g, j] = spread(rows[g, home][:, offset + j:offset + j + 1])
            keep(col[top, j], bank + j)
            for k in range(j, GROUP):
                one[k, j] = spread_row(bank + j, k)
        for g in groups:
            fresh = jnp.where(lane == sub + offset, 1.0, 0.0) if g == top else 0.0
            rows[g, home] = jnp.where(inside, fresh, rows[g, home])
        for j in range(0, GROUP, 2):
            a, b, c = one[j, j], one[j + 1, j], one[j + 1, j + 1]
            first = lax.rsqrt(a)
            both = first * lax.rsqrt(a * c - b * b)
            cross = b * first
            second = a * both
            low = {}
            for k in range(j + 2, GROUP):
                low[k] = one[k, j] * first, (a * one[k, j + 1] - b * one[k, j]) * both
            for k in range(j + 2, GROUP):
                for m in range(k, GROUP):
                    one[m, k] = one[m, k] - (low[m][0] * low[k][0] + low[m][1] * low[k][1])
            scaled = {}
            for g in groups:
                scaled[g] = col[g, j] * first, (a * col[g, j + 1] - b * col[g, j]) * both
            for k in range(j + 2, GROUP):
                for g in groups:
                    col[g, k] = col[g, k] - (scaled[g][0] * low[k][0] + scaled[g][1] * low[k][1])
            below = [jnp.where(sub > j + 1, part, 0.0) for part in scaled[top]]

            def pivots(value, slot):
                slot = bank + GROUP + 3 * (j // 2) + slot
                keep(value, slot)
                upper = spread_row(slot, j) * first
                return upper, (spread_row(slot, j + 1) - cross * upper) * second

            def replaced(value, upper, lower):
                value = value - (below[0] * upper + below[1] * lower)
                return jnp.where(sub == j, upper, jnp.where(sub == j + 1, lower, value))

            diag = replaced(diag, *pivots(diag, 2))
            for t in range(tiles):
                upper, lower = pivots(rows[top, t], t)
                rows[top, t] = replaced(rows[top, t], upper, lower)
                for g in groups[1:]:
                    rows[g, t] = rows[g, t] - (scaled[g][0] * upper + scaled[g][1] * lower)
        for t in range(tiles):
            span = slice(t * LANES, (t + 1) * LANES)
            a_ref[top:top + GROUP, span] = rows[top, t]
            if t < home:
                factor_ref[top:top + GROUP, span] = jnp.zeros((GROUP, LANES), jnp.float32)
            elif t == home:
                factor_ref[top:top + GROUP, span] = jnp.where(lane >= sub + offset, diag, 0.0)
            else:
                factor_ref[top:top + GROUP, span] = rows[top, t]


def trailing(a_ref, base, height, size):
    end = base + height
    if end == size:
        return
    panel = a_ref[base:end, :]
    col = lax.broadcasted_iota(jnp.int32, (height, size), 1)
    row = lax.broadcasted_iota(jnp.int32, (height, size), 0) + base
    right = jnp.where((col <= row) | (col >= end), panel, 0.0)
    left = panel[:, end:]
    update = lax.dot_general(left, right, (((0,), (0,)), ((), ())), precision=lax.Precision.HIGHEST, preferred_element_type=jnp.float32)
    rest = a_ref[end:, :]
    at = lax.broadcasted_iota(jnp.int32, (size - end, size), 1)
    a_ref[end:, :] = jnp.where((at >= base) & (at < end), 0.0, rest) - update


def normalize(a_ref):
    size = a_ref.shape[0]
    col = lax.broadcasted_iota(jnp.int32, (size, size), 1)
    row = lax.broadcasted_iota(jnp.int32, (size, size), 0)
    largest = jnp.max(jnp.where(col == row, a_ref[...], 0.0), axis=(0, 1), keepdims=True)
    shrink = lax.rsqrt(largest)
    a_ref[...] = a_ref[...] * shrink * shrink
    return shrink, largest * shrink


def eliminate(a_ref, factor_ref, buffer_ref, first, last):
    size = a_ref.shape[0]
    for base in range(first, last, PANEL):
        factor_panel(a_ref, factor_ref, buffer_ref, base, PANEL, size)
        trailing(a_ref, base, PANEL, size)


def split(value):
    high = value.astype(jnp.bfloat16)
    return high, (value - high.astype(jnp.float32)).astype(jnp.bfloat16)


def product(left, right, left_dim, right_dim):
    dims = (((left_dim,), (right_dim,)), ((), ()))
    dot = lambda a, b: lax.dot_general(a, b, dims, preferred_element_type=jnp.float32)
    return dot(left[0], right[0]) + (dot(left[0], right[1]) + dot(left[1], right[0]))


def core_bit():
    return lax.rem(lax.axis_index("wide"), 2)


def own_block():
    wide, narrow = lax.axis_index("wide"), lax.axis_index("narrow")
    plane = lax.rem(narrow, 2) + 2 * lax.rem(wide // 2, 2)
    return 16 * lax.rem(wide, 2) + 4 * plane + lax.rem(wide // 4, 4)


def rows_of(block, height):
    return pl.ds(pl.multiple_of(block * height, GROUP), height)


def local_kernel(features_hbm, sketch_hbm, sampled_ref, keep_ref, send_ref, gram_keep_ref, gram_send_ref, features_ref, sketch_ref, pair_ref, high_ref, low_ref, flip_high_ref, flip_low_ref, cross_ref, packed_ref, sems):
    rows, depth = features_ref.shape
    rank = sketch_ref.shape[1]
    chunks = rows // BLOCK
    copies = [pltpu.make_async_copy(sketch_hbm, sketch_ref, sems.at[chunks])]
    for at in range(chunks):
        span = pl.ds(at * BLOCK, BLOCK)
        copies.append(pltpu.make_async_copy(features_hbm.at[span, :], features_ref.at[span, :], sems.at[at]))
    for copy in copies:
        copy.start()
    copies[0].wait()
    pair_ref[:, :rank], pair_ref[:, rank:] = split(sketch_ref[...])
    gram = None
    for at in range(chunks):
        span = slice(at * BLOCK, (at + 1) * BLOCK)
        copies[1 + at].wait()
        features = split(features_ref[span, :])
        high_ref[span, :], low_ref[span, :] = features
        both = lax.dot(features[0], pair_ref[...], preferred_element_type=jnp.float32)
        sampled = both[:, :rank] + (both[:, rank:] + lax.dot(features[1], pair_ref[:, :rank], preferred_element_type=jnp.float32))
        sampled_ref[span, :] = sampled
        flipped = split(sampled.T)
        flip_high_ref[:, span], flip_low_ref[:, span] = flipped
        term = product(flipped, split(sampled), 1, 0)
        gram = term if gram is None else gram + term
    packed_ref[:LANES, :] = gram[:LANES, :LANES]
    packed_ref[LANES:2 * LANES, :] = gram[:LANES, LANES:]
    packed_ref[2 * LANES:, :] = gram[LANES:, LANES:]
    half = packed_ref.shape[0] // 2
    core = core_bit()
    gram_keep_ref[...] = packed_ref[rows_of(core, half), :]
    gram_send_ref[...] = packed_ref[rows_of(1 - core, half), :]
    flipped = flip_high_ref[...], flip_low_ref[...]
    own = own_block()
    height = rank // BLOCKS
    for left in range(0, depth, BLOCK):
        span = slice(left, left + BLOCK)
        cross_ref[:, span] = product(flipped, (high_ref[:, span], low_ref[:, span]), 1, 0)
    for at in range(BLOCKS):
        block = cross_ref[rows_of(at ^ own, height), :]
        if at < BLOCKS // 2:
            keep_ref[at * height:(at + 1) * height, :] = block
        else:
            rest = at - BLOCKS // 2
            send_ref[rest * height:(rest + 1) * height, :] = block


def f32(*shape):
    return jax.ShapeDtypeStruct(shape, jnp.float32)


def local_terms(features, sketch):
    rows, depth = features.shape
    rank = sketch.shape[1]
    packed = 3 * LANES
    hbm = pl.BlockSpec(memory_space=pltpu.HBM)
    return pl.pallas_call(
        local_kernel,
        out_shape=(f32(rows, rank), f32(rank // 2, depth), f32(rank // 2, depth), f32(packed // 2, LANES), f32(packed // 2, LANES)),
        in_specs=[hbm, hbm],
        out_specs=(VMEM,) * 5,
        scratch_shapes=[
            pltpu.VMEM((rows, depth), jnp.float32), pltpu.VMEM((depth, rank), jnp.float32),
            pltpu.VMEM((depth, 2 * rank), jnp.bfloat16),
            pltpu.VMEM((rows, depth), jnp.bfloat16), pltpu.VMEM((rows, depth), jnp.bfloat16),
            pltpu.VMEM((rank, rows), jnp.bfloat16), pltpu.VMEM((rank, rows), jnp.bfloat16),
            pltpu.VMEM((rank, depth), jnp.float32), pltpu.VMEM((packed, LANES), jnp.float32),
            pltpu.SemaphoreType.DMA((rows // BLOCK + 1,)),
        ],
        compiler_params=pltpu.CompilerParams(vmem_limit_bytes=51 * 2**20),
        cost_estimate=pl.CostEstimate(flops=4 * 10**9, bytes_accessed=8 * 2**20, transcendentals=0),
        name="local_terms",
    )(features, sketch)


def call(kernel, name, outs, *operands, after=(), scratch=(), flops=10**6):
    return pl.pallas_call(
        lambda *refs: kernel(*refs[:len(operands)], *refs[len(operands) + len(after):]),
        out_shape=outs,
        in_specs=[VMEM] * len(operands) + [pl.BlockSpec(memory_space=pl.ANY)] * len(after),
        out_specs=jax.tree.map(lambda _: VMEM, outs),
        scratch_shapes=list(scratch),
        compiler_params=pltpu.CompilerParams(vmem_limit_bytes=16 * 2**20),
        cost_estimate=pl.CostEstimate(flops=flops, bytes_accessed=10**6, transcendentals=0),
        name=name,
    )(*operands, *after)


def sum_kernel(masks, *refs):
    cross, outs = refs[:len(masks)], refs[len(masks):]
    at = 0
    for out_ref in outs:
        for top in range(0, out_ref.shape[0], GROUP):
            blocks = [ref[(at ^ mask) * GROUP:(at ^ mask) * GROUP + GROUP, :] for ref, mask in zip(cross, masks)]
            out_ref[top:top + GROUP, :] = sum(blocks)
            at += 1


def sums(cross, pieces=1, masks=None, after=()):
    height, depth = cross[0].shape
    masks = masks or (0,) * len(cross)
    outs = (f32(height // pieces, depth),) * pieces
    return call(lambda *refs: sum_kernel(masks, *refs), "sums", outs, *cross, after=after)


def add_kernel(*refs):
    *terms, out_ref = refs
    out_ref[...] = sum(term[...] for term in terms)


def add(terms, after):
    return call(add_kernel, "add", f32(*terms[0].shape), *terms, after=after)


def first_part_kernel(keep_ref, other_ref, a_ref, factor_ref, norm_ref, packed_ref, buffer_ref):
    half = keep_ref.shape[0]
    core = core_bit()
    packed_ref[rows_of(core, half), :] = keep_ref[...]
    packed_ref[rows_of(1 - core, half), :] = other_ref[...]
    a_ref[:LANES, :LANES] = packed_ref[:LANES, :]
    a_ref[:LANES, LANES:] = packed_ref[LANES:2 * LANES, :]
    a_ref[LANES:, :LANES] = jnp.zeros((LANES, LANES), jnp.float32)
    a_ref[LANES:, LANES:] = packed_ref[2 * LANES:, :]
    shrink, grow = normalize(a_ref)
    norm_ref[:GROUP, :] = jnp.broadcast_to(shrink, (GROUP, LANES))
    norm_ref[GROUP:, :] = jnp.broadcast_to(grow, (GROUP, LANES))
    eliminate(a_ref, factor_ref, buffer_ref, 0, PANEL)


def last_part_kernel(scale, first, from_ref, upper_ref, norm_ref, inverse_ref, factor_ref, a_ref, buffer_ref):
    size = a_ref.shape[0]
    a_ref[...] = from_ref[...]
    eliminate(a_ref, factor_ref, buffer_ref, first, size)
    shrink, grow = norm_ref[:1, :1], norm_ref[GROUP:GROUP + 1, :1] / scale
    factor_ref[:first, :] = upper_ref[:first, :] * grow
    factor_ref[first:, :] = factor_ref[first:, :] * grow
    col = lax.broadcasted_iota(jnp.int32, (size, size), 1)
    row = lax.broadcasted_iota(jnp.int32, (size, size), 0)
    inverse_ref[...] = jnp.where(col <= row, a_ref[...], 0.0) * shrink


def buffers(*shapes):
    return [pltpu.VMEM(shape, jnp.float32) for shape in (*shapes, (40 * GROUP, LANES))]


def first_part(keep, other, size, after):
    outs = f32(size, size), f32(size, size), f32(2 * GROUP, LANES)
    return call(first_part_kernel, "first_part", outs, keep, other, after=after, scratch=buffers((3 * LANES, LANES)), flops=10**6)


def last_part(state, size, scale, first, after):
    kernel = lambda *refs: last_part_kernel(scale, first, *refs)
    return call(kernel, "last_part", (f32(size, size),) * 2, *state, after=after, scratch=buffers((size, size)), flops=3 * 10**9)


def copy_out(block_ref, out_hbm, span, sem):
    copy = pltpu.make_async_copy(block_ref.at[span], out_hbm.at[span], sem)
    copy.start()
    return copy


def basis_kernel(scale, sampled_ref, inverse_ref, basis_hbm, basis_ref, sems):
    inverse = split(inverse_ref[...] * scale)
    copies = []
    for at in range(sampled_ref.shape[0] // BLOCK):
        span = slice(at * BLOCK, (at + 1) * BLOCK)
        basis_ref[span, :] = product(split(sampled_ref[span, :]), inverse, 1, 1)
        copies.append(copy_out(basis_ref, basis_hbm, (pl.ds(at * BLOCK, BLOCK), slice(None)), sems.at[at]))
    for copy in copies:
        copy.wait()


def streamed(kernel, name, out, operands, scratch, flops):
    blocks = max(out.shape) // BLOCK
    return pl.pallas_call(
        kernel,
        out_shape=out,
        in_specs=[VMEM] * len(operands),
        out_specs=pl.BlockSpec(memory_space=pl.ANY),
        scratch_shapes=[pltpu.VMEM(out.shape, jnp.float32), *scratch, pltpu.SemaphoreType.DMA((blocks,))],
        compiler_params=pltpu.CompilerParams(vmem_limit_bytes=16 * 2**20),
        cost_estimate=pl.CostEstimate(flops=flops, bytes_accessed=2 * 2**20, transcendentals=0),
        name=name,
    )(*operands)


def basis_of(sampled, inverse, scale):
    kernel = lambda *refs: basis_kernel(scale, *refs)
    return streamed(kernel, "basis", f32(*sampled.shape), (sampled, inverse), (), 2 * 10**9)


def project_kernel(inverse_ref, *refs):
    *pieces, projection_hbm, projection_ref, cross_ref, sems = refs
    own = own_block()
    height = cross_ref.shape[0] // BLOCKS
    at = 0
    for piece in pieces:
        for top in range(0, piece.shape[0], height):
            cross_ref[rows_of(at ^ own, height), :] = piece[top:top + height, :]
            at += 1
    inverse = split(inverse_ref[...])
    copies = []
    for at in range(cross_ref.shape[1] // BLOCK):
        span = slice(at * BLOCK, (at + 1) * BLOCK)
        projection_ref[:, span] = product(inverse, split(cross_ref[:, span]), 1, 0)
        copies.append(copy_out(projection_ref, projection_hbm, (slice(None), pl.ds(at * BLOCK, BLOCK)), sems.at[at]))
    for copy in copies:
        copy.wait()


def project(inverse, pieces):
    rank, depth = inverse.shape[0], pieces[0].shape[1]
    scratch = (pltpu.VMEM((rank, depth), jnp.float32),)
    return streamed(project_kernel, "project", f32(rank, depth), (inverse, *pieces), scratch, 4 * 10**8)


def send(value, wide, narrow):
    mask = wide * lax.axis_size("narrow") + narrow
    pairs = [(source, source ^ mask) for source in range(lax.axis_size(AXES))]
    return lax.ppermute(value, AXES, pairs)


CORE = (1, 0)
PLANE = [(0, 1), (2, 0), (2, 1)]
NEAR, FAR = (4, 0), (8, 0)


def spare_bits():
    wide = [(2**bit, 0) for bit in range(4, lax.axis_size("wide").bit_length() - 1)]
    narrow = [(0, 2**bit) for bit in range(1, lax.axis_size("narrow").bit_length() - 1)]
    return wide + narrow


def to_plane(parts):
    order = sorted(range(len(PLANE)), key=lambda at: -PLANE[at][0] - PLANE[at][1])
    sent = {at: send(parts[at], *PLANE[at]) for at in order}
    return [sent[at] for at in range(len(PLANE))]


def per_device(features, sketch):
    scale = (features.shape[0] * lax.axis_size(AXES)) ** 0.5
    size = sketch.shape[1]
    sampled, keep, other, gram, gram_other = local_terms(features, sketch)
    gram_other = send(gram_other, *CORE)
    parts = sums([keep, send(other, *CORE)], 4, after=(gram_other,))
    cross = [parts[0]] + to_plane(parts[1:])
    gram = add([gram, gram_other], parts[-1:])
    gram = gram + send(gram, *NEAR)
    gram_other = send(gram, *FAR)
    (line,) = sums(cross)
    gram = add([gram, gram_other], (line,))
    grams = [gram] + to_plane([gram] * 3)
    (line,) = sums([line, send(line, *NEAR)], masks=(0, 1))
    gram = add(grams, (line,))
    for mask in spare_bits():
        line = line + send(line, *mask)
        gram = gram + send(gram, *mask)
    *state, norm = first_part(gram, send(gram, *CORE), size, ())
    (line,) = sums([line, send(line, *FAR)], masks=(0, 2), after=state[:1])
    plane = [line] + to_plane([line] * 3)
    inverse, factor = last_part((*state, norm), size, scale, PANEL, (line,))
    cross = plane + [send(part, *CORE) for part in plane]
    return (basis_of(sampled, inverse, scale), factor, project(inverse, cross))


def solution(mesh):
    rows = P(AXES, None)
    return jax.shard_map(
        per_device, mesh=mesh, in_specs=(rows, P()), out_specs=(rows, P(), P()), check_vma=False
    )
```

```python
import jax, jax.numpy as jnp
from jax import lax
from jax.experimental import pallas as pl
from jax.experimental.pallas import tpu as pltpu
from jax.sharding import PartitionSpec as P

GROUP = 8
LANES = 128
PANEL = 32
FIRST = 64
PACKED = 272
BLOCK = 256
BLOCKS = 32
AXES = ("wide", "narrow")
VMEM = pl.BlockSpec(memory_space=pltpu.VMEM)


def factor_panel(a_ref, factor_ref, buffer_ref, base, height, size):
    lane = lax.broadcasted_iota(jnp.int32, (GROUP, LANES), 1)
    sub = lax.broadcasted_iota(jnp.int32, (GROUP, LANES), 0)
    tiles = size // LANES
    spread = lambda value: jnp.broadcast_to(value, (GROUP, LANES))

    def spread_row(slot, k):
        return spread(buffer_ref[slot * GROUP + k:slot * GROUP + k + 1, :])

    def keep(value, slot):
        buffer_ref[slot * GROUP:(slot + 1) * GROUP, :] = value

    rows = {}
    for g in range(base, base + height, GROUP):
        for t in range(tiles):
            rows[g, t] = a_ref[g:g + GROUP, t * LANES:(t + 1) * LANES]
    for top in range(base, base + height, GROUP):
        groups = list(range(top, base + height, GROUP))
        home = top // LANES
        offset = top - home * LANES
        inside = (lane >= offset) & (lane < offset + GROUP)
        diag = rows[top, home]
        bank = top // GROUP % 2 * 20
        col, one = {}, {}
        for j in range(GROUP):
            for g in groups:
                col[g, j] = spread(rows[g, home][:, offset + j:offset + j + 1])
            keep(col[top, j], bank + j)
            for k in range(j, GROUP):
                one[k, j] = spread_row(bank + j, k)
        for g in groups:
            fresh = jnp.where(lane == sub + offset, 1.0, 0.0) if g == top else 0.0
            rows[g, home] = jnp.where(inside, fresh, rows[g, home])
        for j in range(0, GROUP, 2):
            a, b, c = one[j, j], one[j + 1, j], one[j + 1, j + 1]
            first = lax.rsqrt(a)
            both = first * lax.rsqrt(a * c - b * b)
            cross = b * first
            second = a * both
            low = {}
            for k in range(j + 2, GROUP):
                low[k] = one[k, j] * first, (a * one[k, j + 1] - b * one[k, j]) * both
            for k in range(j + 2, GROUP):
                for m in range(k, GROUP):
                    one[m, k] = one[m, k] - (low[m][0] * low[k][0] + low[m][1] * low[k][1])
            scaled = {}
            for g in groups:
                scaled[g] = col[g, j] * first, (a * col[g, j + 1] - b * col[g, j]) * both
            for k in range(j + 2, GROUP):
                for g in groups:
                    col[g, k] = col[g, k] - (scaled[g][0] * low[k][0] + scaled[g][1] * low[k][1])
            below = [jnp.where(sub > j + 1, part, 0.0) for part in scaled[top]]

            def pivots(value, slot):
                slot = bank + GROUP + 3 * (j // 2) + slot
                keep(value, slot)
                upper = spread_row(slot, j) * first
                return upper, (spread_row(slot, j + 1) - cross * upper) * second

            def replaced(value, upper, lower):
                value = value - (below[0] * upper + below[1] * lower)
                return jnp.where(sub == j, upper, jnp.where(sub == j + 1, lower, value))

            diag = replaced(diag, *pivots(diag, 2))
            for t in range(tiles):
                upper, lower = pivots(rows[top, t], t)
                rows[top, t] = replaced(rows[top, t], upper, lower)
                for g in groups[1:]:
                    rows[g, t] = rows[g, t] - (scaled[g][0] * upper + scaled[g][1] * lower)
        for t in range(tiles):
            span = slice(t * LANES, (t + 1) * LANES)
            a_ref[top:top + GROUP, span] = rows[top, t]
            if t < home:
                factor_ref[top:top + GROUP, span] = jnp.zeros((GROUP, LANES), jnp.float32)
            elif t == home:
                factor_ref[top:top + GROUP, span] = jnp.where(lane >= sub + offset, diag, 0.0)
            else:
                factor_ref[top:top + GROUP, span] = rows[top, t]


def trailing(a_ref, base, height, size):
    end = base + height
    if end == size:
        return
    panel = a_ref[base:end, :]
    col = lax.broadcasted_iota(jnp.int32, (height, size), 1)
    row = lax.broadcasted_iota(jnp.int32, (height, size), 0) + base
    right = jnp.where((col <= row) | (col >= end), panel, 0.0)
    left = panel[:, end:]
    update = product(split(left), split(right), 0, 0)
    rest = a_ref[end:, :]
    at = lax.broadcasted_iota(jnp.int32, (size - end, size), 1)
    a_ref[end:, :] = jnp.where((at >= base) & (at < end), 0.0, rest) - update


def eliminate(a_ref, factor_ref, buffer_ref, first, last):
    size = a_ref.shape[0]
    for base in range(first, last, PANEL):
        factor_panel(a_ref, factor_ref, buffer_ref, base, PANEL, size)
        trailing(a_ref, base, PANEL, size)


def split(value):
    high = value.astype(jnp.bfloat16)
    return high, (value - high.astype(jnp.float32)).astype(jnp.bfloat16)


def product(left, right, left_dim, right_dim):
    dims = (((left_dim,), (right_dim,)), ((), ()))
    dot = lambda a, b: lax.dot_general(a, b, dims, preferred_element_type=jnp.float32)
    return dot(left[0], right[0]) + (dot(left[0], right[1]) + dot(left[1], right[0]))


def core_bit():
    return lax.rem(lax.axis_index("wide"), 2)


def own_block():
    wide, narrow = lax.axis_index("wide"), lax.axis_index("narrow")
    plane = lax.rem(narrow, 2) + 2 * lax.rem(wide // 2, 2)
    return 16 * lax.rem(wide, 2) + 4 * plane + lax.rem(wide // 4, 4)


def rows_of(block, height):
    return pl.ds(pl.multiple_of(block * height, GROUP), height)


def local_kernel(features_hbm, sketch_hbm, sampled_ref, keep_ref, send_ref, gram_keep_ref, gram_send_ref, features_ref, sketch_ref, pair_ref, high_ref, low_ref, flip_high_ref, flip_low_ref, cross_ref, packed_ref, sems):
    rows, depth = features_ref.shape
    rank = sketch_ref.shape[1]
    chunks = rows // BLOCK
    copies = [pltpu.make_async_copy(sketch_hbm, sketch_ref, sems.at[chunks])]
    for at in range(chunks):
        span = pl.ds(at * BLOCK, BLOCK)
        copies.append(pltpu.make_async_copy(features_hbm.at[span, :], features_ref.at[span, :], sems.at[at]))
    for copy in copies:
        copy.start()
    copies[0].wait()
    pair_ref[:, :rank], pair_ref[:, rank:] = split(sketch_ref[...])
    gram = None
    for at in range(chunks):
        span = slice(at * BLOCK, (at + 1) * BLOCK)
        copies[1 + at].wait()
        features = split(features_ref[span, :])
        high_ref[span, :], low_ref[span, :] = features
        both = lax.dot(features[0], pair_ref[...], preferred_element_type=jnp.float32)
        sampled = both[:, :rank] + (both[:, rank:] + lax.dot(features[1], pair_ref[:, :rank], preferred_element_type=jnp.float32))
        sampled_ref[span, :] = sampled
        flipped = split(sampled.T)
        flip_high_ref[:, span], flip_low_ref[:, span] = flipped
        term = product(flipped, split(sampled), 1, 0)
        gram = term if gram is None else gram + term
    row = lax.broadcasted_iota(jnp.int32, (LANES, LANES), 0)
    col = lax.broadcasted_iota(jnp.int32, (LANES, LANES), 1)
    corner = gram[LANES:, LANES:]
    packed_ref[:LANES, :] = gram[:LANES, LANES:]
    packed_ref[LANES:2 * LANES, :] = jnp.where(col >= row, gram[:LANES, :LANES], corner)
    diagonal = jnp.sum(jnp.where(col == row, corner, 0.0), axis=0, keepdims=True)
    packed_ref[2 * LANES:, :] = jnp.broadcast_to(diagonal, (PACKED - 2 * LANES, LANES))
    half = packed_ref.shape[0] // 2
    core = core_bit()
    gram_keep_ref[...] = packed_ref[rows_of(core, half), :]
    gram_send_ref[...] = packed_ref[rows_of(1 - core, half), :]
    flipped = flip_high_ref[...], flip_low_ref[...]
    own = own_block()
    height = rank // BLOCKS
    for left in range(0, depth, BLOCK):
        span = slice(left, left + BLOCK)
        cross_ref[:, span] = product(flipped, (high_ref[:, span], low_ref[:, span]), 1, 0)
    for at in range(BLOCKS):
        block = cross_ref[rows_of(at ^ own, height), :]
        if at < BLOCKS // 2:
            keep_ref[at * height:(at + 1) * height, :] = block
        else:
            rest = at - BLOCKS // 2
            send_ref[rest * height:(rest + 1) * height, :] = block


def f32(*shape):
    return jax.ShapeDtypeStruct(shape, jnp.float32)


def local_terms(features, sketch):
    rows, depth = features.shape
    rank = sketch.shape[1]
    packed = PACKED
    hbm = pl.BlockSpec(memory_space=pltpu.HBM)
    return pl.pallas_call(
        local_kernel,
        out_shape=(f32(rows, rank), f32(rank // 2, depth), f32(rank // 2, depth), f32(packed // 2, LANES), f32(packed // 2, LANES)),
        in_specs=[hbm, hbm],
        out_specs=(VMEM,) * 5,
        scratch_shapes=[
            pltpu.VMEM((rows, depth), jnp.float32), pltpu.VMEM((depth, rank), jnp.float32),
            pltpu.VMEM((depth, 2 * rank), jnp.bfloat16),
            pltpu.VMEM((rows, depth), jnp.bfloat16), pltpu.VMEM((rows, depth), jnp.bfloat16),
            pltpu.VMEM((rank, rows), jnp.bfloat16), pltpu.VMEM((rank, rows), jnp.bfloat16),
            pltpu.VMEM((rank, depth), jnp.float32), pltpu.VMEM((packed, LANES), jnp.float32),
            pltpu.SemaphoreType.DMA((rows // BLOCK + 1,)),
        ],
        compiler_params=pltpu.CompilerParams(vmem_limit_bytes=51 * 2**20),
        cost_estimate=pl.CostEstimate(flops=4 * 10**9, bytes_accessed=8 * 2**20, transcendentals=0),
        name="local_terms",
    )(features, sketch)


def call(kernel, name, outs, *operands, after=(), scratch=(), flops=10**6):
    return pl.pallas_call(
        lambda *refs: kernel(*refs[:len(operands)], *refs[len(operands) + len(after):]),
        out_shape=outs,
        in_specs=[VMEM] * len(operands) + [pl.BlockSpec(memory_space=pl.ANY)] * len(after),
        out_specs=jax.tree.map(lambda _: VMEM, outs),
        scratch_shapes=list(scratch),
        compiler_params=pltpu.CompilerParams(vmem_limit_bytes=16 * 2**20),
        cost_estimate=pl.CostEstimate(flops=flops, bytes_accessed=10**6, transcendentals=0),
        name=name,
    )(*operands, *after)


def sum_kernel(masks, *refs):
    cross, outs = refs[:len(masks)], refs[len(masks):]
    at = 0
    for out_ref in outs:
        for top in range(0, out_ref.shape[0], GROUP):
            blocks = [ref[(at ^ mask) * GROUP:(at ^ mask) * GROUP + GROUP, :] for ref, mask in zip(cross, masks)]
            out_ref[top:top + GROUP, :] = sum(blocks)
            at += 1


def sums(cross, pieces=1, masks=None, after=()):
    height, depth = cross[0].shape
    masks = masks or (0,) * len(cross)
    outs = (f32(height // pieces, depth),) * pieces
    return call(lambda *refs: sum_kernel(masks, *refs), "sums", outs, *cross, after=after)


def add_kernel(*refs):
    *terms, out_ref = refs
    out_ref[...] = sum(term[...] for term in terms)


def add(terms, after):
    return call(add_kernel, "add", f32(*terms[0].shape), *terms, after=after)


def first_part_kernel(keep_ref, other_ref, a_ref, factor_ref, norm_ref, packed_ref, buffer_ref):
    half = keep_ref.shape[0]
    core = core_bit()
    packed_ref[rows_of(core, half), :] = keep_ref[...]
    packed_ref[rows_of(1 - core, half), :] = other_ref[...]
    row = lax.broadcasted_iota(jnp.int32, (LANES, LANES), 0)
    col = lax.broadcasted_iota(jnp.int32, (LANES, LANES), 1)
    mixed = packed_ref[LANES:2 * LANES, :]
    flipped = mixed.T
    diagonal = packed_ref[2 * LANES:2 * LANES + 1, :]
    largest = jnp.maximum(jnp.max(diagonal, axis=(0, 1), keepdims=True), jnp.max(jnp.where(col == row, mixed, 0.0), axis=(0, 1), keepdims=True))
    shrink = lax.rsqrt(largest)
    grow, square = largest * shrink, shrink * shrink
    a_ref[:LANES, :LANES] = jnp.where(col >= row, mixed, flipped) * square
    a_ref[:LANES, LANES:] = packed_ref[:LANES, :] * square
    a_ref[LANES:, :LANES] = jnp.zeros((LANES, LANES), jnp.float32)
    a_ref[LANES:, LANES:] = jnp.where(col < row, mixed, jnp.where(col == row, diagonal, flipped)) * square
    norm_ref[:GROUP, :] = jnp.broadcast_to(shrink, (GROUP, LANES))
    norm_ref[GROUP:, :] = jnp.broadcast_to(grow, (GROUP, LANES))
    eliminate(a_ref, factor_ref, buffer_ref, 0, FIRST)


def last_part_kernel(scale, first, from_ref, upper_ref, norm_ref, inverse_ref, factor_ref, a_ref, buffer_ref):
    size = a_ref.shape[0]
    a_ref[...] = from_ref[...]
    eliminate(a_ref, factor_ref, buffer_ref, first, size)
    shrink, grow = norm_ref[:1, :1], norm_ref[GROUP:GROUP + 1, :1] / scale
    factor_ref[:first, :] = upper_ref[:first, :] * grow
    factor_ref[first:, :] = factor_ref[first:, :] * grow
    col = lax.broadcasted_iota(jnp.int32, (size, size), 1)
    row = lax.broadcasted_iota(jnp.int32, (size, size), 0)
    inverse_ref[...] = jnp.where(col <= row, a_ref[...], 0.0) * shrink


def buffers(*shapes):
    return [pltpu.VMEM(shape, jnp.float32) for shape in (*shapes, (40 * GROUP, LANES))]


def first_part(keep, other, size, after):
    outs = f32(size, size), f32(size, size), f32(2 * GROUP, LANES)
    return call(first_part_kernel, "first_part", outs, keep, other, after=after, scratch=buffers((PACKED, LANES)), flops=10**6)


def last_part(state, size, scale, first, after):
    kernel = lambda *refs: last_part_kernel(scale, first, *refs)
    return call(kernel, "last_part", (f32(size, size),) * 2, *state, after=after, scratch=buffers((size, size)), flops=3 * 10**9)


def copy_out(block_ref, out_hbm, span, sem):
    copy = pltpu.make_async_copy(block_ref.at[span], out_hbm.at[span], sem)
    copy.start()
    return copy


def basis_kernel(scale, sampled_ref, inverse_ref, basis_hbm, basis_ref, sems):
    inverse = split(inverse_ref[...] * scale)
    copies = []
    for at in range(sampled_ref.shape[0] // BLOCK):
        span = slice(at * BLOCK, (at + 1) * BLOCK)
        basis_ref[span, :] = product(split(sampled_ref[span, :]), inverse, 1, 1)
        copies.append(copy_out(basis_ref, basis_hbm, (pl.ds(at * BLOCK, BLOCK), slice(None)), sems.at[at]))
    for copy in copies:
        copy.wait()


def streamed(kernel, name, out, operands, scratch, flops):
    blocks = max(out.shape) // BLOCK
    return pl.pallas_call(
        kernel,
        out_shape=out,
        in_specs=[VMEM] * len(operands),
        out_specs=pl.BlockSpec(memory_space=pl.ANY),
        scratch_shapes=[pltpu.VMEM(out.shape, jnp.float32), *scratch, pltpu.SemaphoreType.DMA((blocks,))],
        compiler_params=pltpu.CompilerParams(vmem_limit_bytes=16 * 2**20),
        cost_estimate=pl.CostEstimate(flops=flops, bytes_accessed=2 * 2**20, transcendentals=0),
        name=name,
    )(*operands)


def basis_of(sampled, inverse, scale):
    kernel = lambda *refs: basis_kernel(scale, *refs)
    return streamed(kernel, "basis", f32(*sampled.shape), (sampled, inverse), (), 2 * 10**9)


def project_kernel(inverse_ref, *refs):
    *pieces, projection_hbm, projection_ref, cross_ref, sems = refs
    own = own_block()
    height = cross_ref.shape[0] // BLOCKS
    at = 0
    for piece in pieces:
        for top in range(0, piece.shape[0], height):
            cross_ref[rows_of(at ^ own, height), :] = piece[top:top + height, :]
            at += 1
    inverse = split(inverse_ref[...])
    copies = []
    for at in range(cross_ref.shape[1] // BLOCK):
        span = slice(at * BLOCK, (at + 1) * BLOCK)
        projection_ref[:, span] = product(inverse, split(cross_ref[:, span]), 1, 0)
        copies.append(copy_out(projection_ref, projection_hbm, (slice(None), pl.ds(at * BLOCK, BLOCK)), sems.at[at]))
    for copy in copies:
        copy.wait()


def project(inverse, pieces):
    rank, depth = inverse.shape[0], pieces[0].shape[1]
    scratch = (pltpu.VMEM((rank, depth), jnp.float32),)
    return streamed(project_kernel, "project", f32(rank, depth), (inverse, *pieces), scratch, 4 * 10**8)


def send(value, wide, narrow):
    mask = wide * lax.axis_size("narrow") + narrow
    pairs = [(source, source ^ mask) for source in range(lax.axis_size(AXES))]
    return lax.ppermute(value, AXES, pairs)


CORE = (1, 0)
PLANE = [(0, 1), (2, 0), (2, 1)]
NEAR, FAR = (4, 0), (8, 0)


def spare_bits():
    wide = [(2**bit, 0) for bit in range(4, lax.axis_size("wide").bit_length() - 1)]
    narrow = [(0, 2**bit) for bit in range(1, lax.axis_size("narrow").bit_length() - 1)]
    return wide + narrow


def to_plane(parts):
    order = sorted(range(len(PLANE)), key=lambda at: -PLANE[at][0] - PLANE[at][1])
    sent = {at: send(parts[at], *PLANE[at]) for at in order}
    return [sent[at] for at in range(len(PLANE))]


def per_device(features, sketch):
    scale = (features.shape[0] * lax.axis_size(AXES)) ** 0.5
    size = sketch.shape[1]
    sampled, keep, other, gram, gram_other = local_terms(features, sketch)
    gram_other = send(gram_other, *CORE)
    parts = sums([keep, send(other, *CORE)], 4, after=(gram_other,))
    cross = [parts[0]] + to_plane(parts[1:])
    gram = add([gram, gram_other], parts[-1:])
    gram = gram + send(gram, *NEAR)
    gram_other = send(gram, *FAR)
    (line,) = sums(cross)
    gram = add([gram, gram_other], (line,))
    grams = [gram] + to_plane([gram] * 3)
    (line,) = sums([line, send(line, *NEAR)], masks=(0, 1))
    gram = add(grams, (line,))
    for mask in spare_bits():
        line = line + send(line, *mask)
        gram = gram + send(gram, *mask)
    *state, norm = first_part(gram, send(gram, *CORE), size, ())
    (line,) = sums([line, send(line, *FAR)], masks=(0, 2), after=state[:1])
    plane = [line] + to_plane([line] * 3)
    inverse, factor = last_part((*state, norm), size, scale, FIRST, (line,))
    cross = plane + [send(part, *CORE) for part in plane]
    return (basis_of(sampled, inverse, scale), factor, project(inverse, cross))


def solution(mesh):
    rows = P(AXES, None)
    return jax.shard_map(
        per_device, mesh=mesh, in_specs=(rows, P()), out_specs=(rows, P(), P()), check_vma=False
    )
```

```python
import jax, jax.numpy as jnp
from jax import lax
from jax.experimental import pallas as pl
from jax.experimental.pallas import tpu as pltpu
from jax.sharding import PartitionSpec as P

GROUP = 8
LANES = 128
PANEL = 64
PACKED = 272
BLOCK = 256
BLOCKS = 32
AXES = ("wide", "narrow")
VMEM = pl.BlockSpec(memory_space=pltpu.VMEM)


def factor_panel(a_ref, factor_ref, buffer_ref, base, height, size):
    lane = lax.broadcasted_iota(jnp.int32, (GROUP, LANES), 1)
    sub = lax.broadcasted_iota(jnp.int32, (GROUP, LANES), 0)
    tiles = size // LANES
    spread = lambda value: jnp.broadcast_to(value, (GROUP, LANES))

    def spread_row(slot, k):
        return spread(buffer_ref[slot * GROUP + k:slot * GROUP + k + 1, :])

    def keep(value, slot):
        buffer_ref[slot * GROUP:(slot + 1) * GROUP, :] = value

    rows = {}
    for g in range(base, base + height, GROUP):
        for t in range(tiles):
            rows[g, t] = a_ref[g:g + GROUP, t * LANES:(t + 1) * LANES]
    for top in range(base, base + height, GROUP):
        groups = list(range(top, base + height, GROUP))
        home = top // LANES
        offset = top - home * LANES
        inside = (lane >= offset) & (lane < offset + GROUP)
        diag = rows[top, home]
        bank = top // GROUP % 2 * 20
        col, one = {}, {}
        for j in range(GROUP):
            for g in groups:
                col[g, j] = spread(rows[g, home][:, offset + j:offset + j + 1])
            keep(col[top, j], bank + j)
            for k in range(j, GROUP):
                one[k, j] = spread_row(bank + j, k)
        for g in groups:
            fresh = jnp.where(lane == sub + offset, 1.0, 0.0) if g == top else 0.0
            rows[g, home] = jnp.where(inside, fresh, rows[g, home])
        for j in range(0, GROUP, 2):
            a, b, c = one[j, j], one[j + 1, j], one[j + 1, j + 1]
            first = lax.rsqrt(a)
            both = first * lax.rsqrt(a * c - b * b)
            cross = b * first
            second = a * both
            low = {}
            for k in range(j + 2, GROUP):
                low[k] = one[k, j] * first, (a * one[k, j + 1] - b * one[k, j]) * both
            for k in range(j + 2, GROUP):
                for m in range(k, GROUP):
                    one[m, k] = one[m, k] - (low[m][0] * low[k][0] + low[m][1] * low[k][1])
            scaled = {}
            for g in groups:
                scaled[g] = col[g, j] * first, (a * col[g, j + 1] - b * col[g, j]) * both
            for k in range(j + 2, GROUP):
                for g in groups:
                    col[g, k] = col[g, k] - (scaled[g][0] * low[k][0] + scaled[g][1] * low[k][1])
            below = [jnp.where(sub > j + 1, part, 0.0) for part in scaled[top]]

            def pivots(value, slot):
                slot = bank + GROUP + 3 * (j // 2) + slot
                keep(value, slot)
                upper = spread_row(slot, j) * first
                return upper, (spread_row(slot, j + 1) - cross * upper) * second

            def replaced(value, upper, lower):
                value = value - (below[0] * upper + below[1] * lower)
                return jnp.where(sub == j, upper, jnp.where(sub == j + 1, lower, value))

            diag = replaced(diag, *pivots(diag, 2))
            for t in range(tiles):
                upper, lower = pivots(rows[top, t], t)
                rows[top, t] = replaced(rows[top, t], upper, lower)
                for g in groups[1:]:
                    rows[g, t] = rows[g, t] - (scaled[g][0] * upper + scaled[g][1] * lower)
        for t in range(tiles):
            span = slice(t * LANES, (t + 1) * LANES)
            a_ref[top:top + GROUP, span] = rows[top, t]
            if t < home:
                factor_ref[top:top + GROUP, span] = jnp.zeros((GROUP, LANES), jnp.float32)
            elif t == home:
                factor_ref[top:top + GROUP, span] = jnp.where(lane >= sub + offset, diag, 0.0)
            else:
                factor_ref[top:top + GROUP, span] = rows[top, t]


def trailing(a_ref, base, height, size):
    end = base + height
    if end == size:
        return
    panel = a_ref[base:end, :]
    col = lax.broadcasted_iota(jnp.int32, (height, size), 1)
    row = lax.broadcasted_iota(jnp.int32, (height, size), 0) + base
    right = jnp.where((col <= row) | (col >= end), panel, 0.0)
    left = panel[:, end:]
    update = product(split(left), split(right), 0, 0)
    rest = a_ref[end:, :]
    at = lax.broadcasted_iota(jnp.int32, (size - end, size), 1)
    a_ref[end:, :] = jnp.where((at >= base) & (at < end), 0.0, rest) - update


def eliminate(a_ref, factor_ref, buffer_ref, first, last):
    size = a_ref.shape[0]
    for base in range(first, last, PANEL):
        factor_panel(a_ref, factor_ref, buffer_ref, base, PANEL, size)
        trailing(a_ref, base, PANEL, size)


def split(value):
    high = value.astype(jnp.bfloat16)
    return high, (value - high.astype(jnp.float32)).astype(jnp.bfloat16)


def product(left, right, left_dim, right_dim):
    dims = (((left_dim,), (right_dim,)), ((), ()))
    dot = lambda a, b: lax.dot_general(a, b, dims, preferred_element_type=jnp.float32)
    return dot(left[0], right[0]) + (dot(left[0], right[1]) + dot(left[1], right[0]))


def core_bit():
    return lax.rem(lax.axis_index("wide"), 2)


def own_block():
    wide, narrow = lax.axis_index("wide"), lax.axis_index("narrow")
    plane = lax.rem(narrow, 2) + 2 * lax.rem(wide // 2, 2)
    return 16 * lax.rem(wide, 2) + 4 * plane + lax.rem(wide // 4, 4)


def rows_of(block, height):
    return pl.ds(pl.multiple_of(block * height, GROUP), height)


def local_kernel(features_hbm, sketch_hbm, sampled_ref, keep_ref, send_ref, gram_keep_ref, gram_send_ref, features_ref, sketch_ref, pair_ref, high_ref, low_ref, flip_high_ref, flip_low_ref, cross_ref, packed_ref, sems):
    rows, depth = features_ref.shape
    rank = sketch_ref.shape[1]
    chunks = rows // BLOCK
    copies = [pltpu.make_async_copy(sketch_hbm, sketch_ref, sems.at[chunks])]
    for at in range(chunks):
        span = pl.ds(at * BLOCK, BLOCK)
        copies.append(pltpu.make_async_copy(features_hbm.at[span, :], features_ref.at[span, :], sems.at[at]))
    for copy in copies:
        copy.start()
    copies[0].wait()
    pair_ref[:, :rank], pair_ref[:, rank:] = split(sketch_ref[...])
    gram = None
    for at in range(chunks):
        span = slice(at * BLOCK, (at + 1) * BLOCK)
        copies[1 + at].wait()
        features = split(features_ref[span, :])
        high_ref[span, :], low_ref[span, :] = features
        both = lax.dot(features[0], pair_ref[...], preferred_element_type=jnp.float32)
        sampled = both[:, :rank] + (both[:, rank:] + lax.dot(features[1], pair_ref[:, :rank], preferred_element_type=jnp.float32))
        sampled_ref[span, :] = sampled
        flipped = split(sampled.T)
        flip_high_ref[:, span], flip_low_ref[:, span] = flipped
        term = product(flipped, split(sampled), 1, 0)
        gram = term if gram is None else gram + term
    row = lax.broadcasted_iota(jnp.int32, (LANES, LANES), 0)
    col = lax.broadcasted_iota(jnp.int32, (LANES, LANES), 1)
    corner = gram[LANES:, LANES:]
    packed_ref[:LANES, :] = gram[:LANES, LANES:]
    packed_ref[LANES:2 * LANES, :] = jnp.where(col >= row, gram[:LANES, :LANES], corner)
    diagonal = jnp.sum(jnp.where(col == row, corner, 0.0), axis=0, keepdims=True)
    packed_ref[2 * LANES:, :] = jnp.broadcast_to(diagonal, (PACKED - 2 * LANES, LANES))
    half = packed_ref.shape[0] // 2
    core = core_bit()
    gram_keep_ref[...] = packed_ref[rows_of(core, half), :]
    gram_send_ref[...] = packed_ref[rows_of(1 - core, half), :]
    flipped = flip_high_ref[...], flip_low_ref[...]
    own = own_block()
    height = rank // BLOCKS
    for left in range(0, depth, BLOCK):
        span = slice(left, left + BLOCK)
        cross_ref[:, span] = product(flipped, (high_ref[:, span], low_ref[:, span]), 1, 0)
    for at in range(BLOCKS):
        block = cross_ref[rows_of(at ^ own, height), :]
        if at < BLOCKS // 2:
            keep_ref[at * height:(at + 1) * height, :] = block
        else:
            rest = at - BLOCKS // 2
            send_ref[rest * height:(rest + 1) * height, :] = block


def f32(*shape):
    return jax.ShapeDtypeStruct(shape, jnp.float32)


def local_terms(features, sketch):
    rows, depth = features.shape
    rank = sketch.shape[1]
    packed = PACKED
    hbm = pl.BlockSpec(memory_space=pltpu.HBM)
    return pl.pallas_call(
        local_kernel,
        out_shape=(f32(rows, rank), f32(rank // 2, depth), f32(rank // 2, depth), f32(packed // 2, LANES), f32(packed // 2, LANES)),
        in_specs=[hbm, hbm],
        out_specs=(VMEM,) * 5,
        scratch_shapes=[
            pltpu.VMEM((rows, depth), jnp.float32), pltpu.VMEM((depth, rank), jnp.float32),
            pltpu.VMEM((depth, 2 * rank), jnp.bfloat16),
            pltpu.VMEM((rows, depth), jnp.bfloat16), pltpu.VMEM((rows, depth), jnp.bfloat16),
            pltpu.VMEM((rank, rows), jnp.bfloat16), pltpu.VMEM((rank, rows), jnp.bfloat16),
            pltpu.VMEM((rank, depth), jnp.float32), pltpu.VMEM((packed, LANES), jnp.float32),
            pltpu.SemaphoreType.DMA((rows // BLOCK + 1,)),
        ],
        compiler_params=pltpu.CompilerParams(vmem_limit_bytes=51 * 2**20),
        cost_estimate=pl.CostEstimate(flops=4 * 10**9, bytes_accessed=8 * 2**20, transcendentals=0),
        name="local_terms",
    )(features, sketch)


def call(kernel, name, outs, *operands, after=(), scratch=(), flops=10**6):
    return pl.pallas_call(
        lambda *refs: kernel(*refs[:len(operands)], *refs[len(operands) + len(after):]),
        out_shape=outs,
        in_specs=[VMEM] * len(operands) + [pl.BlockSpec(memory_space=pl.ANY)] * len(after),
        out_specs=jax.tree.map(lambda _: VMEM, outs),
        scratch_shapes=list(scratch),
        compiler_params=pltpu.CompilerParams(vmem_limit_bytes=16 * 2**20),
        cost_estimate=pl.CostEstimate(flops=flops, bytes_accessed=10**6, transcendentals=0),
        name=name,
    )(*operands, *after)


def sum_kernel(masks, *refs):
    cross, outs = refs[:len(masks)], refs[len(masks):]
    at = 0
    for out_ref in outs:
        for top in range(0, out_ref.shape[0], GROUP):
            blocks = [ref[(at ^ mask) * GROUP:(at ^ mask) * GROUP + GROUP, :] for ref, mask in zip(cross, masks)]
            out_ref[top:top + GROUP, :] = sum(blocks)
            at += 1


def sums(cross, pieces=1, masks=None, after=()):
    height, depth = cross[0].shape
    masks = masks or (0,) * len(cross)
    outs = (f32(height // pieces, depth),) * pieces
    return call(lambda *refs: sum_kernel(masks, *refs), "sums", outs, *cross, after=after)


def add_kernel(*refs):
    *terms, out_ref = refs
    out_ref[...] = sum(term[...] for term in terms)


def add(terms, after):
    return call(add_kernel, "add", f32(*terms[0].shape), *terms, after=after, flops=10**9)


def first_part_kernel(keep_ref, other_ref, a_ref, factor_ref, norm_ref, packed_ref, buffer_ref):
    half = keep_ref.shape[0]
    core = core_bit()
    packed_ref[rows_of(core, half), :] = keep_ref[...]
    packed_ref[rows_of(1 - core, half), :] = other_ref[...]
    row = lax.broadcasted_iota(jnp.int32, (LANES, LANES), 0)
    col = lax.broadcasted_iota(jnp.int32, (LANES, LANES), 1)
    mixed = packed_ref[LANES:2 * LANES, :]
    flipped = mixed.T
    diagonal = packed_ref[2 * LANES:2 * LANES + 1, :]
    largest = jnp.maximum(jnp.max(diagonal, axis=(0, 1), keepdims=True), jnp.max(jnp.where(col == row, mixed, 0.0), axis=(0, 1), keepdims=True))
    shrink = lax.rsqrt(largest)
    grow, square = largest * shrink, shrink * shrink
    a_ref[:LANES, :LANES] = jnp.where(col >= row, mixed, flipped) * square
    a_ref[:LANES, LANES:] = packed_ref[:LANES, :] * square
    a_ref[LANES:, :LANES] = jnp.zeros((LANES, LANES), jnp.float32)
    a_ref[LANES:, LANES:] = jnp.where(col < row, mixed, jnp.where(col == row, diagonal, flipped)) * square
    norm_ref[:GROUP, :] = jnp.broadcast_to(shrink, (GROUP, LANES))
    norm_ref[GROUP:, :] = jnp.broadcast_to(grow, (GROUP, LANES))
    eliminate(a_ref, factor_ref, buffer_ref, 0, PANEL)


def last_part_kernel(scale, first, from_ref, upper_ref, norm_ref, inverse_ref, factor_ref, a_ref, buffer_ref):
    size = a_ref.shape[0]
    a_ref[...] = from_ref[...]
    eliminate(a_ref, factor_ref, buffer_ref, first, size)
    shrink, grow = norm_ref[:1, :1], norm_ref[GROUP:GROUP + 1, :1] / scale
    factor_ref[:first, :] = upper_ref[:first, :] * grow
    factor_ref[first:, :] = factor_ref[first:, :] * grow
    col = lax.broadcasted_iota(jnp.int32, (size, size), 1)
    row = lax.broadcasted_iota(jnp.int32, (size, size), 0)
    inverse_ref[...] = jnp.where(col <= row, a_ref[...], 0.0) * shrink


def buffers(*shapes):
    return [pltpu.VMEM(shape, jnp.float32) for shape in (*shapes, (40 * GROUP, LANES))]


def first_part(keep, other, size, after):
    outs = f32(size, size), f32(size, size), f32(2 * GROUP, LANES)
    return call(first_part_kernel, "first_part", outs, keep, other, after=after, scratch=buffers((PACKED, LANES)), flops=10**6)


def last_part(state, size, scale, first, after):
    kernel = lambda *refs: last_part_kernel(scale, first, *refs)
    return call(kernel, "last_part", (f32(size, size),) * 2, *state, after=after, scratch=buffers((size, size)), flops=3 * 10**9)


def copy_out(block_ref, out_hbm, span, sem):
    copy = pltpu.make_async_copy(block_ref.at[span], out_hbm.at[span], sem)
    copy.start()
    return copy


def basis_kernel(scale, sampled_ref, inverse_ref, basis_hbm, basis_ref, sems):
    inverse = split(inverse_ref[...] * scale)
    copies = []
    for at in range(sampled_ref.shape[0] // BLOCK):
        span = slice(at * BLOCK, (at + 1) * BLOCK)
        basis_ref[span, :] = product(split(sampled_ref[span, :]), inverse, 1, 1)
        copies.append(copy_out(basis_ref, basis_hbm, (pl.ds(at * BLOCK, BLOCK), slice(None)), sems.at[at]))
    for copy in copies:
        copy.wait()


def streamed(kernel, name, out, operands, scratch, flops):
    blocks = max(out.shape) // BLOCK
    return pl.pallas_call(
        kernel,
        out_shape=out,
        in_specs=[VMEM] * len(operands),
        out_specs=pl.BlockSpec(memory_space=pl.ANY),
        scratch_shapes=[pltpu.VMEM(out.shape, jnp.float32), *scratch, pltpu.SemaphoreType.DMA((blocks,))],
        compiler_params=pltpu.CompilerParams(vmem_limit_bytes=16 * 2**20),
        cost_estimate=pl.CostEstimate(flops=flops, bytes_accessed=2 * 2**20, transcendentals=0),
        name=name,
    )(*operands)


def basis_of(sampled, inverse, scale):
    kernel = lambda *refs: basis_kernel(scale, *refs)
    return streamed(kernel, "basis", f32(*sampled.shape), (sampled, inverse), (), 2 * 10**9)


def project_kernel(inverse_ref, *refs):
    *pieces, projection_hbm, projection_ref, cross_ref, sems = refs
    own = own_block()
    height = cross_ref.shape[0] // BLOCKS
    at = 0
    for piece in pieces:
        for top in range(0, piece.shape[0], height):
            cross_ref[rows_of(at ^ own, height), :] = piece[top:top + height, :]
            at += 1
    inverse = split(inverse_ref[...])
    copies = []
    for at in range(cross_ref.shape[1] // BLOCK):
        span = slice(at * BLOCK, (at + 1) * BLOCK)
        projection_ref[:, span] = product(inverse, split(cross_ref[:, span]), 1, 0)
        copies.append(copy_out(projection_ref, projection_hbm, (slice(None), pl.ds(at * BLOCK, BLOCK)), sems.at[at]))
    for copy in copies:
        copy.wait()


def project(inverse, pieces):
    rank, depth = inverse.shape[0], pieces[0].shape[1]
    scratch = (pltpu.VMEM((rank, depth), jnp.float32),)
    return streamed(project_kernel, "project", f32(rank, depth), (inverse, *pieces), scratch, 4 * 10**8)


def send(value, wide, narrow):
    mask = wide * lax.axis_size("narrow") + narrow
    pairs = [(source, source ^ mask) for source in range(lax.axis_size(AXES))]
    return lax.ppermute(value, AXES, pairs)


CORE = (1, 0)
PLANE = [(0, 1), (2, 0), (2, 1)]
NEAR, FAR = (4, 0), (8, 0)


def spare_bits():
    wide = [(2**bit, 0) for bit in range(4, lax.axis_size("wide").bit_length() - 1)]
    narrow = [(0, 2**bit) for bit in range(1, lax.axis_size("narrow").bit_length() - 1)]
    return wide + narrow


def to_plane(parts):
    order = sorted(range(len(PLANE)), key=lambda at: -PLANE[at][0] - PLANE[at][1])
    sent = {at: send(parts[at], *PLANE[at]) for at in order}
    return [sent[at] for at in range(len(PLANE))]


def per_device(features, sketch):
    scale = (features.shape[0] * lax.axis_size(AXES)) ** 0.5
    size = sketch.shape[1]
    sampled, keep, other, gram, gram_other = local_terms(features, sketch)
    gram_other = send(gram_other, *CORE)
    parts = sums([keep, send(other, *CORE)], 4, after=(gram_other,))
    cross = [parts[0]] + to_plane(parts[1:])
    gram = add([gram, gram_other], parts[-1:])
    gram = gram + send(gram, *NEAR)
    gram_other = send(gram, *FAR)
    (line,) = sums(cross)
    gram = add([gram, gram_other], (line,))
    grams = [gram] + to_plane([gram] * 3)
    (line,) = sums([line, send(line, *NEAR)], masks=(0, 1))
    gram = add(grams, (line,))
    for mask in spare_bits():
        line = line + send(line, *mask)
        gram = gram + send(gram, *mask)
    *state, norm = first_part(gram, send(gram, *CORE), size, ())
    (line,) = sums([line, send(line, *FAR)], masks=(0, 2), after=state[:1])
    plane = [line] + to_plane([line] * 3)
    inverse, factor = last_part((*state, norm), size, scale, PANEL, (line,))
    cross = plane + [send(part, *CORE) for part in plane]
    return (basis_of(sampled, inverse, scale), factor, project(inverse, cross))


def solution(mesh):
    rows = P(AXES, None)
    return jax.shard_map(
        per_device, mesh=mesh, in_specs=(rows, P()), out_specs=(rows, P(), P()), check_vma=False
    )
```

```python
import jax, jax.numpy as jnp
from jax import lax
from jax.experimental import pallas as pl
from jax.experimental.pallas import tpu as pltpu
from jax.sharding import PartitionSpec as P

GROUP = 8
LANES = 128
PANEL = 64
PACKED = 272
BLOCK = 256
BLOCKS = 32
AXES = ("wide", "narrow")
VMEM = pl.BlockSpec(memory_space=pltpu.VMEM)


def factor_panel(a_ref, factor_ref, buffer_ref, base, height, size):
    lane = lax.broadcasted_iota(jnp.int32, (GROUP, LANES), 1)
    sub = lax.broadcasted_iota(jnp.int32, (GROUP, LANES), 0)
    tiles = size // LANES
    spread = lambda value: jnp.broadcast_to(value, (GROUP, LANES))

    def spread_row(slot, k):
        return spread(buffer_ref[slot * GROUP + k:slot * GROUP + k + 1, :])

    def keep(value, slot):
        buffer_ref[slot * GROUP:(slot + 1) * GROUP, :] = value

    rows = {}
    for g in range(base, base + height, GROUP):
        for t in range(tiles):
            rows[g, t] = a_ref[g:g + GROUP, t * LANES:(t + 1) * LANES]
    for top in range(base, base + height, GROUP):
        groups = list(range(top, base + height, GROUP))
        home = top // LANES
        offset = top - home * LANES
        inside = (lane >= offset) & (lane < offset + GROUP)
        diag = rows[top, home]
        bank = top // GROUP % 2 * 20
        col, one = {}, {}
        for j in range(GROUP):
            for g in groups:
                col[g, j] = spread(rows[g, home][:, offset + j:offset + j + 1])
            keep(col[top, j], bank + j)
            for k in range(j, GROUP):
                one[k, j] = spread_row(bank + j, k)
        for g in groups:
            fresh = jnp.where(lane == sub + offset, 1.0, 0.0) if g == top else 0.0
            rows[g, home] = jnp.where(inside, fresh, rows[g, home])
        for j in range(0, GROUP, 2):
            a, b, c = one[j, j], one[j + 1, j], one[j + 1, j + 1]
            first = lax.rsqrt(a)
            both = first * lax.rsqrt(a * c - b * b)
            cross = b * first
            second = a * both
            low = {}
            for k in range(j + 2, GROUP):
                low[k] = one[k, j] * first, (a * one[k, j + 1] - b * one[k, j]) * both
            for k in range(j + 2, GROUP):
                for m in range(k, GROUP):
                    one[m, k] = one[m, k] - (low[m][0] * low[k][0] + low[m][1] * low[k][1])
            scaled = {}
            for g in groups:
                scaled[g] = col[g, j] * first, (a * col[g, j + 1] - b * col[g, j]) * both
            for k in range(j + 2, GROUP):
                for g in groups:
                    col[g, k] = col[g, k] - (scaled[g][0] * low[k][0] + scaled[g][1] * low[k][1])
            below = [jnp.where(sub > j + 1, part, 0.0) for part in scaled[top]]

            def pivots(value, slot):
                slot = bank + GROUP + 3 * (j // 2) + slot
                keep(value, slot)
                upper = spread_row(slot, j) * first
                return upper, (spread_row(slot, j + 1) - cross * upper) * second

            def replaced(value, upper, lower):
                value = value - (below[0] * upper + below[1] * lower)
                return jnp.where(sub == j, upper, jnp.where(sub == j + 1, lower, value))

            diag = replaced(diag, *pivots(diag, 2))
            for t in range(tiles):
                upper, lower = pivots(rows[top, t], t)
                rows[top, t] = replaced(rows[top, t], upper, lower)
                for g in groups[1:]:
                    rows[g, t] = rows[g, t] - (scaled[g][0] * upper + scaled[g][1] * lower)
        for t in range(tiles):
            span = slice(t * LANES, (t + 1) * LANES)
            a_ref[top:top + GROUP, span] = rows[top, t]
            if t < home:
                factor_ref[top:top + GROUP, span] = jnp.zeros((GROUP, LANES), jnp.float32)
            elif t == home:
                factor_ref[top:top + GROUP, span] = jnp.where(lane >= sub + offset, diag, 0.0)
            else:
                factor_ref[top:top + GROUP, span] = rows[top, t]


def trailing(a_ref, base, height, size):
    end = base + height
    if end == size:
        return
    panel = a_ref[base:end, :]
    col = lax.broadcasted_iota(jnp.int32, (height, size), 1)
    row = lax.broadcasted_iota(jnp.int32, (height, size), 0) + base
    right = jnp.where((col <= row) | (col >= end), panel, 0.0)
    right = split(right)
    at = lax.broadcasted_iota(jnp.int32, (height, size), 1)
    for top in range(end, size, height):
        rows = slice(top, top + height)
        rest = jnp.where((at >= base) & (at < end), 0.0, a_ref[rows, :])
        a_ref[rows, :] = rest - product(split(panel[:, rows]), right, 0, 0)


def eliminate(a_ref, factor_ref, buffer_ref, first, last):
    size = a_ref.shape[0]
    for base in range(first, last, PANEL):
        factor_panel(a_ref, factor_ref, buffer_ref, base, PANEL, size)
        trailing(a_ref, base, PANEL, size)


def split(value):
    high = value.astype(jnp.bfloat16)
    return high, (value - high.astype(jnp.float32)).astype(jnp.bfloat16)


def product(left, right, left_dim, right_dim):
    dims = (((left_dim,), (right_dim,)), ((), ()))
    dot = lambda a, b: lax.dot_general(a, b, dims, preferred_element_type=jnp.float32)
    return dot(left[0], right[0]) + (dot(left[0], right[1]) + dot(left[1], right[0]))


def core_bit():
    return lax.rem(lax.axis_index("wide"), 2)


def own_block():
    wide, narrow = lax.axis_index("wide"), lax.axis_index("narrow")
    plane = lax.rem(narrow, 2) + 2 * lax.rem(wide // 2, 2)
    return 16 * lax.rem(wide, 2) + 4 * plane + lax.rem(wide // 4, 4)


def rows_of(block, height):
    return pl.ds(pl.multiple_of(block * height, GROUP), height)


def local_kernel(features_hbm, sketch_hbm, sampled_ref, keep_ref, send_ref, gram_keep_ref, gram_send_ref, features_ref, sketch_ref, pair_ref, high_ref, low_ref, flip_high_ref, flip_low_ref, cross_ref, packed_ref, sems):
    rows, depth = features_ref.shape
    rank = sketch_ref.shape[1]
    chunks = rows // BLOCK
    copies = [pltpu.make_async_copy(sketch_hbm, sketch_ref, sems.at[chunks])]
    for at in range(chunks):
        span = pl.ds(at * BLOCK, BLOCK)
        copies.append(pltpu.make_async_copy(features_hbm.at[span, :], features_ref.at[span, :], sems.at[at]))
    for copy in copies[:2]:
        copy.start()
    copies[0].wait()
    for copy in copies[2:]:
        copy.start()
    pair_ref[:, :rank], pair_ref[:, rank:] = split(sketch_ref[...])
    gram = None
    for at in range(chunks):
        span = slice(at * BLOCK, (at + 1) * BLOCK)
        copies[1 + at].wait()
        features = split(features_ref[span, :])
        high_ref[span, :], low_ref[span, :] = features
        both = lax.dot(features[0], pair_ref[...], preferred_element_type=jnp.float32)
        sampled = both[:, :rank] + (both[:, rank:] + lax.dot(features[1], pair_ref[:, :rank], preferred_element_type=jnp.float32))
        sampled_ref[span, :] = sampled
        flipped = split(sampled.T)
        flip_high_ref[:, span], flip_low_ref[:, span] = flipped
        term = product(flipped, split(sampled), 1, 0)
        gram = term if gram is None else gram + term
    row = lax.broadcasted_iota(jnp.int32, (LANES, LANES), 0)
    col = lax.broadcasted_iota(jnp.int32, (LANES, LANES), 1)
    corner = gram[LANES:, LANES:]
    packed_ref[:LANES, :] = gram[:LANES, LANES:]
    packed_ref[LANES:2 * LANES, :] = jnp.where(col >= row, gram[:LANES, :LANES], corner)
    diagonal = jnp.sum(jnp.where(col == row, corner, 0.0), axis=0, keepdims=True)
    packed_ref[2 * LANES:, :] = jnp.broadcast_to(diagonal, (PACKED - 2 * LANES, LANES))
    half = packed_ref.shape[0] // 2
    core = core_bit()
    gram_keep_ref[...] = packed_ref[rows_of(core, half), :]
    gram_send_ref[...] = packed_ref[rows_of(1 - core, half), :]
    flipped = flip_high_ref[...], flip_low_ref[...]
    own = own_block()
    height = rank // BLOCKS
    for left in range(0, depth, BLOCK):
        span = slice(left, left + BLOCK)
        cross_ref[:, span] = product(flipped, (high_ref[:, span], low_ref[:, span]), 1, 0)
    for at in range(BLOCKS):
        block = cross_ref[rows_of(at ^ own, height), :]
        if at < BLOCKS // 2:
            keep_ref[at * height:(at + 1) * height, :] = block
        else:
            rest = at - BLOCKS // 2
            send_ref[rest * height:(rest + 1) * height, :] = block


def f32(*shape):
    return jax.ShapeDtypeStruct(shape, jnp.float32)


def local_terms(features, sketch):
    rows, depth = features.shape
    rank = sketch.shape[1]
    packed = PACKED
    hbm = pl.BlockSpec(memory_space=pltpu.HBM)
    return pl.pallas_call(
        local_kernel,
        out_shape=(f32(rows, rank), f32(rank // 2, depth), f32(rank // 2, depth), f32(packed // 2, LANES), f32(packed // 2, LANES)),
        in_specs=[hbm, hbm],
        out_specs=(VMEM,) * 5,
        scratch_shapes=[
            pltpu.VMEM((rows, depth), jnp.float32), pltpu.VMEM((depth, rank), jnp.float32),
            pltpu.VMEM((depth, 2 * rank), jnp.bfloat16),
            pltpu.VMEM((rows, depth), jnp.bfloat16), pltpu.VMEM((rows, depth), jnp.bfloat16),
            pltpu.VMEM((rank, rows), jnp.bfloat16), pltpu.VMEM((rank, rows), jnp.bfloat16),
            pltpu.VMEM((rank, depth), jnp.float32), pltpu.VMEM((packed, LANES), jnp.float32),
            pltpu.SemaphoreType.DMA((rows // BLOCK + 1,)),
        ],
        compiler_params=pltpu.CompilerParams(vmem_limit_bytes=51 * 2**20),
        cost_estimate=pl.CostEstimate(flops=4 * 10**9, bytes_accessed=8 * 2**20, transcendentals=0),
        name="local_terms",
    )(features, sketch)


def call(kernel, name, outs, *operands, after=(), scratch=(), flops=10**6):
    return pl.pallas_call(
        lambda *refs: kernel(*refs[:len(operands)], *refs[len(operands) + len(after):]),
        out_shape=outs,
        in_specs=[VMEM] * len(operands) + [pl.BlockSpec(memory_space=pl.ANY)] * len(after),
        out_specs=jax.tree.map(lambda _: VMEM, outs),
        scratch_shapes=list(scratch),
        compiler_params=pltpu.CompilerParams(vmem_limit_bytes=16 * 2**20),
        cost_estimate=pl.CostEstimate(flops=flops, bytes_accessed=10**6, transcendentals=0),
        name=name,
    )(*operands, *after)


def sum_kernel(masks, *refs):
    cross, outs = refs[:len(masks)], refs[len(masks):]
    at = 0
    for out_ref in outs:
        for top in range(0, out_ref.shape[0], GROUP):
            blocks = [ref[(at ^ mask) * GROUP:(at ^ mask) * GROUP + GROUP, :] for ref, mask in zip(cross, masks)]
            out_ref[top:top + GROUP, :] = sum(blocks)
            at += 1


def sums(cross, pieces=1, masks=None, after=()):
    height, depth = cross[0].shape
    masks = masks or (0,) * len(cross)
    outs = (f32(height // pieces, depth),) * pieces
    return call(lambda *refs: sum_kernel(masks, *refs), "sums", outs, *cross, after=after)


def add_kernel(*refs):
    *terms, out_ref = refs
    out_ref[...] = sum(term[...] for term in terms)


def add(terms, after):
    return call(add_kernel, "add", f32(*terms[0].shape), *terms, after=after, flops=10**9)


def first_part_kernel(keep_ref, other_ref, a_ref, factor_ref, norm_ref, packed_ref, buffer_ref):
    half = keep_ref.shape[0]
    core = core_bit()
    packed_ref[rows_of(core, half), :] = keep_ref[...]
    packed_ref[rows_of(1 - core, half), :] = other_ref[...]
    row = lax.broadcasted_iota(jnp.int32, (LANES, LANES), 0)
    col = lax.broadcasted_iota(jnp.int32, (LANES, LANES), 1)
    mixed = packed_ref[LANES:2 * LANES, :]
    flipped = mixed.T
    diagonal = packed_ref[2 * LANES:2 * LANES + 1, :]
    largest = jnp.maximum(jnp.max(diagonal, axis=(0, 1), keepdims=True), jnp.max(jnp.where(col == row, mixed, 0.0), axis=(0, 1), keepdims=True))
    shrink = lax.rsqrt(largest)
    grow, square = largest * shrink, shrink * shrink
    a_ref[:LANES, :LANES] = jnp.where(col >= row, mixed, flipped) * square
    a_ref[:LANES, LANES:] = packed_ref[:LANES, :] * square
    a_ref[LANES:, :LANES] = jnp.zeros((LANES, LANES), jnp.float32)
    a_ref[LANES:, LANES:] = jnp.where(col < row, mixed, jnp.where(col == row, diagonal, flipped)) * square
    norm_ref[:GROUP, :] = jnp.broadcast_to(shrink, (GROUP, LANES))
    norm_ref[GROUP:, :] = jnp.broadcast_to(grow, (GROUP, LANES))
    eliminate(a_ref, factor_ref, buffer_ref, 0, PANEL)


def last_part_kernel(scale, first, from_ref, upper_ref, norm_ref, inverse_ref, factor_ref, a_ref, buffer_ref):
    size = a_ref.shape[0]
    a_ref[...] = from_ref[...]
    eliminate(a_ref, factor_ref, buffer_ref, first, size)
    shrink, grow = norm_ref[:1, :1], norm_ref[GROUP:GROUP + 1, :1] / scale
    factor_ref[:first, :] = upper_ref[:first, :] * grow
    factor_ref[first:, :] = factor_ref[first:, :] * grow
    col = lax.broadcasted_iota(jnp.int32, (size, size), 1)
    row = lax.broadcasted_iota(jnp.int32, (size, size), 0)
    inverse_ref[...] = jnp.where(col <= row, a_ref[...], 0.0) * shrink


def buffers(*shapes):
    return [pltpu.VMEM(shape, jnp.float32) for shape in (*shapes, (40 * GROUP, LANES))]


def first_part(keep, other, size, after):
    outs = f32(size, size), f32(size, size), f32(2 * GROUP, LANES)
    return call(first_part_kernel, "first_part", outs, keep, other, after=after, scratch=buffers((PACKED, LANES)), flops=10**6)


def last_part(state, size, scale, first, after):
    kernel = lambda *refs: last_part_kernel(scale, first, *refs)
    return call(kernel, "last_part", (f32(size, size),) * 2, *state, after=after, scratch=buffers((size, size)), flops=3 * 10**9)


def copy_out(block_ref, out_hbm, span, sem):
    copy = pltpu.make_async_copy(block_ref.at[span], out_hbm.at[span], sem)
    copy.start()
    return copy


def basis_kernel(scale, sampled_ref, inverse_ref, basis_hbm, basis_ref, sems):
    inverse = split(inverse_ref[...] * scale)
    copies = []
    for at in range(sampled_ref.shape[0] // BLOCK):
        span = slice(at * BLOCK, (at + 1) * BLOCK)
        basis_ref[span, :] = product(split(sampled_ref[span, :]), inverse, 1, 1)
        copies.append(copy_out(basis_ref, basis_hbm, (pl.ds(at * BLOCK, BLOCK), slice(None)), sems.at[at]))
    for copy in copies:
        copy.wait()


def streamed(kernel, name, out, operands, scratch, flops):
    blocks = max(out.shape) // BLOCK
    return pl.pallas_call(
        kernel,
        out_shape=out,
        in_specs=[VMEM] * len(operands),
        out_specs=pl.BlockSpec(memory_space=pl.ANY),
        scratch_shapes=[pltpu.VMEM(out.shape, jnp.float32), *scratch, pltpu.SemaphoreType.DMA((blocks,))],
        compiler_params=pltpu.CompilerParams(vmem_limit_bytes=16 * 2**20),
        cost_estimate=pl.CostEstimate(flops=flops, bytes_accessed=2 * 2**20, transcendentals=0),
        name=name,
    )(*operands)


def basis_of(sampled, inverse, scale):
    kernel = lambda *refs: basis_kernel(scale, *refs)
    return streamed(kernel, "basis", f32(*sampled.shape), (sampled, inverse), (), 2 * 10**9)


def project_kernel(inverse_ref, *refs):
    *pieces, projection_hbm, projection_ref, cross_ref, sems = refs
    own = own_block()
    height = cross_ref.shape[0] // BLOCKS
    at = 0
    for piece in pieces:
        for top in range(0, piece.shape[0], height):
            cross_ref[rows_of(at ^ own, height), :] = piece[top:top + height, :]
            at += 1
    inverse = split(inverse_ref[...])
    copies = []
    for at in range(cross_ref.shape[1] // BLOCK):
        span = slice(at * BLOCK, (at + 1) * BLOCK)
        projection_ref[:, span] = product(inverse, split(cross_ref[:, span]), 1, 0)
        copies.append(copy_out(projection_ref, projection_hbm, (slice(None), pl.ds(at * BLOCK, BLOCK)), sems.at[at]))
    for copy in copies:
        copy.wait()


def project(inverse, pieces):
    rank, depth = inverse.shape[0], pieces[0].shape[1]
    scratch = (pltpu.VMEM((rank, depth), jnp.float32),)
    return streamed(project_kernel, "project", f32(rank, depth), (inverse, *pieces), scratch, 4 * 10**8)


def send(value, wide, narrow):
    mask = wide * lax.axis_size("narrow") + narrow
    pairs = [(source, source ^ mask) for source in range(lax.axis_size(AXES))]
    return lax.ppermute(value, AXES, pairs)


CORE = (1, 0)
PLANE = [(0, 1), (2, 0), (2, 1)]
NEAR, FAR = (4, 0), (8, 0)


def spare_bits():
    wide = [(2**bit, 0) for bit in range(4, lax.axis_size("wide").bit_length() - 1)]
    narrow = [(0, 2**bit) for bit in range(1, lax.axis_size("narrow").bit_length() - 1)]
    return wide + narrow


def to_plane(parts):
    order = sorted(range(len(PLANE)), key=lambda at: -PLANE[at][0] - PLANE[at][1])
    sent = {at: send(parts[at], *PLANE[at]) for at in order}
    return [sent[at] for at in range(len(PLANE))]


def per_device(features, sketch):
    scale = (features.shape[0] * lax.axis_size(AXES)) ** 0.5
    size = sketch.shape[1]
    sampled, keep, other, gram, gram_other = local_terms(features, sketch)
    gram_other = send(gram_other, *CORE)
    parts = sums([keep, send(other, *CORE)], 4, after=(gram_other,))
    cross = [parts[0]] + to_plane(parts[1:])
    gram = add([gram, gram_other], parts[-1:])
    gram = gram + send(gram, *NEAR)
    gram_other = send(gram, *FAR)
    (line,) = sums(cross)
    gram = add([gram, gram_other], (line,))
    grams = [gram] + to_plane([gram] * 3)
    (line,) = sums([line, send(line, *NEAR)], masks=(0, 1))
    gram = add(grams, (line,))
    for mask in spare_bits():
        line = line + send(line, *mask)
        gram = gram + send(gram, *mask)
    *state, norm = first_part(gram, send(gram, *CORE), size, ())
    (line,) = sums([line, send(line, *FAR)], masks=(0, 2), after=state[:1])
    plane = [line] + to_plane([line] * 3)
    inverse, factor = last_part((*state, norm), size, scale, PANEL, (line,))
    cross = plane + [send(part, *CORE) for part in plane]
    return (basis_of(sampled, inverse, scale), factor, project(inverse, cross))


def solution(mesh):
    rows = P(AXES, None)
    return jax.shard_map(
        per_device, mesh=mesh, in_specs=(rows, P()), out_specs=(rows, P(), P()), check_vma=False
    )
```

```python
import jax, jax.numpy as jnp
from jax import lax
from jax.experimental import pallas as pl
from jax.experimental.pallas import tpu as pltpu
from jax.sharding import PartitionSpec as P

GROUP = 8
LANES = 128
PANEL = 64
PACKED = 272
BLOCK = 256
BLOCKS = 32
AXES = ("wide", "narrow")
VMEM = pl.BlockSpec(memory_space=pltpu.VMEM)


def factor_panel(a_ref, factor_ref, buffer_ref, base, height, size):
    lane = lax.broadcasted_iota(jnp.int32, (GROUP, LANES), 1)
    sub = lax.broadcasted_iota(jnp.int32, (GROUP, LANES), 0)
    tiles = size // LANES
    spread = lambda value: jnp.broadcast_to(value, (GROUP, LANES))

    def spread_row(slot, k):
        return spread(buffer_ref[slot * GROUP + k:slot * GROUP + k + 1, :])

    def keep(value, slot):
        buffer_ref[slot * GROUP:(slot + 1) * GROUP, :] = value

    rows = {}
    for g in range(base, base + height, GROUP):
        for t in range(tiles):
            rows[g, t] = a_ref[g:g + GROUP, t * LANES:(t + 1) * LANES]
    for top in range(base, base + height, GROUP):
        groups = list(range(top, base + height, GROUP))
        home = top // LANES
        offset = top - home * LANES
        inside = (lane >= offset) & (lane < offset + GROUP)
        diag = rows[top, home]
        bank = top // GROUP % 2 * 20
        col, one = {}, {}
        for j in range(GROUP):
            for g in groups:
                col[g, j] = spread(rows[g, home][:, offset + j:offset + j + 1])
            keep(col[top, j], bank + j)
            for k in range(j, GROUP):
                one[k, j] = spread_row(bank + j, k)
        for g in groups:
            fresh = jnp.where(lane == sub + offset, 1.0, 0.0) if g == top else 0.0
            rows[g, home] = jnp.where(inside, fresh, rows[g, home])
        for j in range(0, GROUP, 2):
            a, b, c = one[j, j], one[j + 1, j], one[j + 1, j + 1]
            first = lax.rsqrt(a)
            both = first * lax.rsqrt(a * c - b * b)
            cross = b * first
            second = a * both
            low = {}
            for k in range(j + 2, GROUP):
                low[k] = one[k, j] * first, (a * one[k, j + 1] - b * one[k, j]) * both
            for k in range(j + 2, GROUP):
                for m in range(k, GROUP):
                    one[m, k] = one[m, k] - (low[m][0] * low[k][0] + low[m][1] * low[k][1])
            scaled = {}
            for g in groups:
                scaled[g] = col[g, j] * first, (a * col[g, j + 1] - b * col[g, j]) * both
            for k in range(j + 2, GROUP):
                for g in groups:
                    col[g, k] = col[g, k] - (scaled[g][0] * low[k][0] + scaled[g][1] * low[k][1])
            below = [jnp.where(sub > j + 1, part, 0.0) for part in scaled[top]]

            def pivots(value, slot):
                slot = bank + GROUP + 3 * (j // 2) + slot
                keep(value, slot)
                upper = spread_row(slot, j) * first
                return upper, (spread_row(slot, j + 1) - cross * upper) * second

            def replaced(value, upper, lower):
                value = value - (below[0] * upper + below[1] * lower)
                return jnp.where(sub == j, upper, jnp.where(sub == j + 1, lower, value))

            diag = replaced(diag, *pivots(diag, 2))
            for t in range(tiles):
                upper, lower = pivots(rows[top, t], t)
                rows[top, t] = replaced(rows[top, t], upper, lower)
                for g in groups[1:]:
                    rows[g, t] = rows[g, t] - (scaled[g][0] * upper + scaled[g][1] * lower)
        for t in range(tiles):
            span = slice(t * LANES, (t + 1) * LANES)
            a_ref[top:top + GROUP, span] = rows[top, t]
            if t < home:
                factor_ref[top:top + GROUP, span] = jnp.zeros((GROUP, LANES), jnp.float32)
            elif t == home:
                factor_ref[top:top + GROUP, span] = jnp.where(lane >= sub + offset, diag, 0.0)
            else:
                factor_ref[top:top + GROUP, span] = rows[top, t]


def trailing(a_ref, base, height, size):
    end = base + height
    if end == size:
        return
    panel = a_ref[base:end, :]
    col = lax.broadcasted_iota(jnp.int32, (height, size), 1)
    row = lax.broadcasted_iota(jnp.int32, (height, size), 0) + base
    right = jnp.where((col <= row) | (col >= end), panel, 0.0)
    right = split(right)
    at = lax.broadcasted_iota(jnp.int32, (height, size), 1)
    for top in range(end, size, height):
        rows = slice(top, top + height)
        rest = jnp.where((at >= base) & (at < end), 0.0, a_ref[rows, :])
        a_ref[rows, :] = rest - product(split(panel[:, rows]), right, 0, 0)


def eliminate(a_ref, factor_ref, buffer_ref, first, last):
    size = a_ref.shape[0]
    for base in range(first, last, PANEL):
        factor_panel(a_ref, factor_ref, buffer_ref, base, PANEL, size)
        trailing(a_ref, base, PANEL, size)


def split(value):
    high = value.astype(jnp.bfloat16)
    return high, (value - high.astype(jnp.float32)).astype(jnp.bfloat16)


def product(left, right, left_dim, right_dim):
    dims = (((left_dim,), (right_dim,)), ((), ()))
    dot = lambda a, b: lax.dot_general(a, b, dims, preferred_element_type=jnp.float32)
    return dot(left[0], right[0]) + (dot(left[0], right[1]) + dot(left[1], right[0]))


def core_bit():
    return lax.rem(lax.axis_index("wide"), 2)


def own_block():
    wide, narrow = lax.axis_index("wide"), lax.axis_index("narrow")
    plane = lax.rem(narrow, 2) + 2 * lax.rem(wide // 2, 2)
    return 16 * lax.rem(wide, 2) + 4 * plane + lax.rem(wide // 4, 4)


def rows_of(block, height):
    return pl.ds(pl.multiple_of(block * height, GROUP), height)


def local_kernel(features_hbm, sketch_hbm, sampled_ref, keep_ref, send_ref, gram_keep_ref, gram_send_ref, features_ref, sketch_ref, pair_ref, high_ref, low_ref, flip_high_ref, flip_low_ref, cross_ref, packed_ref, sems):
    rows, depth = features_ref.shape
    rank = sketch_ref.shape[1]
    chunks = rows // BLOCK
    copies = [pltpu.make_async_copy(sketch_hbm, sketch_ref, sems.at[chunks])]
    for at in range(chunks):
        span = pl.ds(at * BLOCK, BLOCK)
        copies.append(pltpu.make_async_copy(features_hbm.at[span, :], features_ref.at[span, :], sems.at[at]))
    for copy in copies:
        copy.start()
    copies[0].wait()
    pair_ref[:, :rank], pair_ref[:, rank:] = split(sketch_ref[...])
    gram = None
    for at in range(chunks):
        span = slice(at * BLOCK, (at + 1) * BLOCK)
        copies[1 + at].wait()
        features = split(features_ref[span, :])
        high_ref[span, :], low_ref[span, :] = features
        both = lax.dot(features[0], pair_ref[...], preferred_element_type=jnp.float32)
        sampled = both[:, :rank] + (both[:, rank:] + lax.dot(features[1], pair_ref[:, :rank], preferred_element_type=jnp.float32))
        sampled_ref[span, :] = sampled
        flipped = split(sampled.T)
        flip_high_ref[:, span], flip_low_ref[:, span] = flipped
        term = product(flipped, split(sampled), 1, 0)
        gram = term if gram is None else gram + term
    row = lax.broadcasted_iota(jnp.int32, (LANES, LANES), 0)
    col = lax.broadcasted_iota(jnp.int32, (LANES, LANES), 1)
    corner = gram[LANES:, LANES:]
    packed_ref[:LANES, :] = gram[:LANES, LANES:]
    packed_ref[LANES:2 * LANES, :] = jnp.where(col >= row, gram[:LANES, :LANES], corner)
    diagonal = jnp.sum(jnp.where(col == row, corner, 0.0), axis=0, keepdims=True)
    packed_ref[2 * LANES:, :] = jnp.broadcast_to(diagonal, (PACKED - 2 * LANES, LANES))
    half = packed_ref.shape[0] // 2
    core = core_bit()
    gram_keep_ref[...] = packed_ref[rows_of(core, half), :]
    gram_send_ref[...] = packed_ref[rows_of(1 - core, half), :]
    flipped = flip_high_ref[...], flip_low_ref[...]
    own = own_block()
    height = rank // BLOCKS
    for left in range(0, depth, BLOCK):
        span = slice(left, left + BLOCK)
        cross_ref[:, span] = product(flipped, (high_ref[:, span], low_ref[:, span]), 1, 0)
    for at in range(BLOCKS):
        block = cross_ref[rows_of(at ^ own, height), :]
        if at < BLOCKS // 2:
            keep_ref[at * height:(at + 1) * height, :] = block
        else:
            rest = at - BLOCKS // 2
            send_ref[rest * height:(rest + 1) * height, :] = block


def f32(*shape):
    return jax.ShapeDtypeStruct(shape, jnp.float32)


def local_terms(features, sketch):
    rows, depth = features.shape
    rank = sketch.shape[1]
    packed = PACKED
    hbm = pl.BlockSpec(memory_space=pltpu.HBM)
    return pl.pallas_call(
        local_kernel,
        out_shape=(f32(rows, rank), f32(rank // 2, depth), f32(rank // 2, depth), f32(packed // 2, LANES), f32(packed // 2, LANES)),
        in_specs=[hbm, hbm],
        out_specs=(VMEM,) * 5,
        scratch_shapes=[
            pltpu.VMEM((rows, depth), jnp.float32), pltpu.VMEM((depth, rank), jnp.float32),
            pltpu.VMEM((depth, 2 * rank), jnp.bfloat16),
            pltpu.VMEM((rows, depth), jnp.bfloat16), pltpu.VMEM((rows, depth), jnp.bfloat16),
            pltpu.VMEM((rank, rows), jnp.bfloat16), pltpu.VMEM((rank, rows), jnp.bfloat16),
            pltpu.VMEM((rank, depth), jnp.float32), pltpu.VMEM((packed, LANES), jnp.float32),
            pltpu.SemaphoreType.DMA((rows // BLOCK + 1,)),
        ],
        compiler_params=pltpu.CompilerParams(vmem_limit_bytes=51 * 2**20),
        cost_estimate=pl.CostEstimate(flops=4 * 10**9, bytes_accessed=8 * 2**20, transcendentals=0),
        name="local_terms",
    )(features, sketch)


def call(kernel, name, outs, *operands, after=(), scratch=(), flops=10**6):
    return pl.pallas_call(
        lambda *refs: kernel(*refs[:len(operands)], *refs[len(operands) + len(after):]),
        out_shape=outs,
        in_specs=[VMEM] * len(operands) + [pl.BlockSpec(memory_space=pl.ANY)] * len(after),
        out_specs=jax.tree.map(lambda _: VMEM, outs),
        scratch_shapes=list(scratch),
        compiler_params=pltpu.CompilerParams(vmem_limit_bytes=16 * 2**20),
        cost_estimate=pl.CostEstimate(flops=flops, bytes_accessed=10**6, transcendentals=0),
        name=name,
    )(*operands, *after)


def sum_kernel(masks, *refs):
    cross, outs = refs[:len(masks)], refs[len(masks):]
    at = 0
    for out_ref in outs:
        for top in range(0, out_ref.shape[0], GROUP):
            blocks = [ref[(at ^ mask) * GROUP:(at ^ mask) * GROUP + GROUP, :] for ref, mask in zip(cross, masks)]
            out_ref[top:top + GROUP, :] = sum(blocks)
            at += 1


def sums(cross, pieces=1, masks=None, after=()):
    height, depth = cross[0].shape
    masks = masks or (0,) * len(cross)
    outs = (f32(height // pieces, depth),) * pieces
    return call(lambda *refs: sum_kernel(masks, *refs), "sums", outs, *cross, after=after)


def add_kernel(*refs):
    *terms, out_ref = refs
    out_ref[...] = sum(term[...] for term in terms)


def add(terms, after):
    return call(add_kernel, "add", f32(*terms[0].shape), *terms, after=after, flops=10**9)


def first_part_kernel(keep_ref, other_ref, a_ref, factor_ref, norm_ref, packed_ref, buffer_ref):
    half = keep_ref.shape[0]
    core = core_bit()
    packed_ref[rows_of(core, half), :] = keep_ref[...]
    packed_ref[rows_of(1 - core, half), :] = other_ref[...]
    row = lax.broadcasted_iota(jnp.int32, (LANES, LANES), 0)
    col = lax.broadcasted_iota(jnp.int32, (LANES, LANES), 1)
    mixed = packed_ref[LANES:2 * LANES, :]
    flipped = mixed.T
    diagonal = packed_ref[2 * LANES:2 * LANES + 1, :]
    largest = jnp.maximum(jnp.max(diagonal, axis=(0, 1), keepdims=True), jnp.max(jnp.where(col == row, mixed, 0.0), axis=(0, 1), keepdims=True))
    shrink = lax.rsqrt(largest)
    grow, square = largest * shrink, shrink * shrink
    a_ref[:LANES, :LANES] = jnp.where(col >= row, mixed, flipped) * square
    a_ref[:LANES, LANES:] = packed_ref[:LANES, :] * square
    a_ref[LANES:, :LANES] = jnp.zeros((LANES, LANES), jnp.float32)
    a_ref[LANES:, LANES:] = jnp.where(col < row, mixed, jnp.where(col == row, diagonal, flipped)) * square
    norm_ref[:GROUP, :] = jnp.broadcast_to(shrink, (GROUP, LANES))
    norm_ref[GROUP:, :] = jnp.broadcast_to(grow, (GROUP, LANES))
    eliminate(a_ref, factor_ref, buffer_ref, 0, PANEL)


def last_part_kernel(scale, first, from_ref, upper_ref, norm_ref, inverse_ref, factor_ref, a_ref, buffer_ref):
    size = a_ref.shape[0]
    a_ref[...] = from_ref[...]
    eliminate(a_ref, factor_ref, buffer_ref, first, size)
    shrink, grow = norm_ref[:1, :1], norm_ref[GROUP:GROUP + 1, :1] / scale
    factor_ref[:first, :] = upper_ref[:first, :] * grow
    factor_ref[first:, :] = factor_ref[first:, :] * grow
    col = lax.broadcasted_iota(jnp.int32, (size, size), 1)
    row = lax.broadcasted_iota(jnp.int32, (size, size), 0)
    inverse_ref[...] = jnp.where(col <= row, a_ref[...], 0.0) * shrink


def buffers(*shapes):
    return [pltpu.VMEM(shape, jnp.float32) for shape in (*shapes, (40 * GROUP, LANES))]


def first_part(keep, other, size, after):
    outs = f32(size, size), f32(size, size), f32(2 * GROUP, LANES)
    return call(first_part_kernel, "first_part", outs, keep, other, after=after, scratch=buffers((PACKED, LANES)), flops=10**6)


def last_part(state, size, scale, first, after):
    kernel = lambda *refs: last_part_kernel(scale, first, *refs)
    return call(kernel, "last_part", (f32(size, size),) * 2, *state, after=after, scratch=buffers((size, size)), flops=3 * 10**9)


def copy_out(block_ref, out_hbm, span, sem):
    copy = pltpu.make_async_copy(block_ref.at[span], out_hbm.at[span], sem)
    copy.start()
    return copy


def basis_kernel(scale, sampled_ref, inverse_ref, basis_hbm, basis_ref, sems):
    inverse = split(inverse_ref[...] * scale)
    copies = []
    for at in range(sampled_ref.shape[0] // BLOCK):
        span = slice(at * BLOCK, (at + 1) * BLOCK)
        basis_ref[span, :] = product(split(sampled_ref[span, :]), inverse, 1, 1)
        copies.append(copy_out(basis_ref, basis_hbm, (pl.ds(at * BLOCK, BLOCK), slice(None)), sems.at[at]))
    for copy in copies:
        copy.wait()


def streamed(kernel, name, out, operands, scratch, flops):
    blocks = max(out.shape) // BLOCK
    return pl.pallas_call(
        kernel,
        out_shape=out,
        in_specs=[VMEM] * len(operands),
        out_specs=pl.BlockSpec(memory_space=pl.ANY),
        scratch_shapes=[pltpu.VMEM(out.shape, jnp.float32), *scratch, pltpu.SemaphoreType.DMA((blocks,))],
        compiler_params=pltpu.CompilerParams(vmem_limit_bytes=16 * 2**20),
        cost_estimate=pl.CostEstimate(flops=flops, bytes_accessed=2 * 2**20, transcendentals=0),
        name=name,
    )(*operands)


def basis_of(sampled, inverse, scale):
    kernel = lambda *refs: basis_kernel(scale, *refs)
    return streamed(kernel, "basis", f32(*sampled.shape), (sampled, inverse), (), 2 * 10**9)


def project_kernel(inverse_ref, *refs):
    *pieces, projection_hbm, projection_ref, cross_ref, sems = refs
    own = own_block()
    height = cross_ref.shape[0] // BLOCKS
    at = 0
    for piece in pieces:
        for top in range(0, piece.shape[0], height):
            cross_ref[rows_of(at ^ own, height), :] = piece[top:top + height, :]
            at += 1
    inverse = split(inverse_ref[...])
    copies = []
    for at in range(cross_ref.shape[1] // BLOCK):
        span = slice(at * BLOCK, (at + 1) * BLOCK)
        projection_ref[:, span] = product(inverse, split(cross_ref[:, span]), 1, 0)
        copies.append(copy_out(projection_ref, projection_hbm, (slice(None), pl.ds(at * BLOCK, BLOCK)), sems.at[at]))
    for copy in copies:
        copy.wait()


def project(inverse, pieces):
    rank, depth = inverse.shape[0], pieces[0].shape[1]
    scratch = (pltpu.VMEM((rank, depth), jnp.float32),)
    return streamed(project_kernel, "project", f32(rank, depth), (inverse, *pieces), scratch, 4 * 10**8)


def send(value, wide, narrow):
    mask = wide * lax.axis_size("narrow") + narrow
    pairs = [(source, source ^ mask) for source in range(lax.axis_size(AXES))]
    return lax.ppermute(value, AXES, pairs)


CORE = (1, 0)
PLANE = [(0, 1), (2, 0), (2, 1)]
NEAR, FAR = (4, 0), (8, 0)


def spare_bits():
    wide = [(2**bit, 0) for bit in range(4, lax.axis_size("wide").bit_length() - 1)]
    narrow = [(0, 2**bit) for bit in range(1, lax.axis_size("narrow").bit_length() - 1)]
    return wide + narrow


def to_plane(parts):
    order = sorted(range(len(PLANE)), key=lambda at: -PLANE[at][0] - PLANE[at][1])
    sent = {at: send(parts[at], *PLANE[at]) for at in order}
    return [sent[at] for at in range(len(PLANE))]


def per_device(features, sketch):
    scale = (features.shape[0] * lax.axis_size(AXES)) ** 0.5
    size = sketch.shape[1]
    sampled, keep, other, gram, gram_other = local_terms(features, sketch)
    gram_other = send(gram_other, *CORE)
    parts = sums([keep, send(other, *CORE)], 4, after=(gram_other,))
    cross = [parts[0]] + to_plane(parts[1:])
    gram = add([gram, gram_other], parts[-1:])
    gram = gram + send(gram, *NEAR)
    gram_other = send(gram, *FAR)
    (line,) = sums(cross)
    gram = add([gram, gram_other], (line,))
    grams = [gram] + to_plane([gram] * 3)
    (line,) = sums([line, send(line, *FAR)], masks=(0, 2))
    gram = add(grams, (line,))
    for mask in spare_bits():
        line = line + send(line, *mask)
        gram = gram + send(gram, *mask)
    *state, norm = first_part(gram, send(gram, *CORE), size, ())
    (line,) = sums([line, send(line, *NEAR)], masks=(0, 1), after=state[:1])
    plane = [line] + to_plane([line] * 3)
    inverse, factor = last_part((*state, norm), size, scale, PANEL, (line,))
    cross = plane + [send(part, *CORE) for part in plane]
    return (basis_of(sampled, inverse, scale), factor, project(inverse, cross))


def solution(mesh):
    rows = P(AXES, None)
    return jax.shard_map(
        per_device, mesh=mesh, in_specs=(rows, P()), out_specs=(rows, P(), P()), check_vma=False
    )
```

```python
import jax, jax.numpy as jnp
from jax import lax
from jax.experimental import pallas as pl
from jax.experimental.pallas import tpu as pltpu
from jax.sharding import PartitionSpec as P

GROUP = 8
LANES = 128
PANEL = 64
PACKED = 272
BLOCK = 256
BLOCKS = 32
AXES = ("wide", "narrow")
VMEM = pl.BlockSpec(memory_space=pltpu.VMEM)


def factor_panel(a_ref, factor_ref, buffer_ref, base, height, size):
    lane = lax.broadcasted_iota(jnp.int32, (GROUP, LANES), 1)
    sub = lax.broadcasted_iota(jnp.int32, (GROUP, LANES), 0)
    tiles = size // LANES
    spread = lambda value: jnp.broadcast_to(value, (GROUP, LANES))

    def spread_row(slot, k):
        return spread(buffer_ref[slot * GROUP + k:slot * GROUP + k + 1, :])

    def keep(value, slot):
        buffer_ref[slot * GROUP:(slot + 1) * GROUP, :] = value

    rows = {}
    for g in range(base, base + height, GROUP):
        for t in range(tiles):
            rows[g, t] = a_ref[g:g + GROUP, t * LANES:(t + 1) * LANES]
    for top in range(base, base + height, GROUP):
        groups = list(range(top, base + height, GROUP))
        home = top // LANES
        offset = top - home * LANES
        inside = (lane >= offset) & (lane < offset + GROUP)
        diag = rows[top, home]
        bank = top // GROUP % 2 * 20
        col, one = {}, {}
        for j in range(GROUP):
            for g in groups:
                col[g, j] = spread(rows[g, home][:, offset + j:offset + j + 1])
            keep(col[top, j], bank + j)
            for k in range(j, GROUP):
                one[k, j] = spread_row(bank + j, k)
        for g in groups:
            fresh = jnp.where(lane == sub + offset, 1.0, 0.0) if g == top else 0.0
            rows[g, home] = jnp.where(inside, fresh, rows[g, home])
        for j in range(0, GROUP, 2):
            a, b, c = one[j, j], one[j + 1, j], one[j + 1, j + 1]
            first = lax.rsqrt(a)
            both = first * lax.rsqrt(a * c - b * b)
            cross = b * first
            second = a * both
            low = {}
            for k in range(j + 2, GROUP):
                low[k] = one[k, j] * first, (a * one[k, j + 1] - b * one[k, j]) * both
            for k in range(j + 2, GROUP):
                for m in range(k, GROUP):
                    one[m, k] = one[m, k] - (low[m][0] * low[k][0] + low[m][1] * low[k][1])
            scaled = {}
            for g in groups:
                scaled[g] = col[g, j] * first, (a * col[g, j + 1] - b * col[g, j]) * both
            for k in range(j + 2, GROUP):
                for g in groups:
                    col[g, k] = col[g, k] - (scaled[g][0] * low[k][0] + scaled[g][1] * low[k][1])
            below = [jnp.where(sub > j + 1, part, 0.0) for part in scaled[top]]

            def pivots(value, slot):
                slot = bank + GROUP + 3 * (j // 2) + slot
                keep(value, slot)
                upper = spread_row(slot, j) * first
                return upper, (spread_row(slot, j + 1) - cross * upper) * second

            def replaced(value, upper, lower):
                value = value - (below[0] * upper + below[1] * lower)
                return jnp.where(sub == j, upper, jnp.where(sub == j + 1, lower, value))

            diag = replaced(diag, *pivots(diag, 2))
            for t in range(tiles):
                upper, lower = pivots(rows[top, t], t)
                rows[top, t] = replaced(rows[top, t], upper, lower)
                for g in groups[1:]:
                    rows[g, t] = rows[g, t] - (scaled[g][0] * upper + scaled[g][1] * lower)
        for t in range(tiles):
            span = slice(t * LANES, (t + 1) * LANES)
            a_ref[top:top + GROUP, span] = rows[top, t]
            if t < home:
                factor_ref[top:top + GROUP, span] = jnp.zeros((GROUP, LANES), jnp.float32)
            elif t == home:
                factor_ref[top:top + GROUP, span] = jnp.where(lane >= sub + offset, diag, 0.0)
            else:
                factor_ref[top:top + GROUP, span] = rows[top, t]


def trailing(a_ref, base, height, size):
    end = base + height
    if end == size:
        return
    panel = a_ref[base:end, :]
    col = lax.broadcasted_iota(jnp.int32, (height, size), 1)
    row = lax.broadcasted_iota(jnp.int32, (height, size), 0) + base
    right = jnp.where((col <= row) | (col >= end), panel, 0.0)
    right = split(right)
    at = lax.broadcasted_iota(jnp.int32, (height, size), 1)
    for top in range(end, size, height):
        rows = slice(top, top + height)
        rest = jnp.where((at >= base) & (at < end), 0.0, a_ref[rows, :])
        a_ref[rows, :] = rest - product(split(panel[:, rows]), right, 0, 0)


def eliminate(a_ref, factor_ref, buffer_ref, first, last):
    size = a_ref.shape[0]
    for base in range(first, last, PANEL):
        factor_panel(a_ref, factor_ref, buffer_ref, base, PANEL, size)
        trailing(a_ref, base, PANEL, size)


def split(value):
    high = value.astype(jnp.bfloat16)
    return high, (value - high.astype(jnp.float32)).astype(jnp.bfloat16)


def product(left, right, left_dim, right_dim):
    dims = (((left_dim,), (right_dim,)), ((), ()))
    dot = lambda a, b: lax.dot_general(a, b, dims, preferred_element_type=jnp.float32)
    return dot(left[0], right[0]) + (dot(left[0], right[1]) + dot(left[1], right[0]))


def core_bit():
    return lax.rem(lax.axis_index("wide"), 2)


def own_block():
    wide, narrow = lax.axis_index("wide"), lax.axis_index("narrow")
    plane = lax.rem(narrow, 2) + 2 * lax.rem(wide // 2, 2)
    return 16 * lax.rem(wide, 2) + 4 * plane + lax.rem(wide // 4, 4)


def rows_of(block, height):
    return pl.ds(pl.multiple_of(block * height, GROUP), height)


def local_kernel(features_hbm, sketch_hbm, sampled_high_ref, sampled_low_ref, keep_ref, send_ref, gram_keep_ref, gram_send_ref, features_ref, sketch_ref, pair_ref, high_ref, low_ref, flip_high_ref, flip_low_ref, cross_ref, packed_ref, sems):
    rows, depth = features_ref.shape
    rank = sketch_ref.shape[1]
    chunks = rows // BLOCK
    copies = [pltpu.make_async_copy(sketch_hbm, sketch_ref, sems.at[chunks])]
    for at in range(chunks):
        span = pl.ds(at * BLOCK, BLOCK)
        copies.append(pltpu.make_async_copy(features_hbm.at[span, :], features_ref.at[span, :], sems.at[at]))
    for copy in copies:
        copy.start()
    copies[0].wait()
    pair_ref[:, :rank], pair_ref[:, rank:] = split(sketch_ref[...])
    gram = None
    for at in range(chunks):
        span = slice(at * BLOCK, (at + 1) * BLOCK)
        copies[1 + at].wait()
        features = split(features_ref[span, :])
        high_ref[span, :], low_ref[span, :] = features
        both = lax.dot(features[0], pair_ref[...], preferred_element_type=jnp.float32)
        sampled = both[:, :rank] + (both[:, rank:] + lax.dot(features[1], pair_ref[:, :rank], preferred_element_type=jnp.float32))
        parts = split(sampled)
        sampled_high_ref[span, :], sampled_low_ref[span, :] = parts
        flipped = split(sampled.T)
        flip_high_ref[:, span], flip_low_ref[:, span] = flipped
        term = product(flipped, parts, 1, 0)
        gram = term if gram is None else gram + term
    row = lax.broadcasted_iota(jnp.int32, (LANES, LANES), 0)
    col = lax.broadcasted_iota(jnp.int32, (LANES, LANES), 1)
    corner = gram[LANES:, LANES:]
    packed_ref[:LANES, :] = gram[:LANES, LANES:]
    packed_ref[LANES:2 * LANES, :] = jnp.where(col >= row, gram[:LANES, :LANES], corner)
    diagonal = jnp.sum(jnp.where(col == row, corner, 0.0), axis=0, keepdims=True)
    packed_ref[2 * LANES:, :] = jnp.broadcast_to(diagonal, (PACKED - 2 * LANES, LANES))
    half = packed_ref.shape[0] // 2
    core = core_bit()
    gram_keep_ref[...] = packed_ref[rows_of(core, half), :]
    gram_send_ref[...] = packed_ref[rows_of(1 - core, half), :]
    flipped = flip_high_ref[...], flip_low_ref[...]
    own = own_block()
    height = rank // BLOCKS
    for left in range(0, depth, BLOCK):
        span = slice(left, left + BLOCK)
        cross_ref[:, span] = product(flipped, (high_ref[:, span], low_ref[:, span]), 1, 0)
    for at in range(BLOCKS):
        block = cross_ref[rows_of(at ^ own, height), :]
        if at < BLOCKS // 2:
            keep_ref[at * height:(at + 1) * height, :] = block
        else:
            rest = at - BLOCKS // 2
            send_ref[rest * height:(rest + 1) * height, :] = block


def f32(*shape):
    return jax.ShapeDtypeStruct(shape, jnp.float32)


def local_terms(features, sketch):
    rows, depth = features.shape
    rank = sketch.shape[1]
    packed = PACKED
    half = jax.ShapeDtypeStruct((rows, rank), jnp.bfloat16)
    hbm = pl.BlockSpec(memory_space=pltpu.HBM)
    return pl.pallas_call(
        local_kernel,
        out_shape=(half, half, f32(rank // 2, depth), f32(rank // 2, depth), f32(packed // 2, LANES), f32(packed // 2, LANES)),
        in_specs=[hbm, hbm],
        out_specs=(VMEM,) * 6,
        scratch_shapes=[
            pltpu.VMEM((rows, depth), jnp.float32), pltpu.VMEM((depth, rank), jnp.float32),
            pltpu.VMEM((depth, 2 * rank), jnp.bfloat16),
            pltpu.VMEM((rows, depth), jnp.bfloat16), pltpu.VMEM((rows, depth), jnp.bfloat16),
            pltpu.VMEM((rank, rows), jnp.bfloat16), pltpu.VMEM((rank, rows), jnp.bfloat16),
            pltpu.VMEM((rank, depth), jnp.float32), pltpu.VMEM((packed, LANES), jnp.float32),
            pltpu.SemaphoreType.DMA((rows // BLOCK + 1,)),
        ],
        compiler_params=pltpu.CompilerParams(vmem_limit_bytes=51 * 2**20),
        cost_estimate=pl.CostEstimate(flops=4 * 10**9, bytes_accessed=8 * 2**20, transcendentals=0),
        name="local_terms",
    )(features, sketch)


def call(kernel, name, outs, *operands, after=(), scratch=(), flops=10**6):
    return pl.pallas_call(
        lambda *refs: kernel(*refs[:len(operands)], *refs[len(operands) + len(after):]),
        out_shape=outs,
        in_specs=[VMEM] * len(operands) + [pl.BlockSpec(memory_space=pl.ANY)] * len(after),
        out_specs=jax.tree.map(lambda _: VMEM, outs),
        scratch_shapes=list(scratch),
        compiler_params=pltpu.CompilerParams(vmem_limit_bytes=16 * 2**20),
        cost_estimate=pl.CostEstimate(flops=flops, bytes_accessed=10**6, transcendentals=0),
        name=name,
    )(*operands, *after)


def sum_kernel(masks, *refs):
    cross, outs = refs[:len(masks)], refs[len(masks):]
    at = 0
    for out_ref in outs:
        for top in range(0, out_ref.shape[0], GROUP):
            blocks = [ref[(at ^ mask) * GROUP:(at ^ mask) * GROUP + GROUP, :] for ref, mask in zip(cross, masks)]
            out_ref[top:top + GROUP, :] = sum(blocks)
            at += 1


def sums(cross, pieces=1, masks=None, after=()):
    height, depth = cross[0].shape
    masks = masks or (0,) * len(cross)
    outs = (f32(height // pieces, depth),) * pieces
    return call(lambda *refs: sum_kernel(masks, *refs), "sums", outs, *cross, after=after)


def add_kernel(*refs):
    *terms, out_ref = refs
    out_ref[...] = sum(term[...] for term in terms)


def add(terms, after):
    return call(add_kernel, "add", f32(*terms[0].shape), *terms, after=after, flops=10**9)


def first_part_kernel(keep_ref, other_ref, a_ref, factor_ref, norm_ref, packed_ref, buffer_ref):
    half = keep_ref.shape[0]
    core = core_bit()
    packed_ref[rows_of(core, half), :] = keep_ref[...]
    packed_ref[rows_of(1 - core, half), :] = other_ref[...]
    row = lax.broadcasted_iota(jnp.int32, (LANES, LANES), 0)
    col = lax.broadcasted_iota(jnp.int32, (LANES, LANES), 1)
    mixed = packed_ref[LANES:2 * LANES, :]
    flipped = mixed.T
    diagonal = packed_ref[2 * LANES:2 * LANES + 1, :]
    largest = jnp.maximum(jnp.max(diagonal, axis=(0, 1), keepdims=True), jnp.max(jnp.where(col == row, mixed, 0.0), axis=(0, 1), keepdims=True))
    shrink = lax.rsqrt(largest)
    grow, square = largest * shrink, shrink * shrink
    a_ref[:LANES, :LANES] = jnp.where(col >= row, mixed, flipped) * square
    a_ref[:LANES, LANES:] = packed_ref[:LANES, :] * square
    a_ref[LANES:, :LANES] = jnp.zeros((LANES, LANES), jnp.float32)
    a_ref[LANES:, LANES:] = jnp.where(col < row, mixed, jnp.where(col == row, diagonal, flipped)) * square
    norm_ref[:GROUP, :] = jnp.broadcast_to(shrink, (GROUP, LANES))
    norm_ref[GROUP:, :] = jnp.broadcast_to(grow, (GROUP, LANES))
    eliminate(a_ref, factor_ref, buffer_ref, 0, PANEL)


def last_part_kernel(scale, first, from_ref, upper_ref, norm_ref, inverse_ref, factor_ref, a_ref, buffer_ref):
    size = a_ref.shape[0]
    a_ref[...] = from_ref[...]
    eliminate(a_ref, factor_ref, buffer_ref, first, size)
    shrink, grow = norm_ref[:1, :1], norm_ref[GROUP:GROUP + 1, :1] / scale
    factor_ref[:first, :] = upper_ref[:first, :] * grow
    factor_ref[first:, :] = factor_ref[first:, :] * grow
    col = lax.broadcasted_iota(jnp.int32, (size, size), 1)
    row = lax.broadcasted_iota(jnp.int32, (size, size), 0)
    inverse_ref[...] = jnp.where(col <= row, a_ref[...], 0.0) * shrink


def buffers(*shapes):
    return [pltpu.VMEM(shape, jnp.float32) for shape in (*shapes, (40 * GROUP, LANES))]


def first_part(keep, other, size, after):
    outs = f32(size, size), f32(size, size), f32(2 * GROUP, LANES)
    return call(first_part_kernel, "first_part", outs, keep, other, after=after, scratch=buffers((PACKED, LANES)), flops=10**6)


def last_part(state, size, scale, first, after):
    kernel = lambda *refs: last_part_kernel(scale, first, *refs)
    return call(kernel, "last_part", (f32(size, size),) * 2, *state, after=after, scratch=buffers((size, size)), flops=3 * 10**9)


def copy_out(block_ref, out_hbm, span, sem):
    copy = pltpu.make_async_copy(block_ref.at[span], out_hbm.at[span], sem)
    copy.start()
    return copy


def basis_kernel(scale, high_ref, low_ref, inverse_ref, basis_hbm, basis_ref, sems):
    inverse = split(inverse_ref[...] * scale)
    copies = []
    for at in range(high_ref.shape[0] // BLOCK):
        span = slice(at * BLOCK, (at + 1) * BLOCK)
        basis_ref[span, :] = product((high_ref[span, :], low_ref[span, :]), inverse, 1, 1)
        copies.append(copy_out(basis_ref, basis_hbm, (pl.ds(at * BLOCK, BLOCK), slice(None)), sems.at[at]))
    for copy in copies:
        copy.wait()


def streamed(kernel, name, out, operands, scratch, flops):
    blocks = max(out.shape) // BLOCK
    return pl.pallas_call(
        kernel,
        out_shape=out,
        in_specs=[VMEM] * len(operands),
        out_specs=pl.BlockSpec(memory_space=pl.ANY),
        scratch_shapes=[pltpu.VMEM(out.shape, jnp.float32), *scratch, pltpu.SemaphoreType.DMA((blocks,))],
        compiler_params=pltpu.CompilerParams(vmem_limit_bytes=16 * 2**20),
        cost_estimate=pl.CostEstimate(flops=flops, bytes_accessed=2 * 2**20, transcendentals=0),
        name=name,
    )(*operands)


def basis_of(sampled, inverse, scale):
    kernel = lambda *refs: basis_kernel(scale, *refs)
    return streamed(kernel, "basis", f32(*sampled[0].shape), (*sampled, inverse), (), 2 * 10**9)


def project_kernel(inverse_ref, *refs):
    *pieces, projection_hbm, projection_ref, cross_ref, sems = refs
    own = own_block()
    height = cross_ref.shape[0] // BLOCKS
    at = 0
    for piece in pieces:
        for top in range(0, piece.shape[0], height):
            cross_ref[rows_of(at ^ own, height), :] = piece[top:top + height, :]
            at += 1
    inverse = split(inverse_ref[...])
    copies = []
    for at in range(cross_ref.shape[1] // BLOCK):
        span = slice(at * BLOCK, (at + 1) * BLOCK)
        projection_ref[:, span] = product(inverse, split(cross_ref[:, span]), 1, 0)
        copies.append(copy_out(projection_ref, projection_hbm, (slice(None), pl.ds(at * BLOCK, BLOCK)), sems.at[at]))
    for copy in copies:
        copy.wait()


def project(inverse, pieces):
    rank, depth = inverse.shape[0], pieces[0].shape[1]
    scratch = (pltpu.VMEM((rank, depth), jnp.float32),)
    return streamed(project_kernel, "project", f32(rank, depth), (inverse, *pieces), scratch, 4 * 10**8)


def send(value, wide, narrow):
    mask = wide * lax.axis_size("narrow") + narrow
    pairs = [(source, source ^ mask) for source in range(lax.axis_size(AXES))]
    return lax.ppermute(value, AXES, pairs)


CORE = (1, 0)
PLANE = [(0, 1), (2, 0), (2, 1)]
NEAR, FAR = (4, 0), (8, 0)


def spare_bits():
    wide = [(2**bit, 0) for bit in range(4, lax.axis_size("wide").bit_length() - 1)]
    narrow = [(0, 2**bit) for bit in range(1, lax.axis_size("narrow").bit_length() - 1)]
    return wide + narrow


def to_plane(parts):
    order = sorted(range(len(PLANE)), key=lambda at: -PLANE[at][0] - PLANE[at][1])
    sent = {at: send(parts[at], *PLANE[at]) for at in order}
    return [sent[at] for at in range(len(PLANE))]


def per_device(features, sketch):
    scale = (features.shape[0] * lax.axis_size(AXES)) ** 0.5
    size = sketch.shape[1]
    *sampled, keep, other, gram, gram_other = local_terms(features, sketch)
    gram_other = send(gram_other, *CORE)
    parts = sums([keep, send(other, *CORE)], 4, after=(gram_other,))
    cross = [parts[0]] + to_plane(parts[1:])
    gram = add([gram, gram_other], parts[-1:])
    gram = gram + send(gram, *NEAR)
    gram_other = send(gram, *FAR)
    (line,) = sums(cross)
    gram = add([gram, gram_other], (line,))
    grams = [gram] + to_plane([gram] * 3)
    (line,) = sums([line, send(line, *NEAR)], masks=(0, 1))
    gram = add(grams, (line,))
    for mask in spare_bits():
        line = line + send(line, *mask)
        gram = gram + send(gram, *mask)
    *state, norm = first_part(gram, send(gram, *CORE), size, ())
    (line,) = sums([line, send(line, *FAR)], masks=(0, 2), after=state[:1])
    plane = [line] + to_plane([line] * 3)
    inverse, factor = last_part((*state, norm), size, scale, PANEL, (line,))
    cross = plane + [send(part, *CORE) for part in plane]
    return (basis_of(sampled, inverse, scale), factor, project(inverse, cross))


def solution(mesh):
    rows = P(AXES, None)
    return jax.shard_map(
        per_device, mesh=mesh, in_specs=(rows, P()), out_specs=(rows, P(), P()), check_vma=False
    )
```
